128 devices in a mesh: inner: 8 (over z, core), outer: 8 (over x, y_lo), head: 2 (over y_hi).
Axes of the slice: x: 4, y: 4 (y_hi: 2, y_lo: 2; y = y_hi * 2 + y_lo), z: 4, core: 2. Of those that a mesh axis runs over, the one named last changes fastest.
Arguments:
- queries: bfloat16 [8192, 2048], P(('inner', 'outer'), 'head'), parts along dimension 1, may hold values from -120 to 120
- keys: bfloat16 [8192, 256], P(('inner', 'outer'), 'head'), parts along dimension 1, may hold values from -6 to 6
- values: bfloat16 [8192, 256], P(('inner', 'outer'), 'head'), parts along dimension 1, may hold values from -6 to 6
- grad_out: bfloat16 [8192, 2048], P(('inner', 'outer'), 'head'), parts along dimension 1, may hold values from -6 to 6
- block_docs: int32 [64], P(('inner', 'outer')), may hold values from 0 to 7, never falling along the last dimension, each value on 1 to 40 neighbouring positions
Outputs:
- grad_queries: bfloat16 [8192, 2048], P(('inner', 'outer'), 'head'), parts along dimension 1
- grad_keys: bfloat16 [8192, 256], P(('inner', 'outer'), 'head'), parts along dimension 1
- grad_values: bfloat16 [8192, 256], P(('inner', 'outer'), 'head'), parts along dimension 1
The draws below stay inside these ranges and needn't reach their ends.
There are 2 independent parts, one for each index of `head`. The reference program is written for one: setup_inputs(seed, part) draws one part's arguments, and reference() takes and returns one part's arrays. A program takes and returns all parts, laid end to end along the dimension named above; an argument that names none is the same for every part. Nothing has to cross between parts.
Inputs may be any that keep to these rules, and one draw needn't show every extreme that they name: `block_docs`: documents are runs of whole blocks in order; the longest has 40 blocks.
All inputs are finite; a program needn't handle non-finite values.
Results may differ from the reference program's by a relative error of at most 0.0065.
Values may be sent and summed in bfloat16 or wider, within the bound.
No kernel may reach another device: no remote copies, remote signals or barrier semaphores. Data moves between devices by JAX's collectives and lax.ppermute only.
A program may use at most 64 MiB of HBM per device.

```python
import math
import jax
import jax.numpy as jnp
import numpy as np
from jax import lax

GROUP = 8
HD = 128
BLK = 128
TOK_DEV = 128
DOCS = 8
TOKENS = 8192
NBLK = 64
MOST = 40


def shared_keys(key):
    return jnp.clip(jax.random.normal(jax.random.fold_in(key, 7), (TOKENS, HD), jnp.float32), -6.0, 6.0)


def draw_keys(key, part):
    base = shared_keys(key)
    return base.astype(jnp.bfloat16)


def draw_queries(key, part):
    key = jax.random.fold_in(key, 5)
    drawn = jnp.clip(jax.random.normal(key, (TOKENS, GROUP * HD), jnp.float32), -6.0, 6.0)
    return drawn.astype(jnp.bfloat16)


def levels(rng, extent, pieces, least, high):
    def one(position, parts):
        draws = jax.random.uniform(jax.random.fold_in(jax.random.fold_in(rng, 6), position), (parts,), jnp.float32, least / len(pieces), high / len(pieces))
        return jnp.repeat(jnp.exp(draws), extent[position] // parts).reshape((-1,) + (1,) * (len(extent) - position - 1))

    level = one(*pieces[0])
    for cut in pieces[1:]:
        level = level * one(*cut)
    return level


def length_profile(number_of, total, bound, slope):
    portions = [(1 << 20) // math.isqrt(rank ** slope) + 1 for rank in range(2, number_of + 1)]
    surplus, given = total - bound - (number_of - 1), [1] * (number_of - 1)
    while surplus > 0:
        candidates = [i for i in range(number_of - 1) if given[i] < bound]
        pool, left = sum([portions[i] for i in candidates]), surplus
        for i in candidates:
            extra = min(bound - given[i], max(1, left * portions[i] // pool), surplus)
            given[i] = given[i] + extra
            surplus = surplus - extra
    return np.array([bound] + given)


def ragged(rng, count, total, most, skew):
    if count == 2:
        one = jax.random.randint(rng, (), max(1, total - most), min(most, total - 1) + 1)
        return jnp.stack([one, total - one])
    tallies = jnp.asarray(length_profile(count, total, most, skew), jnp.int32)
    couples = (count - 1) // 2
    donor, taker = tallies[1:1 + 2 * couples:2], tallies[2:2 + 2 * couples:2]
    slack = jnp.minimum(donor - 1, most - taker)
    moved = jax.random.randint(jax.random.fold_in(rng, 1), (couples,), 0, 1 << 20) % (slack + 1)
    tallies = tallies.at[1:1 + 2 * couples:2].set(donor - moved).at[2:2 + 2 * couples:2].set(taker + moved)
    return tallies[jax.random.permutation(jax.random.fold_in(rng, 2), count)]


def bell_draw(key, extent, spread, bound, pieces=(), kind=jnp.bfloat16):
    result = jax.random.normal(key, extent, jnp.float32) * spread
    if len(pieces) > 0:
        result = levels(key, extent, pieces, -0.22, 0.18) * result
    return jnp.clip(result, min=-bound, max=bound).astype(kind)


def setup_inputs(seed: int = 0, part: int = 0) -> dict:
    arg_keys = jax.random.split(jax.random.key(seed), 6)
    own_keys = jax.random.split(jax.random.fold_in(arg_keys[5], part), 6)
    queries = draw_queries(jax.random.fold_in(jax.random.fold_in(arg_keys[5], part), 71), part)
    keys = draw_keys(jax.random.fold_in(jax.random.fold_in(arg_keys[5], part), 71), part)
    values = bell_draw(own_keys[2], (TOKENS, HD), 1.0, 6.0, ((0, 64),))
    grad_out = bell_draw(own_keys[3], (TOKENS, GROUP * HD), 1.0, 6.0, ((0, 64),))
    block_docs = jnp.searchsorted(jnp.cumsum(ragged(arg_keys[4], DOCS, NBLK, MOST, 0)), jnp.arange(NBLK), side="right").astype(jnp.int32)
    return {"queries": queries, "keys": keys, "values": values, "grad_out": grad_out, "block_docs": block_docs}


NEG = -1.0e30


def rounded(x):
    return lax.optimization_barrier(x.astype(jnp.bfloat16)).astype(jnp.float32)


def reference(queries, keys, values, grad_out, block_docs):
    scale = float(HD) ** -0.5
    count = TOKENS // TOK_DEV
    tok_doc = jnp.repeat(block_docs.astype(jnp.int32), BLK, total_repeat_length=TOKENS).reshape(count, TOK_DEV)
    tok_pos = jnp.arange(TOKENS, dtype=jnp.int32).reshape(count, TOK_DEV)
    q4 = queries.astype(jnp.float32).reshape(count, TOK_DEV, GROUP, HD)
    d4 = grad_out.astype(jnp.float32).reshape(count, TOK_DEV, GROUP, HD)
    k3 = keys.astype(jnp.float32).reshape(count, TOK_DEV, HD)
    v3 = values.astype(jnp.float32).reshape(count, TOK_DEV, HD)

    def allowed(qi, kj):
        return (tok_pos[kj][None, :] <= tok_pos[qi][:, None]) & (tok_doc[kj][None, :] == tok_doc[qi][:, None])

    def masked_scores(qi, kj, mask):
        s = jnp.einsum("rhd,kd->hrk", q4[qi], k3[kj]) * scale
        return jnp.where(mask[None], s, NEG)

    def stat_row(qi):
        def step(carry, kj):
            mask = allowed(qi, kj)

            def update(current):
                top, total, weighted = current
                s = masked_scores(qi, kj, mask)
                new_top = jnp.maximum(top, jnp.max(s, axis=-1))
                probs = jnp.where(mask[None], jnp.exp(s - new_top[:, :, None]), 0.0)
                dprobs = jnp.einsum("rhd,kd->hrk", d4[qi], v3[kj])
                factor = jnp.exp(top - new_top)
                return new_top, total * factor + jnp.sum(probs, axis=-1), weighted * factor + jnp.sum(probs * dprobs, axis=-1)

            return lax.cond(jnp.any(mask), update, lambda current: current, carry), None

        start = (jnp.full((GROUP, TOK_DEV), NEG, jnp.float32), jnp.zeros((GROUP, TOK_DEV), jnp.float32), jnp.zeros((GROUP, TOK_DEV), jnp.float32))
        (top, total, weighted), _ = lax.scan(step, start, jnp.arange(count, dtype=jnp.int32))
        return top + jnp.log(total), weighted / total

    lse, delta = lax.map(stat_row, jnp.arange(count, dtype=jnp.int32))

    def grad_row(carry, qi):
        def step(inner, kj):
            mask = allowed(qi, kj)

            def work(current):
                dq, dk_all, dv_all = current
                s = masked_scores(qi, kj, mask)
                probs = jnp.where(mask[None], jnp.exp(s - lse[qi][:, :, None]), 0.0)
                dprobs = jnp.einsum("rhd,kd->hrk", d4[qi], v3[kj])
                dscores = probs * (dprobs - delta[qi][:, :, None])
                probs_low = rounded(probs)
                dscores_low = rounded(dscores)
                dq = dq + jnp.einsum("hrk,kd->rhd", dscores_low, k3[kj])
                dk_all = dk_all.at[kj].add(jnp.einsum("hrk,rhd->kd", dscores_low, q4[qi]))
                dv_all = dv_all.at[kj].add(jnp.einsum("hrk,rhd->kd", probs_low, d4[qi]))
                return dq, dk_all, dv_all

            return lax.cond(jnp.any(mask), work, lambda current: current, inner), None

        dq_start = jnp.zeros((TOK_DEV, GROUP, HD), jnp.float32)
        (dq, dk_all, dv_all), _ = lax.scan(step, (dq_start, carry[0], carry[1]), jnp.arange(count, dtype=jnp.int32))
        return (dk_all, dv_all), (scale * dq).reshape(TOK_DEV, GROUP * HD).astype(jnp.bfloat16)

    empty = jnp.zeros((count, TOK_DEV, HD), jnp.float32)
    (dk_all, dv_all), grad_queries = lax.scan(grad_row, (empty, empty), jnp.arange(count, dtype=jnp.int32))
    grad_queries = grad_queries.reshape(TOKENS, GROUP * HD)
    grad_keys = (scale * dk_all).reshape(TOKENS, HD).astype(jnp.bfloat16)
    grad_values = dv_all.reshape(TOKENS, HD).astype(jnp.bfloat16)
    return (grad_queries, grad_keys, grad_values)
```

```python
import math

import jax
import jax.numpy as jnp
from jax import lax
from jax.experimental import pallas as pl
from jax.experimental.pallas import tpu as pltpu
from jax.sharding import PartitionSpec as P

NEG = -1e30
HEAD = 128
BLOCK = 128
DOC_ROWS = 16
CHUNK_BLOCKS = 4
CHUNK = CHUNK_BLOCKS * BLOCK
LONGEST = 40
SCALE = float(HEAD) ** (-0.5)
TO_EXP2 = SCALE * math.log2(math.e)
CONTEXT = ("inner", "outer")


def dot(lhs, rhs, over):
    return lax.dot_general(lhs, rhs, ((over[:1], over[1:]), ((), ())), preferred_element_type=jnp.float32)


def attention_grads(sizes, *refs):
    nz, nx = sizes
    place_ref, q_ref, g_ref = refs[:3]
    k_pieces = (refs[3 : 3 + nx], refs[3 + nx : 3 + 2 * nx])
    refs = refs[3 + 2 * nx :]
    v_pieces = (refs[:nz], refs[nz : 2 * nz])
    refs = refs[2 * nz :]
    dq_ref, dk_own, dk_sib, dv_own, dv_sib = refs[:5]
    q_rows, g_rows, k_all, v_all, scores, dprobs, dk_total, dv_total, sem = refs[5:]
    blocks = k_all.shape[0]
    tiles, part, width = q_ref.shape
    heads = width // HEAD
    rows = heads * part
    z, x, y, core = (place_ref[i] for i in range(4))

    def block_of(dz, dx, dc):
        c = core if dc == 0 else 1 - core
        return (lax.rem(z + dz, nz) * 2 + c) * (2 * nx) + lax.rem(x + dx, nx) * 2

    copies = []
    for dc in range(2):
        for dx in range(nx):
            for dz in range(nz):
                to = pl.ds(block_of(nz - dz, nx - dx, dc), 2)
                for piece, whole in ((k_pieces[dc][dx].at[dz], k_all), (v_pieces[dc][dz].at[dx], v_all)):
                    copies.append(pltpu.make_async_copy(piece, whole.at[to], sem.at[len(copies)]))
    for copy in copies:
        copy.start()
    dk_total[...] = jnp.zeros_like(dk_total)
    dv_total[...] = jnp.zeros_like(dv_total)
    row_token = z * part + lax.rem(lax.broadcasted_iota(jnp.int32, (CHUNK, rows), 1), part)
    key_token = lax.broadcasted_iota(jnp.int32, (CHUNK, rows), 0)
    for copy in copies:
        copy.wait()

    def fold(value, combine):
        return combine(value.reshape(CHUNK // 8, 8, rows), axis=0)

    def tile(j, carry):
        block = (lax.rem(z + nz - j, nz) * 2 + core) * (2 * nx) + x * 2 + y
        docs = k_all[:, BLOCK:, :].astype(jnp.float32)
        mine = k_all[pl.ds(block, 1), BLOCK:, :].astype(jnp.float32)
        before = jnp.sum(jnp.where(docs < mine, 1.0, 0.0), axis=0)
        first = jnp.max(before).astype(jnp.int32)
        for h in range(heads):
            q_rows[h * part : (h + 1) * part, :] = q_ref[j, :, h * HEAD : (h + 1) * HEAD]
            g_rows[h * part : (h + 1) * part, :] = g_ref[j, :, h * HEAD : (h + 1) * HEAD]
        q = q_rows[...]
        g = g_rows[...]
        chunks = lax.div(block - first + CHUNK_BLOCKS, CHUNK_BLOCKS)

        def keys_at(t):
            return jnp.minimum(first + t * CHUNK_BLOCKS, blocks - CHUNK_BLOCKS)

        def key_rows(t):
            return k_all[pl.ds(keys_at(t), CHUNK_BLOCKS), :BLOCK, :].reshape(CHUNK, HEAD)

        def slot(t):
            return pl.ds(pl.multiple_of(t * CHUNK, CHUNK), CHUNK)

        def full_scores(t, top):
            s = dot(key_rows(t), q, (1, 1))
            scores[slot(t), :] = s
            return jnp.maximum(top, fold(s, jnp.max))

        last = chunks - 1
        top = lax.fori_loop(0, last, full_scores, jnp.full((8, rows), NEG, jnp.float32))
        begin = keys_at(last)
        skipped = (first + last * CHUNK_BLOCKS - begin) * BLOCK
        mask = (key_token <= row_token + (block - begin) * BLOCK) & (key_token >= skipped)
        s = jnp.where(mask, dot(key_rows(last), q, (1, 1)), NEG)
        scores[slot(last), :] = s
        top = jnp.max(jnp.maximum(top, fold(s, jnp.max)), axis=0, keepdims=True) * TO_EXP2

        def sums(t, state):
            norm, weighted = state
            e = jnp.exp2(scores[slot(t), :] * TO_EXP2 - top)
            scores[slot(t), :] = e
            value_rows = v_all[pl.ds(keys_at(t), CHUNK_BLOCKS)].reshape(CHUNK, HEAD)
            dp = dot(value_rows, g, (1, 1))
            dprobs[slot(t), :] = dp
            return norm + fold(e, jnp.sum), weighted + fold(e * dp, jnp.sum)

        zeros = jnp.zeros((8, rows), jnp.float32)
        norm, weighted = lax.fori_loop(0, chunks, sums, (zeros, zeros))
        inverse = 1.0 / jnp.sum(norm, axis=0, keepdims=True)
        delta = jnp.sum(weighted, axis=0, keepdims=True) * inverse

        def grads(t, dq):
            keys = pl.ds(pl.multiple_of(keys_at(t) * BLOCK, BLOCK), CHUNK)
            p = scores[slot(t), :] * inverse
            ds = p * (dprobs[slot(t), :] - delta)
            p_low = p.astype(jnp.bfloat16)
            ds_low = ds.astype(jnp.bfloat16)
            dk_total[keys, :] += dot(ds_low, q, (1, 0))
            dv_total[keys, :] += dot(p_low, g, (1, 0))
            return dq + dot(key_rows(t), ds_low, (0, 0))

        dq = lax.fori_loop(0, chunks, grads, jnp.zeros((HEAD, rows), jnp.float32))
        dq = (dq * SCALE).T.astype(jnp.bfloat16)
        for h in range(heads):
            dq_ref[j, :, h * HEAD : (h + 1) * HEAD] = dq[h * part : (h + 1) * part, :]
        return carry

    lax.fori_loop(0, tiles, tile, 0)
    for dc, dk_out, dv_out in ((0, dk_own, dv_own), (1, dk_sib, dv_sib)):
        for dx in range(nx):
            for dz in range(nz):
                begin = pl.multiple_of(block_of(dz, dx, dc) * BLOCK, BLOCK)
                dk_out[dx, dz] = dk_total[pl.ds(begin, 2 * BLOCK), :].astype(jnp.bfloat16)
                dv_out[dz, dx] = dv_total[pl.ds(begin, 2 * BLOCK), :].astype(jnp.bfloat16)


def grads_call(place, q, g, k_own, k_sib, v_own, v_sib):
    part, width = q.shape[1:]
    rows = part * width // HEAD
    nx, nz = len(k_own), len(v_own)
    blocks = nx * nz * 4
    pieces = [*k_own, *k_sib, *v_own, *v_sib]
    whole = pl.BlockSpec(memory_space=pltpu.VMEM)
    dk_shape = jax.ShapeDtypeStruct((nx, nz, 2 * BLOCK, HEAD), jnp.bfloat16)
    dv_shape = jax.ShapeDtypeStruct((nz, nx, 2 * BLOCK, HEAD), jnp.bfloat16)
    return pl.pallas_call(
        lambda *refs: attention_grads((nz, nx), *refs),
        name="attention_grads",
        out_shape=(jax.ShapeDtypeStruct(q.shape, jnp.bfloat16), dk_shape, dk_shape, dv_shape, dv_shape),
        in_specs=[pl.BlockSpec(memory_space=pltpu.SMEM), whole, whole]
        + [pl.BlockSpec(memory_space=pl.ANY)] * len(pieces),
        out_specs=(whole,) * 5,
        scratch_shapes=[
            pltpu.VMEM((rows, HEAD), jnp.bfloat16),
            pltpu.VMEM((rows, HEAD), jnp.bfloat16),
            pltpu.VMEM((blocks, BLOCK + DOC_ROWS, HEAD), jnp.bfloat16),
            pltpu.VMEM((blocks, BLOCK, HEAD), jnp.bfloat16),
            pltpu.VMEM((LONGEST * BLOCK, rows), jnp.float32),
            pltpu.VMEM((LONGEST * BLOCK, rows), jnp.float32),
            pltpu.VMEM((blocks * BLOCK, HEAD), jnp.float32),
            pltpu.VMEM((blocks * BLOCK, HEAD), jnp.float32),
            pltpu.SemaphoreType.DMA((blocks,)),
        ],
        compiler_params=pltpu.CompilerParams(vmem_limit_bytes=48 * 1024 * 1024),
        cost_estimate=pl.CostEstimate(
            flops=10 * 20 * 1024 * 128 * 128, bytes_accessed=16 * 1024 * 1024, transcendentals=0
        ),
    )(place, q, g, *pieces)


def per_device(queries, keys, values, grad_out, block_docs):
    rows, width = queries.shape
    inner_size, outer_size = lax.axis_size("inner"), lax.axis_size("outer")
    nz, nx = inner_size // 2, outer_size // 2
    inner, outer = lax.axis_index("inner"), lax.axis_index("outer")
    z, core = lax.div(inner, 2), lax.rem(inner, 2)
    x, y = lax.div(outer, 2), lax.rem(outer, 2)
    part = rows // nz

    def moved(value, dz=0, dx=0, dy=0, dc=0):
        hops = []
        for source in range(inner_size * outer_size):
            i, o = divmod(source, outer_size)
            to_inner = (i // 2 + dz) % nz * 2 + (i % 2 + dc) % 2
            to_outer = (o // 2 + dx) % nx * 2 + (o % 2 + dy) % 2
            hops.append((source, to_inner * outer_size + to_outer))
        return lax.ppermute(value, CONTEXT, hops)

    doc_rows = jnp.broadcast_to(block_docs.astype(jnp.bfloat16)[:, None], (DOC_ROWS, HEAD))
    packed = jnp.concatenate([keys, doc_rows, values])
    other = moved(packed, dy=1)
    pair = jnp.where(y == 0, jnp.stack([packed, other]), jnp.stack([other, packed]))
    split = BLOCK + DOC_ROWS
    k_pair, v_pair = pair[:, :split], pair[:, split:]

    both = jnp.concatenate([queries, grad_out], axis=1)

    def piece_for(peer):
        return lax.dynamic_slice_in_dim(both, lax.rem(peer, nz) * part, part, 0)

    pieces = [piece_for(z)] + [moved(piece_for(z + by), dz=by) for by in range(1, nz)]
    q = jnp.stack([piece[:, :width] for piece in pieces])
    g = jnp.stack([piece[:, width:] for piece in pieces])

    k_line = jnp.stack([k_pair] + [moved(k_pair, dz=by) for by in range(1, nz)])
    v_line = jnp.stack([v_pair] + [moved(v_pair, dx=by) for by in range(1, nx)])
    k_own = [k_line] + [moved(k_line, dx=by) for by in range(1, nx)]
    v_own = [v_line] + [moved(v_line, dz=by) for by in range(1, nz)]
    k_sib = [moved(piece, dc=1) for piece in k_own]
    v_sib = [moved(piece, dc=1) for piece in v_own]

    place = jnp.stack([z, x, y, core]).astype(jnp.int32)
    dq, dk_own, dk_sib, dv_own, dv_sib = grads_call(place, q, g, k_own, k_sib, v_own, v_sib)

    returned = jnp.stack([dq[0]] + [moved(dq[by], dz=-by) for by in range(1, nz)])
    order = lax.rem(jnp.arange(nz) - z + nz, nz)
    grad_queries = jnp.take(returned, order, axis=0).reshape(rows, width)

    def added(terms):
        total = terms[0].astype(jnp.float32)
        for term in terms[1:]:
            total = total + term.astype(jnp.float32)
        return total

    def low(value):
        return value.astype(jnp.bfloat16)

    def line_sum(value, **axis):
        ((name, count),) = axis.items()
        return added([value[0]] + [moved(value[by], **{name: by}) for by in range(1, count)])

    dk = low(added([dk_own, moved(dk_sib, dc=1)]))
    dv = low(added([dv_own, moved(dv_sib, dc=1)]))
    dk = low(line_sum(dk, dx=nx))
    dv = low(line_sum(dv, dz=nz))
    dk = low(line_sum(dk, dz=nz))
    dv = low(line_sum(dv, dx=nx))
    sums = jnp.concatenate([dk, dv], axis=1).reshape(2, BLOCK, 2 * HEAD)
    keep = jnp.where(y == 0, sums[0], sums[1])
    send = jnp.where(y == 0, sums[1], sums[0])
    total = added([keep, moved(send, dy=1)])
    return grad_queries, low(SCALE * total[:, :HEAD]), low(total[:, HEAD:])


def solution(mesh):
    wide = P(CONTEXT, "head")
    return jax.shard_map(
        per_device,
        mesh=mesh,
        in_specs=(wide, wide, wide, wide, P(CONTEXT)),
        out_specs=(wide, wide, wide),
        check_vma=False,
    )
```

```python
import math

import jax
import jax.numpy as jnp
from jax import lax
from jax.experimental import pallas as pl
from jax.experimental.pallas import tpu as pltpu
from jax.sharding import PartitionSpec as P

NEG = -1e30
HEAD = 128
BLOCK = 128
DOC_ROWS = 16
CHUNK_BLOCKS = 4
CHUNK = CHUNK_BLOCKS * BLOCK
LONGEST = 40
SCALE = float(HEAD) ** (-0.5)
TO_EXP2 = SCALE * math.log2(math.e)
CONTEXT = ("inner", "outer")


def dot(lhs, rhs, over):
    return lax.dot_general(lhs, rhs, ((over[:1], over[1:]), ((), ())), preferred_element_type=jnp.float32)


def attention_grads(sizes, *refs):
    nz, nx = sizes
    lines = nz
    place_ref, q_ref, g_ref = refs[:3]
    pieces = (refs[3 : 3 + lines], refs[3 + lines : 3 + 2 * lines])
    dq_ref, keep_ref, send_ref = refs[3 + 2 * lines : 6 + 2 * lines]
    q_rows, g_rows, kv_all, scores, dprobs, totals, sem = refs[6 + 2 * lines :]
    blocks = kv_all.shape[1]
    tiles, part, width = q_ref.shape
    heads = width // HEAD
    rows = heads * part
    z, x, y, core = (place_ref[i] for i in range(4))
    k_all = kv_all.at[0]
    v_all = kv_all.at[1]
    dk_total = totals.at[0]
    dv_total = totals.at[1]

    def block_of(dz, dx, c):
        return (lax.rem(z + dz, nz) * 2 + c) * (2 * nx) + lax.rem(x + dx, nx) * 2

    def ordered(which, i, j):
        return jnp.where(which == 0, j, i), jnp.where(which == 0, i, j)

    copies = []
    for which, arrived in ((core, pieces[0]), (1 - core, pieces[1])):
        for i in range(lines):
            for j in range(lines):
                dz, dx = ordered(which, lines - i, lines - j)
                for c in range(2):
                    to = kv_all.at[which, pl.ds(block_of(dz, dx, c), 2)]
                    copies.append(pltpu.make_async_copy(arrived[i].at[j, c], to, sem.at[len(copies)]))
    for copy in copies:
        copy.start()
    totals[...] = jnp.zeros_like(totals)
    row_token = z * part + lax.rem(lax.broadcasted_iota(jnp.int32, (CHUNK, rows), 1), part)
    key_token = lax.broadcasted_iota(jnp.int32, (CHUNK, rows), 0)
    for copy in copies:
        copy.wait()

    def fold(value, combine):
        return combine(value.reshape(CHUNK // 8, 8, rows), axis=0)

    def tile(j, carry):
        block = (lax.rem(z + nz - j, nz) * 2 + core) * (2 * nx) + x * 2 + y
        docs = k_all[:, BLOCK:, :].astype(jnp.float32)
        mine = k_all[pl.ds(block, 1), BLOCK:, :].astype(jnp.float32)
        before = jnp.sum(jnp.where(docs < mine, 1.0, 0.0), axis=0)
        first = jnp.max(before).astype(jnp.int32)
        for h in range(heads):
            q_rows[h * part : (h + 1) * part, :] = q_ref[j, :, h * HEAD : (h + 1) * HEAD]
            g_rows[h * part : (h + 1) * part, :] = g_ref[j, :, h * HEAD : (h + 1) * HEAD]
        q = q_rows[...]
        g = g_rows[...]
        chunks = lax.div(block - first + CHUNK_BLOCKS, CHUNK_BLOCKS)

        def keys_at(t):
            return jnp.minimum(first + t * CHUNK_BLOCKS, blocks - CHUNK_BLOCKS)

        def key_rows(t):
            return k_all[pl.ds(keys_at(t), CHUNK_BLOCKS), :BLOCK, :].reshape(CHUNK, HEAD)

        def slot(t):
            return pl.ds(pl.multiple_of(t * CHUNK, CHUNK), CHUNK)

        def full_scores(t, top):
            s = dot(key_rows(t), q, (1, 1))
            scores[slot(t), :] = s
            return jnp.maximum(top, fold(s, jnp.max))

        last = chunks - 1
        top = lax.fori_loop(0, last, full_scores, jnp.full((8, rows), NEG, jnp.float32))
        begin = keys_at(last)
        skipped = (first + last * CHUNK_BLOCKS - begin) * BLOCK
        mask = (key_token <= row_token + (block - begin) * BLOCK) & (key_token >= skipped)
        s = jnp.where(mask, dot(key_rows(last), q, (1, 1)), NEG)
        scores[slot(last), :] = s
        top = jnp.max(jnp.maximum(top, fold(s, jnp.max)), axis=0, keepdims=True) * TO_EXP2

        def sums(t, state):
            norm, weighted = state
            e = jnp.exp2(scores[slot(t), :] * TO_EXP2 - top)
            scores[slot(t), :] = e
            value_rows = v_all[pl.ds(keys_at(t), CHUNK_BLOCKS), :BLOCK, :].reshape(CHUNK, HEAD)
            dp = dot(value_rows, g, (1, 1))
            dprobs[slot(t), :] = dp
            return norm + fold(e, jnp.sum), weighted + fold(e * dp, jnp.sum)

        zeros = jnp.zeros((8, rows), jnp.float32)
        norm, weighted = lax.fori_loop(0, chunks, sums, (zeros, zeros))
        inverse = 1.0 / jnp.sum(norm, axis=0, keepdims=True)
        delta = jnp.sum(weighted, axis=0, keepdims=True) * inverse

        def grads(t, dq):
            keys = pl.ds(pl.multiple_of(keys_at(t) * BLOCK, BLOCK), CHUNK)
            p = scores[slot(t), :] * inverse
            ds = p * (dprobs[slot(t), :] - delta)
            p_low = p.astype(jnp.bfloat16)
            ds_low = ds.astype(jnp.bfloat16)
            dk_total[keys, :] += dot(ds_low, q, (1, 0))
            dv_total[keys, :] += dot(p_low, g, (1, 0))
            return dq + dot(key_rows(t), ds_low, (0, 0))

        dq = lax.fori_loop(0, chunks, grads, jnp.zeros((HEAD, rows), jnp.float32))
        dq = (dq * SCALE).T.astype(jnp.bfloat16)
        for h in range(heads):
            dq_ref[j, :, h * HEAD : (h + 1) * HEAD] = dq[h * part : (h + 1) * part, :]
        return carry

    lax.fori_loop(0, tiles, tile, 0)
    for which, out in ((core, keep_ref), (1 - core, send_ref)):
        for i in range(lines):
            for j in range(lines):
                dz, dx = ordered(which, i, j)
                for c in range(2):
                    begin = pl.multiple_of(block_of(dz, dx, c) * BLOCK, BLOCK)
                    out[i, j, c] = totals[which, pl.ds(begin, 2 * BLOCK), :].astype(jnp.bfloat16)


def grads_call(sizes, place, q, g, mine, theirs):
    part, width = q.shape[1:]
    rows = part * width // HEAD
    nz, nx = sizes
    blocks = nx * nz * 4
    pieces = [*mine, *theirs]
    whole = pl.BlockSpec(memory_space=pltpu.VMEM)
    sums_shape = jax.ShapeDtypeStruct((nz, nx, 2, 2 * BLOCK, HEAD), jnp.bfloat16)
    return pl.pallas_call(
        lambda *refs: attention_grads(sizes, *refs),
        name="attention_grads",
        out_shape=(jax.ShapeDtypeStruct(q.shape, jnp.bfloat16), sums_shape, sums_shape),
        in_specs=[pl.BlockSpec(memory_space=pltpu.SMEM), whole, whole]
        + [pl.BlockSpec(memory_space=pl.ANY)] * len(pieces),
        out_specs=(whole,) * 3,
        scratch_shapes=[
            pltpu.VMEM((rows, HEAD), jnp.bfloat16),
            pltpu.VMEM((rows, HEAD), jnp.bfloat16),
            pltpu.VMEM((2, blocks, BLOCK + DOC_ROWS, HEAD), jnp.bfloat16),
            pltpu.VMEM((LONGEST * BLOCK, rows), jnp.float32),
            pltpu.VMEM((LONGEST * BLOCK, rows), jnp.float32),
            pltpu.VMEM((2, blocks * BLOCK, HEAD), jnp.float32),
            pltpu.SemaphoreType.DMA((blocks,)),
        ],
        compiler_params=pltpu.CompilerParams(vmem_limit_bytes=48 * 1024 * 1024),
        cost_estimate=pl.CostEstimate(
            flops=10 * 20 * 1024 * 128 * 128, bytes_accessed=16 * 1024 * 1024, transcendentals=0
        ),
    )(place, q, g, *pieces)


def low(value):
    return value.astype(jnp.bfloat16)


def added(terms):
    total = terms[0].astype(jnp.float32)
    for term in terms[1:]:
        total = total + term.astype(jnp.float32)
    return total


def per_device(queries, keys, values, grad_out, block_docs):
    rows, width = queries.shape
    inner_size, outer_size = lax.axis_size("inner"), lax.axis_size("outer")
    nz, nx = inner_size // 2, outer_size // 2
    inner, outer = lax.axis_index("inner"), lax.axis_index("outer")
    z, core = lax.div(inner, 2), lax.rem(inner, 2)
    x, y = lax.div(outer, 2), lax.rem(outer, 2)
    part = rows // nz
    lines = nz

    def moved(value, step):
        hops = []
        for source in range(inner_size * outer_size):
            i, o = divmod(source, outer_size)
            dz, dx, dy, dc = step(i % 2)
            to_inner = (i // 2 + dz) % nz * 2 + (i % 2 + dc) % 2
            to_outer = (o // 2 + dx) % nx * 2 + (o % 2 + dy) % 2
            hops.append((source, to_inner * outer_size + to_outer))
        return lax.ppermute(value, CONTEXT, hops)

    def other_core(value):
        return moved(value, lambda c: (0, 0, 0, 1))

    def other_y(value):
        return moved(value, lambda c: (0, 0, 1, 0))

    def along_z(value, by):
        return moved(value, lambda c: (by, 0, 0, 0))

    def along_first(value, by):
        return moved(value, lambda c: (0, by, 0, 0) if c else (by, 0, 0, 0))

    def along_second(value, by):
        return moved(value, lambda c: (by, 0, 0, 0) if c else (0, by, 0, 0))

    def in_order(index, mine, theirs, axis):
        return jnp.where(
            index == 0, jnp.stack([mine, theirs], axis=axis), jnp.stack([theirs, mine], axis=axis)
        )

    docs = jnp.broadcast_to(low(block_docs)[:, None], (DOC_ROWS, HEAD))
    k_rows, v_rows = jnp.concatenate([keys, docs]), jnp.concatenate([values, docs])
    kept = jnp.where(core == 0, k_rows, v_rows)
    given = jnp.where(core == 0, v_rows, k_rows)
    unit = in_order(core, kept, other_core(given), 0)
    unit = in_order(y, unit, other_y(unit), 1)
    line = jnp.stack([unit] + [along_first(unit, by) for by in range(1, lines)])
    mine = [line] + [along_second(line, by) for by in range(1, lines)]
    theirs = [other_core(piece) for piece in mine]

    both = jnp.concatenate([queries, grad_out], axis=1)

    def piece_for(peer):
        return lax.dynamic_slice_in_dim(both, lax.rem(peer, nz) * part, part, 0)

    pieces = [piece_for(z)] + [along_z(piece_for(z + by), by) for by in range(1, nz)]
    q = jnp.stack([piece[:, :width] for piece in pieces])
    g = jnp.stack([piece[:, width:] for piece in pieces])

    place = jnp.stack([z, x, y, core]).astype(jnp.int32)
    dq, keep, send = grads_call((nz, nx), place, q, g, mine, theirs)

    total = low(added([keep, other_core(send)]))
    arrived = [along_second(total[by], by) for by in range(1, lines)]
    dq, arrived[0] = lax.optimization_barrier((dq, arrived[0]))
    returned = jnp.stack([dq[0]] + [along_z(dq[by], -by) for by in range(1, nz)])
    total = low(added([total[0]] + arrived))
    total = low(added([total[0]] + [along_first(total[by], by) for by in range(1, lines)]))
    total = total.reshape(2, 2, BLOCK, HEAD)
    ours = jnp.where(y == 0, total[:, 0], total[:, 1])
    far = jnp.where(y == 0, total[:, 1], total[:, 0])
    total = added([ours, other_y(far)])
    total = low(jnp.where(core == 0, SCALE * total, total))
    mine = jnp.where(core == 0, total[0], total[1])
    theirs = other_core(jnp.where(core == 0, total[1], total[0]))
    grad_keys = jnp.where(core == 0, mine, theirs)
    grad_values = jnp.where(core == 0, theirs, mine)

    order = lax.rem(jnp.arange(nz) - z + nz, nz)
    grad_queries = jnp.take(returned, order, axis=0).reshape(rows, width)
    return grad_queries, grad_keys, grad_values


def solution(mesh):
    wide = P(CONTEXT, "head")
    return jax.shard_map(
        per_device,
        mesh=mesh,
        in_specs=(wide, wide, wide, wide, P(CONTEXT)),
        out_specs=(wide, wide, wide),
        check_vma=False,
    )
```

```python
import math

import jax
import jax.numpy as jnp
from jax import lax
from jax.experimental import pallas as pl
from jax.experimental.pallas import tpu as pltpu
from jax.sharding import PartitionSpec as P

NEG = -1e30
HEAD = 128
BLOCK = 128
DOC_ROWS = 16
CHUNK_BLOCKS = 8
CHUNK = CHUNK_BLOCKS * BLOCK
LONGEST = 40
SCALE = float(HEAD) ** (-0.5)
TO_EXP2 = SCALE * math.log2(math.e)
CONTEXT = ("inner", "outer")


def dot(lhs, rhs, over):
    return lax.dot_general(lhs, rhs, ((over[:1], over[1:]), ((), ())), preferred_element_type=jnp.float32)


def attention_grads(sizes, *refs):
    nz, nx = sizes
    lines = nz
    place_ref, q_ref, g_ref = refs[:3]
    pieces = (refs[3 : 3 + lines], refs[3 + lines : 3 + 2 * lines])
    refs = refs[3 + 2 * lines :]
    dq_ref = refs[0]
    sums = (refs[1 : 1 + lines], refs[1 + lines : 1 + 2 * lines])
    q_rows, g_rows, q_cols, g_cols, docs_all, kv_all, scores, dprobs, totals = refs[1 + 2 * lines :]
    blocks = kv_all.shape[1]
    tiles, part, width = q_ref.shape
    heads = width // HEAD
    rows = heads * part
    z, x, y, core = (place_ref[i] for i in range(4))
    k_all = kv_all.at[0]
    v_all = kv_all.at[1]
    dk_total = totals.at[0]
    dv_total = totals.at[1]

    steps = range(lines)
    z_at = [lax.rem(z + by, nz) * (4 * nx) for by in steps]
    x_at = [lax.rem(x + by, nx) * 2 for by in steps]

    def places(which):
        return [
            [
                jnp.where(which == 0, x_at[i], z_at[i]) + jnp.where(which == 0, z_at[j], x_at[j])
                for j in steps
            ]
            for i in steps
        ]

    spots = (places(core), places(1 - core))

    for which, arrived, spot in ((core, pieces[0], spots[0]), (1 - core, pieces[1], spots[1])):
        for i in steps:
            for j in steps:
                for c in range(2):
                    rows_of = arrived[i][j, 2 * c * BLOCK : 2 * (c + 1) * BLOCK]
                    kv_all[which, pl.ds(spot[-i][-j] + 2 * nx * c, 2)] = rows_of.reshape(2, BLOCK, HEAD)
    for i in steps:
        for j in steps:
            docs_all[i * lines + j] = pieces[0][i][j, 4 * BLOCK :].astype(jnp.float32)
    totals[...] = jnp.zeros_like(totals)
    row_token = z * part + lax.rem(lax.broadcasted_iota(jnp.int32, (CHUNK, rows), 1), part)
    key_token = lax.broadcasted_iota(jnp.int32, (CHUNK, rows), 0)

    def fold(value, combine):
        return combine(value.reshape(CHUNK // 8, 8, rows), axis=0)

    def tile(j, carry):
        block = (lax.rem(z + nz - j, nz) * 2 + core) * (2 * nx) + x * 2 + y
        doc = docs_all[jnp.where(core == 0, j, j * lines), pl.ds(4 * (2 * core + y), 1), :]
        before = jnp.sum(jnp.where(docs_all[...] < doc, 0.25, 0.0), axis=(0, 1))
        first = jnp.max(before).astype(jnp.int32)
        for h in range(heads):
            q_rows[h * part : (h + 1) * part, :] = q_ref[j, :, h * HEAD : (h + 1) * HEAD]
            g_rows[h * part : (h + 1) * part, :] = g_ref[j, :, h * HEAD : (h + 1) * HEAD]
        q = q_rows[...]
        g = g_rows[...]
        q_cols[...] = q.T
        g_cols[...] = g.T
        chunks = lax.div(block - first + CHUNK_BLOCKS, CHUNK_BLOCKS)

        def keys_at(t):
            return jnp.minimum(first + t * CHUNK_BLOCKS, blocks - CHUNK_BLOCKS)

        def key_rows(t):
            return k_all[pl.ds(keys_at(t), CHUNK_BLOCKS)].reshape(CHUNK, HEAD)

        def slot(t):
            return pl.ds(pl.multiple_of(t * CHUNK, CHUNK), CHUNK)

        def full_scores(t, top):
            s = dot(key_rows(t), q_cols[...], (1, 0))
            scores[slot(t), :] = s
            return jnp.maximum(top, fold(s, jnp.max))

        last = chunks - 1
        top = lax.fori_loop(0, last, full_scores, jnp.full((8, rows), NEG, jnp.float32))
        begin = keys_at(last)
        skipped = (first + last * CHUNK_BLOCKS - begin) * BLOCK
        mask = (key_token <= row_token + (block - begin) * BLOCK) & (key_token >= skipped)
        s = jnp.where(mask, dot(key_rows(last), q_cols[...], (1, 0)), NEG)
        scores[slot(last), :] = s
        top = jnp.max(jnp.maximum(top, fold(s, jnp.max)), axis=0, keepdims=True) * TO_EXP2

        def sums(t, state):
            norm, weighted = state
            e = jnp.exp2(scores[slot(t), :] * TO_EXP2 - top)
            scores[slot(t), :] = e
            value_rows = v_all[pl.ds(keys_at(t), CHUNK_BLOCKS)].reshape(CHUNK, HEAD)
            dp = dot(value_rows, g_cols[...], (1, 0))
            dprobs[slot(t), :] = dp
            return norm + fold(e, jnp.sum), weighted + fold(e * dp, jnp.sum)

        zeros = jnp.zeros((8, rows), jnp.float32)
        norm, weighted = lax.fori_loop(0, chunks, sums, (zeros, zeros))
        inverse = 1.0 / jnp.sum(norm, axis=0, keepdims=True)
        delta = jnp.sum(weighted, axis=0, keepdims=True) * inverse

        def grads(t, dq):
            keys = pl.ds(pl.multiple_of(keys_at(t) * BLOCK, BLOCK), CHUNK)
            p = scores[slot(t), :] * inverse
            ds = p * (dprobs[slot(t), :] - delta)
            p_low = p.astype(jnp.bfloat16)
            ds_low = ds.astype(jnp.bfloat16)
            dk_total[keys, :] += dot(ds_low, q, (1, 0))
            dv_total[keys, :] += dot(p_low, g, (1, 0))
            return dq + dot(key_rows(t), ds_low, (0, 0))

        dq = lax.fori_loop(0, chunks, grads, jnp.zeros((HEAD, rows), jnp.float32))
        dq = (dq * SCALE).T.astype(jnp.bfloat16)
        for h in range(heads):
            dq_ref[j, :, h * HEAD : (h + 1) * HEAD] = dq[h * part : (h + 1) * part, :]
        return carry

    lax.fori_loop(0, tiles, tile, 0)
    for which, out, spot in ((core, sums[0], spots[0]), (1 - core, sums[1], spots[1])):
        for i in steps:
            for j in steps:
                for c in range(2):
                    begin = pl.multiple_of((spot[i][j] + 2 * nx * c) * BLOCK, BLOCK)
                    out[i][j, c] = totals[which, pl.ds(begin, 2 * BLOCK), :].astype(jnp.bfloat16)


def grads_call(sizes, place, q, g, mine, theirs):
    part, width = q.shape[1:]
    rows = part * width // HEAD
    nz, nx = sizes
    blocks = nx * nz * 4
    pieces = [*mine, *theirs]
    whole = pl.BlockSpec(memory_space=pltpu.VMEM)
    sums_shape = jax.ShapeDtypeStruct((nx, 2, 2 * BLOCK, HEAD), jnp.bfloat16)
    return pl.pallas_call(
        lambda *refs: attention_grads(sizes, *refs),
        name="attention_grads",
        out_shape=(jax.ShapeDtypeStruct(q.shape, jnp.bfloat16),) + (sums_shape,) * len(pieces),
        in_specs=[pl.BlockSpec(memory_space=pltpu.SMEM)] + [whole] * (2 + len(pieces)),
        out_specs=(whole,) * (1 + len(pieces)),
        scratch_shapes=[
            pltpu.VMEM((rows, HEAD), jnp.bfloat16),
            pltpu.VMEM((rows, HEAD), jnp.bfloat16),
            pltpu.VMEM((HEAD, rows), jnp.bfloat16),
            pltpu.VMEM((HEAD, rows), jnp.bfloat16),
            pltpu.VMEM((nz * nx, DOC_ROWS, HEAD), jnp.float32),
            pltpu.VMEM((2, blocks, BLOCK, HEAD), jnp.bfloat16),
            pltpu.VMEM((LONGEST * BLOCK, rows), jnp.float32),
            pltpu.VMEM((LONGEST * BLOCK, rows), jnp.float32),
            pltpu.VMEM((2, blocks * BLOCK, HEAD), jnp.float32),
        ],
        compiler_params=pltpu.CompilerParams(vmem_limit_bytes=48 * 1024 * 1024),
        cost_estimate=pl.CostEstimate(
            flops=10 * 20 * 1024 * 128 * 128, bytes_accessed=16 * 1024 * 1024, transcendentals=0
        ),
    )(place, q, g, *pieces)


def low(value):
    return value.astype(jnp.bfloat16)


def added(terms):
    total = terms[0].astype(jnp.float32)
    for term in terms[1:]:
        total = total + term.astype(jnp.float32)
    return total


def per_device(queries, keys, values, grad_out, block_docs):
    rows, width = queries.shape
    inner_size, outer_size = lax.axis_size("inner"), lax.axis_size("outer")
    nz, nx = inner_size // 2, outer_size // 2
    inner, outer = lax.axis_index("inner"), lax.axis_index("outer")
    z, core = lax.div(inner, 2), lax.rem(inner, 2)
    x, y = lax.div(outer, 2), lax.rem(outer, 2)
    part = rows // nz
    lines = nz

    def moved(value, step):
        hops = []
        for source in range(inner_size * outer_size):
            i, o = divmod(source, outer_size)
            dz, dx, dy, dc = step(i % 2)
            to_inner = (i // 2 + dz) % nz * 2 + (i % 2 + dc) % 2
            to_outer = (o // 2 + dx) % nx * 2 + (o % 2 + dy) % 2
            hops.append((source, to_inner * outer_size + to_outer))
        return lax.ppermute(value, CONTEXT, hops)

    def other_core(value):
        return moved(value, lambda c: (0, 0, 0, 1))

    def other_y(value):
        return moved(value, lambda c: (0, 0, 1, 0))

    def along_z(value, by):
        return moved(value, lambda c: (by, 0, 0, 0))

    def along_first(value, by):
        return moved(value, lambda c: (0, by, 0, 0) if c else (by, 0, 0, 0))

    def along_second(value, by):
        return moved(value, lambda c: (by, 0, 0, 0) if c else (0, by, 0, 0))

    def in_order(index, mine, theirs, axis):
        return jnp.where(
            index == 0, jnp.stack([mine, theirs], axis=axis), jnp.stack([theirs, mine], axis=axis)
        )

    both = jnp.concatenate([queries, grad_out], axis=1)

    def piece_for(peer):
        return lax.dynamic_slice_in_dim(both, lax.rem(peer, nz) * part, part, 0)

    pieces = [piece_for(z)] + [along_z(piece_for(z + by), by) for by in range(1, nz)]
    docs = jnp.broadcast_to(low(block_docs)[:, None], (DOC_ROWS, HEAD))
    k_rows, v_rows = jnp.concatenate([keys, docs]), jnp.concatenate([values, docs])
    kept = jnp.where(core == 0, k_rows, v_rows)
    given = jnp.where(core == 0, v_rows, k_rows)
    unit = in_order(core, kept, other_core(given), 0)
    unit = in_order(y, unit, other_y(unit), 1)
    unit = jnp.concatenate(
        [unit[:, :, :BLOCK].reshape(4 * BLOCK, HEAD), unit[:, :, BLOCK : BLOCK + 4].reshape(DOC_ROWS, HEAD)]
    )
    line = jnp.stack([unit] + [along_first(unit, by) for by in range(1, lines)])
    line, *pieces = lax.optimization_barrier((line, *pieces))
    q = jnp.stack([piece[:, :width] for piece in pieces])
    g = jnp.stack([piece[:, width:] for piece in pieces])
    mine = [line] + [along_second(line, by) for by in range(1, lines)]
    theirs = [other_core(piece) for piece in mine]

    place = jnp.stack([z, x, y, core]).astype(jnp.int32)
    dq, *sums = grads_call((nz, nx), place, q, g, mine, theirs)
    keep, send = sums[:lines], sums[lines:]

    totals = [None] * lines
    for by in [*range(1, lines), 0]:
        totals[by] = low(added([keep[by], other_core(send[by])]))
    arrived = [along_second(totals[by], by) for by in range(1, lines)]
    dq, totals[0] = lax.optimization_barrier((dq, totals[0]))
    returned = [dq[0]] + [along_z(dq[by], -by) for by in range(1, nz)]
    arrived, returned = lax.optimization_barrier((arrived, returned))
    total = low(added([totals[0]] + arrived))
    total = low(added([total[0]] + [along_first(total[by], by) for by in range(1, lines)]))
    total = total.reshape(2, 2, BLOCK, HEAD)
    ours = jnp.where(y == 0, total[:, 0], total[:, 1])
    far = jnp.where(y == 0, total[:, 1], total[:, 0])
    total = added([ours, other_y(far)])
    total = low(jnp.where(core == 0, SCALE * total, total))
    mine = jnp.where(core == 0, total[0], total[1])
    theirs = other_core(jnp.where(core == 0, total[1], total[0]))
    grad_keys = jnp.where(core == 0, mine, theirs)
    grad_values = jnp.where(core == 0, theirs, mine)

    order = lax.rem(jnp.arange(nz) - z + nz, nz)
    grad_queries = jnp.take(jnp.stack(returned), order, axis=0).reshape(rows, width)
    return grad_queries, grad_keys, grad_values


def solution(mesh):
    wide = P(CONTEXT, "head")
    return jax.shard_map(
        per_device,
        mesh=mesh,
        in_specs=(wide, wide, wide, wide, P(CONTEXT)),
        out_specs=(wide, wide, wide),
        check_vma=False,
    )
```

```python
import math

import jax
import jax.numpy as jnp
from jax import lax
from jax.experimental import pallas as pl
from jax.experimental.pallas import tpu as pltpu
from jax.sharding import PartitionSpec as P

NEG = -1e30
HEAD = 128
BLOCK = 128
DOC_ROWS = 16
CHUNK_BLOCKS = 8
CHUNK = CHUNK_BLOCKS * BLOCK
LONGEST = 40
SCALE = float(HEAD) ** (-0.5)
TO_EXP2 = SCALE * math.log2(math.e)
CONTEXT = ("inner", "outer")


def dot(lhs, rhs, over):
    return lax.dot_general(lhs, rhs, ((over[:1], over[1:]), ((), ())), preferred_element_type=jnp.float32)


def attention_grads(sizes, *refs):
    nz, nx = sizes
    lines = nz
    place_ref, q_ref, g_ref = refs[:3]
    pieces = (refs[3 : 4 + lines], refs[4 + lines : 5 + 2 * lines])
    refs = refs[5 + 2 * lines :]
    dq_ref = refs[0]
    sums = (refs[1 : 1 + lines], refs[1 + lines : 1 + 2 * lines])
    q_rows, g_rows, q_cols, g_cols, docs_all, kv_all, scores, dprobs, totals = refs[1 + 2 * lines :]
    blocks = kv_all.shape[1]
    tiles, part, width = q_ref.shape
    heads = width // HEAD
    rows = heads * part
    z, x, y, core = (place_ref[i] for i in range(4))
    k_all = kv_all.at[0]
    v_all = kv_all.at[1]
    dk_total = totals.at[0]
    dv_total = totals.at[1]

    steps = range(lines)
    z_at = [lax.rem(z + by, nz) * (4 * nx) for by in steps]
    x_at = [lax.rem(x + by, nx) * 2 for by in steps]

    def places(which):
        return [
            [
                jnp.where(which == 0, x_at[i], z_at[i]) + jnp.where(which == 0, z_at[j], x_at[j])
                for j in steps
            ]
            for i in steps
        ]

    spots = (places(core), places(1 - core))

    def unit_of(arrived, i, j):
        if i < 2:
            return arrived[i].at[j]
        if i == 2:
            return arrived[2 + j // 2].at[j % 2]
        return arrived[4].at[j]

    for which, arrived, spot in ((core, pieces[0], spots[0]), (1 - core, pieces[1], spots[1])):
        for i in steps:
            for j in steps:
                for c in range(2):
                    rows_of = unit_of(arrived, i, j)[2 * c * BLOCK : 2 * (c + 1) * BLOCK]
                    kv_all[which, pl.ds(spot[-i][-j] + 2 * nx * c, 2)] = rows_of.reshape(2, BLOCK, HEAD)
    for i in steps:
        for j in steps:
            docs_all[i * lines + j] = unit_of(pieces[0], i, j)[4 * BLOCK :].astype(jnp.float32)
    totals[...] = jnp.zeros_like(totals)
    row_token = z * part + lax.rem(lax.broadcasted_iota(jnp.int32, (CHUNK, rows), 1), part)
    key_token = lax.broadcasted_iota(jnp.int32, (CHUNK, rows), 0)

    def fold(value, combine):
        return combine(value.reshape(CHUNK // 8, 8, rows), axis=0)

    def tile(j, carry):
        block = (lax.rem(z + nz - j, nz) * 2 + core) * (2 * nx) + x * 2 + y
        doc = docs_all[jnp.where(core == 0, j, j * lines), pl.ds(4 * (2 * core + y), 1), :]
        before = jnp.sum(jnp.where(docs_all[...] < doc, 0.25, 0.0), axis=(0, 1))
        first = jnp.max(before).astype(jnp.int32)
        for h in range(heads):
            q_rows[h * part : (h + 1) * part, :] = q_ref[j, :, h * HEAD : (h + 1) * HEAD]
            g_rows[h * part : (h + 1) * part, :] = g_ref[j, :, h * HEAD : (h + 1) * HEAD]
        q = q_rows[...]
        g = g_rows[...]
        q_cols[...] = q.T
        g_cols[...] = g.T
        chunks = lax.div(block - first + CHUNK_BLOCKS, CHUNK_BLOCKS)

        def keys_at(t):
            return jnp.minimum(first + t * CHUNK_BLOCKS, blocks - CHUNK_BLOCKS)

        def key_rows(t):
            return k_all[pl.ds(keys_at(t), CHUNK_BLOCKS)].reshape(CHUNK, HEAD)

        def slot(t):
            return pl.ds(pl.multiple_of(t * CHUNK, CHUNK), CHUNK)

        def full_scores(t, top):
            s = dot(key_rows(t), q_cols[...], (1, 0))
            scores[slot(t), :] = s
            return jnp.maximum(top, fold(s, jnp.max))

        last = chunks - 1
        top = lax.fori_loop(0, last, full_scores, jnp.full((8, rows), NEG, jnp.float32))
        begin = keys_at(last)
        skipped = (first + last * CHUNK_BLOCKS - begin) * BLOCK
        mask = (key_token <= row_token + (block - begin) * BLOCK) & (key_token >= skipped)
        s = jnp.where(mask, dot(key_rows(last), q_cols[...], (1, 0)), NEG)
        scores[slot(last), :] = s
        top = jnp.max(jnp.maximum(top, fold(s, jnp.max)), axis=0, keepdims=True) * TO_EXP2

        def sums(t, state):
            norm, weighted = state
            e = jnp.exp2(scores[slot(t), :] * TO_EXP2 - top)
            scores[slot(t), :] = e
            value_rows = v_all[pl.ds(keys_at(t), CHUNK_BLOCKS)].reshape(CHUNK, HEAD)
            dp = dot(value_rows, g_cols[...], (1, 0))
            dprobs[slot(t), :] = dp
            return norm + fold(e, jnp.sum), weighted + fold(e * dp, jnp.sum)

        zeros = jnp.zeros((8, rows), jnp.float32)
        norm, weighted = lax.fori_loop(0, chunks, sums, (zeros, zeros))
        inverse = 1.0 / jnp.sum(norm, axis=0, keepdims=True)
        delta = jnp.sum(weighted, axis=0, keepdims=True) * inverse

        def grads(t, dq):
            keys = pl.ds(pl.multiple_of(keys_at(t) * BLOCK, BLOCK), CHUNK)
            p = scores[slot(t), :] * inverse
            ds = p * (dprobs[slot(t), :] - delta)
            p_low = p.astype(jnp.bfloat16)
            ds_low = ds.astype(jnp.bfloat16)
            dk_total[keys, :] += dot(ds_low, q, (1, 0))
            dv_total[keys, :] += dot(p_low, g, (1, 0))
            return dq + dot(key_rows(t), ds_low, (0, 0))

        dq = lax.fori_loop(0, chunks, grads, jnp.zeros((HEAD, rows), jnp.float32))
        dq = (dq * SCALE).T.astype(jnp.bfloat16)
        for h in range(heads):
            dq_ref[j, :, h * HEAD : (h + 1) * HEAD] = dq[h * part : (h + 1) * part, :]
        return carry

    lax.fori_loop(0, tiles, tile, 0)
    for which, out, spot in ((core, sums[0], spots[0]), (1 - core, sums[1], spots[1])):
        for i in steps:
            for j in steps:
                for c in range(2):
                    begin = pl.multiple_of((spot[i][j] + 2 * nx * c) * BLOCK, BLOCK)
                    out[i][j, c] = totals[which, pl.ds(begin, 2 * BLOCK), :].astype(jnp.bfloat16)


def grads_call(sizes, place, q, g, mine, theirs):
    part, width = q.shape[1:]
    rows = part * width // HEAD
    nz, nx = sizes
    blocks = nx * nz * 4
    pieces = [*mine, *theirs]
    whole = pl.BlockSpec(memory_space=pltpu.VMEM)
    sums_shape = jax.ShapeDtypeStruct((nx, 2, 2 * BLOCK, HEAD), jnp.bfloat16)
    return pl.pallas_call(
        lambda *refs: attention_grads(sizes, *refs),
        name="attention_grads",
        out_shape=(jax.ShapeDtypeStruct(q.shape, jnp.bfloat16),) + (sums_shape,) * (2 * nz),
        in_specs=[pl.BlockSpec(memory_space=pltpu.SMEM)] + [whole] * (2 + len(pieces)),
        out_specs=(whole,) * (1 + 2 * nz),
        scratch_shapes=[
            pltpu.VMEM((rows, HEAD), jnp.bfloat16),
            pltpu.VMEM((rows, HEAD), jnp.bfloat16),
            pltpu.VMEM((HEAD, rows), jnp.bfloat16),
            pltpu.VMEM((HEAD, rows), jnp.bfloat16),
            pltpu.VMEM((nz * nx, DOC_ROWS, HEAD), jnp.float32),
            pltpu.VMEM((2, blocks, BLOCK, HEAD), jnp.bfloat16),
            pltpu.VMEM((LONGEST * BLOCK, rows), jnp.float32),
            pltpu.VMEM((LONGEST * BLOCK, rows), jnp.float32),
            pltpu.VMEM((2, blocks * BLOCK, HEAD), jnp.float32),
        ],
        compiler_params=pltpu.CompilerParams(vmem_limit_bytes=48 * 1024 * 1024),
        cost_estimate=pl.CostEstimate(
            flops=10 * 20 * 1024 * 128 * 128, bytes_accessed=16 * 1024 * 1024, transcendentals=0
        ),
    )(place, q, g, *pieces)


def low(value):
    return value.astype(jnp.bfloat16)


def added(terms):
    total = terms[0].astype(jnp.float32)
    for term in terms[1:]:
        total = total + term.astype(jnp.float32)
    return total


def per_device(queries, keys, values, grad_out, block_docs):
    rows, width = queries.shape
    inner_size, outer_size = lax.axis_size("inner"), lax.axis_size("outer")
    nz, nx = inner_size // 2, outer_size // 2
    inner, outer = lax.axis_index("inner"), lax.axis_index("outer")
    z, core = lax.div(inner, 2), lax.rem(inner, 2)
    x, y = lax.div(outer, 2), lax.rem(outer, 2)
    part = rows // nz
    lines = nz

    def moved(value, step):
        hops = []
        for source in range(inner_size * outer_size):
            i, o = divmod(source, outer_size)
            dz, dx, dy, dc = step(i % 2)
            to_inner = (i // 2 + dz) % nz * 2 + (i % 2 + dc) % 2
            to_outer = (o // 2 + dx) % nx * 2 + (o % 2 + dy) % 2
            hops.append((source, to_inner * outer_size + to_outer))
        return lax.ppermute(value, CONTEXT, hops)

    def other_core(value):
        return moved(value, lambda c: (0, 0, 0, 1))

    def other_y(value):
        return moved(value, lambda c: (0, 0, 1, 0))

    def along_z(value, by):
        return moved(value, lambda c: (by, 0, 0, 0))

    def along_first(value, by):
        return moved(value, lambda c: (0, by, 0, 0) if c else (by, 0, 0, 0))

    def along_second(value, by):
        return moved(value, lambda c: (by, 0, 0, 0) if c else (0, by, 0, 0))

    def in_order(index, mine, theirs, axis):
        return jnp.where(
            index == 0, jnp.stack([mine, theirs], axis=axis), jnp.stack([theirs, mine], axis=axis)
        )

    both = jnp.concatenate([queries, grad_out], axis=1)

    def piece_for(peer):
        return lax.dynamic_slice_in_dim(both, lax.rem(peer, nz) * part, part, 0)

    pieces = [piece_for(z)] + [along_z(piece_for(z + by), by) for by in range(1, nz)]
    docs = jnp.broadcast_to(low(block_docs)[:, None], (DOC_ROWS, HEAD))
    k_rows, v_rows = jnp.concatenate([keys, docs]), jnp.concatenate([values, docs])
    kept = jnp.where(core == 0, k_rows, v_rows)
    given = jnp.where(core == 0, v_rows, k_rows)
    unit = in_order(core, kept, other_core(given), 0)
    unit = in_order(y, unit, other_y(unit), 1)
    unit, pieces[1], pieces[3] = lax.optimization_barrier((unit, pieces[1], pieces[3]))
    unit = jnp.concatenate(
        [unit[:, :, :BLOCK].reshape(4 * BLOCK, HEAD), unit[:, :, BLOCK : BLOCK + 4].reshape(DOC_ROWS, HEAD)]
    )
    line = jnp.stack([unit] + [along_first(unit, by) for by in range(1, lines)])
    line, *pieces = lax.optimization_barrier((line, *pieces))
    q = jnp.stack([piece[:, :width] for piece in pieces])
    g = jnp.stack([piece[:, width:] for piece in pieces])
    before, after = along_second(line, 1), along_second(line, -1)
    mine = [line, before, along_second(before[:2], 1), along_second(after[2:], -1), after]
    theirs = [other_core(piece) for piece in mine]

    place = jnp.stack([z, x, y, core]).astype(jnp.int32)
    dq, *sums = grads_call((nz, nx), place, q, g, mine, theirs)
    keep, send = sums[:lines], sums[lines:]

    swapped = [None] * lines
    for by in (2, 1, 3, 0):
        swapped[by] = other_core(send[by])
    far_up = low(added([keep[2][:2], swapped[2][:2]]))
    far_down = low(added([keep[2][2:], swapped[2][2:]]))
    far_up, far_down = along_second(far_up, 1), along_second(far_down, -1)
    rest = ((0, 0),) * 3
    up = low(added([keep[1], swapped[1], jnp.pad(far_up, ((0, 2),) + rest)]))
    down = low(added([keep[3], swapped[3], jnp.pad(far_down, ((2, 0),) + rest)]))
    dq, up, down = lax.optimization_barrier((dq, up, down))
    arrived = [along_second(up, 1), along_second(down, -1)]
    returned = [dq[0]] + [along_z(dq[by], -by) for by in range(1, nz)]
    arrived, returned = lax.optimization_barrier((arrived, returned))
    total = low(added([keep[0], swapped[0]] + arrived))
    total = low(added([total[0]] + [along_first(total[by], by) for by in range(1, lines)]))
    total = total.reshape(2, 2, BLOCK, HEAD)
    ours = jnp.where(y == 0, total[:, 0], total[:, 1])
    far = jnp.where(y == 0, total[:, 1], total[:, 0])
    total = added([ours, other_y(far)])
    total = low(jnp.where(core == 0, SCALE * total, total))
    mine = jnp.where(core == 0, total[0], total[1])
    theirs = other_core(jnp.where(core == 0, total[1], total[0]))
    grad_keys = jnp.where(core == 0, mine, theirs)
    grad_values = jnp.where(core == 0, theirs, mine)

    order = lax.rem(jnp.arange(nz) - z + nz, nz)
    grad_queries = jnp.take(jnp.stack(returned), order, axis=0).reshape(rows, width)
    return grad_queries, grad_keys, grad_values


def solution(mesh):
    wide = P(CONTEXT, "head")
    return jax.shard_map(
        per_device,
        mesh=mesh,
        in_specs=(wide, wide, wide, wide, P(CONTEXT)),
        out_specs=(wide, wide, wide),
        check_vma=False,
    )
```

```python
import math

import jax
import jax.numpy as jnp
from jax import lax
from jax.experimental import pallas as pl
from jax.experimental.pallas import tpu as pltpu
from jax.sharding import PartitionSpec as P

NEG = -1e30
HEAD = 128
BLOCK = 128
DOC_ROWS = 16
CHUNK_BLOCKS = 8
CHUNK = CHUNK_BLOCKS * BLOCK
LONGEST = 40
PEERS = 2
SCALE = float(HEAD) ** (-0.5)
TO_EXP2 = SCALE * math.log2(math.e)
CONTEXT = ("inner", "outer")


def dot(lhs, rhs, over):
    return lax.dot_general(lhs, rhs, ((over[:1], over[1:]), ((), ())), preferred_element_type=jnp.float32)


def attention_grads(sizes, *refs):
    nz, nx = sizes
    lines = nz
    place_ref, q_ref, g_ref = refs[:3]
    pieces = (refs[3 : 3 + lines], refs[3 + lines : 3 + 2 * lines])
    refs = refs[3 + 2 * lines :]
    dq_ref = refs[0]
    sums = (refs[1 : 1 + lines], refs[1 + lines : 1 + 2 * lines])
    q_rows, g_rows, q_cols, g_cols, docs_all, kv_all, scores, totals = refs[1 + 2 * lines :]
    blocks = kv_all.shape[1]
    tiles, part, width = q_ref.shape
    heads = width // HEAD
    rows = heads * part
    z, x, y, core = (place_ref[i] for i in range(4))
    k_all = kv_all.at[0]
    v_all = kv_all.at[1]
    dk_total = totals.at[0]
    dv_total = totals.at[1]

    steps = range(lines)
    z_at = [lax.rem(z + by, nz) * (4 * nx) for by in steps]
    x_at = [lax.rem(x + by, nx) * 2 for by in steps]

    def places(which):
        return [
            [
                jnp.where(which == 0, x_at[i], z_at[i]) + jnp.where(which == 0, z_at[j], x_at[j])
                for j in steps
            ]
            for i in steps
        ]

    spots = (places(core), places(1 - core))

    for which, arrived, spot in ((core, pieces[0], spots[0]), (1 - core, pieces[1], spots[1])):
        for i in steps:
            for j in steps:
                for c in range(2):
                    rows_of = arrived[i][j, 2 * c * BLOCK : 2 * (c + 1) * BLOCK]
                    kv_all[which, pl.ds(spot[-i][-j] + 2 * nx * c, 2)] = rows_of.reshape(2, BLOCK, HEAD)
    for i in steps:
        for j in steps:
            docs_all[i * lines + j] = pieces[0][i][j, 4 * BLOCK :].astype(jnp.float32)
    totals[...] = jnp.zeros_like(totals)
    apart = nz // tiles
    row_token = lax.div(z, apart) * part + lax.rem(lax.broadcasted_iota(jnp.int32, (CHUNK, rows), 1), part)
    key_token = lax.broadcasted_iota(jnp.int32, (CHUNK, rows), 0)

    def fold(value, combine):
        return combine(value.reshape(CHUNK // 8, 8, rows), axis=0)

    def tile(j, carry):
        dz = j * apart
        block = (lax.rem(z + nz - dz, nz) * 2 + core) * (2 * nx) + x * 2 + y
        doc = docs_all[jnp.where(core == 0, dz, dz * lines), pl.ds(4 * (2 * core + y), 1), :]
        before = jnp.sum(jnp.where(docs_all[...] < doc, 0.25, 0.0), axis=(0, 1))
        first = jnp.max(before).astype(jnp.int32)
        for h in range(heads):
            q_rows[h * part : (h + 1) * part, :] = q_ref[j, :, h * HEAD : (h + 1) * HEAD]
            g_rows[h * part : (h + 1) * part, :] = g_ref[j, :, h * HEAD : (h + 1) * HEAD]
        q = q_rows[...]
        g = g_rows[...]
        q_cols[...] = q.T
        g_cols[...] = g.T
        chunks = lax.div(block - first + CHUNK_BLOCKS, CHUNK_BLOCKS)

        def keys_at(t):
            return jnp.minimum(first + t * CHUNK_BLOCKS, blocks - CHUNK_BLOCKS)

        def key_rows(t):
            return k_all[pl.ds(keys_at(t), CHUNK_BLOCKS)].reshape(CHUNK, HEAD)

        def slot(t):
            return pl.ds(pl.multiple_of(t * CHUNK, CHUNK), CHUNK)

        def full_scores(t, top):
            s = dot(key_rows(t), q_cols[...], (1, 0))
            scores[slot(t), :] = s
            return jnp.maximum(top, fold(s, jnp.max))

        last = chunks - 1
        top = lax.fori_loop(0, last, full_scores, jnp.full((8, rows), NEG, jnp.float32))
        begin = keys_at(last)
        skipped = (first + last * CHUNK_BLOCKS - begin) * BLOCK
        mask = (key_token <= row_token + (block - begin) * BLOCK) & (key_token >= skipped)
        s = jnp.where(mask, dot(key_rows(last), q_cols[...], (1, 0)), NEG)
        scores[slot(last), :] = s
        top = jnp.max(jnp.maximum(top, fold(s, jnp.max)), axis=0, keepdims=True) * TO_EXP2

        def sums(t, state):
            norm, weighted = state
            e = jnp.exp2(scores[slot(t), :] * TO_EXP2 - top)
            scores[slot(t), :] = e
            value_rows = v_all[pl.ds(keys_at(t), CHUNK_BLOCKS)].reshape(CHUNK, HEAD)
            dp = dot(value_rows, g_cols[...], (1, 0))
            return norm + fold(e, jnp.sum), weighted + fold(e * dp, jnp.sum)

        zeros = jnp.zeros((8, rows), jnp.float32)
        norm, weighted = lax.fori_loop(0, chunks, sums, (zeros, zeros))
        inverse = 1.0 / jnp.sum(norm, axis=0, keepdims=True)
        delta = jnp.sum(weighted, axis=0, keepdims=True) * inverse

        def grads(t, dq):
            keys = pl.ds(pl.multiple_of(keys_at(t) * BLOCK, BLOCK), CHUNK)
            p = scores[slot(t), :] * inverse
            value_rows = v_all[pl.ds(keys_at(t), CHUNK_BLOCKS)].reshape(CHUNK, HEAD)
            ds = p * (dot(value_rows, g_cols[...], (1, 0)) - delta)
            p_low = p.astype(jnp.bfloat16)
            ds_low = ds.astype(jnp.bfloat16)
            dk_total[keys, :] += dot(ds_low, q, (1, 0))
            dv_total[keys, :] += dot(p_low, g, (1, 0))
            return dq + dot(key_rows(t), ds_low, (0, 0))

        dq = lax.fori_loop(0, chunks, grads, jnp.zeros((HEAD, rows), jnp.float32))
        dq = (dq * SCALE).T.astype(jnp.bfloat16)
        for h in range(heads):
            dq_ref[j, :, h * HEAD : (h + 1) * HEAD] = dq[h * part : (h + 1) * part, :]
        return carry

    lax.fori_loop(0, tiles, tile, 0)
    for which, out, spot in ((core, sums[0], spots[0]), (1 - core, sums[1], spots[1])):
        for i in steps:
            for j in steps:
                for c in range(2):
                    begin = pl.multiple_of((spot[i][j] + 2 * nx * c) * BLOCK, BLOCK)
                    out[i][j, c] = totals[which, pl.ds(begin, 2 * BLOCK), :].astype(jnp.bfloat16)


def grads_call(sizes, place, q, g, mine, theirs):
    part, width = q.shape[1:]
    rows = part * width // HEAD
    nz, nx = sizes
    blocks = nx * nz * 4
    pieces = [*mine, *theirs]
    whole = pl.BlockSpec(memory_space=pltpu.VMEM)
    sums_shape = jax.ShapeDtypeStruct((nx, 2, 2 * BLOCK, HEAD), jnp.bfloat16)
    return pl.pallas_call(
        lambda *refs: attention_grads(sizes, *refs),
        name="attention_grads",
        out_shape=(jax.ShapeDtypeStruct(q.shape, jnp.bfloat16),) + (sums_shape,) * len(pieces),
        in_specs=[pl.BlockSpec(memory_space=pltpu.SMEM)] + [whole] * (2 + len(pieces)),
        out_specs=(whole,) * (1 + len(pieces)),
        scratch_shapes=[
            pltpu.VMEM((rows, HEAD), jnp.bfloat16),
            pltpu.VMEM((rows, HEAD), jnp.bfloat16),
            pltpu.VMEM((HEAD, rows), jnp.bfloat16),
            pltpu.VMEM((HEAD, rows), jnp.bfloat16),
            pltpu.VMEM((nz * nx, DOC_ROWS, HEAD), jnp.float32),
            pltpu.VMEM((2, blocks, BLOCK, HEAD), jnp.bfloat16),
            pltpu.VMEM((LONGEST * BLOCK, rows), jnp.float32),
            pltpu.VMEM((2, blocks * BLOCK, HEAD), jnp.float32),
        ],
        compiler_params=pltpu.CompilerParams(vmem_limit_bytes=36 * 1024 * 1024),
        cost_estimate=pl.CostEstimate(
            flops=10 * 20 * 1024 * 128 * 128, bytes_accessed=16 * 1024 * 1024, transcendentals=0
        ),
    )(place, q, g, *pieces)


def low(value):
    return value.astype(jnp.bfloat16)


def added(terms):
    total = terms[0].astype(jnp.float32)
    for term in terms[1:]:
        total = total + term.astype(jnp.float32)
    return total


def per_device(queries, keys, values, grad_out, block_docs):
    rows, width = queries.shape
    inner_size, outer_size = lax.axis_size("inner"), lax.axis_size("outer")
    nz, nx = inner_size // 2, outer_size // 2
    inner, outer = lax.axis_index("inner"), lax.axis_index("outer")
    z, core = lax.div(inner, 2), lax.rem(inner, 2)
    x, y = lax.div(outer, 2), lax.rem(outer, 2)
    part = rows // PEERS
    apart = nz // PEERS
    lines = nz

    def moved(value, step):
        hops = []
        for source in range(inner_size * outer_size):
            i, o = divmod(source, outer_size)
            dz, dx, dy, dc = step(i % 2)
            to_inner = (i // 2 + dz) % nz * 2 + (i % 2 + dc) % 2
            to_outer = (o // 2 + dx) % nx * 2 + (o % 2 + dy) % 2
            hops.append((source, to_inner * outer_size + to_outer))
        return lax.ppermute(value, CONTEXT, hops)

    def other_core(value):
        return moved(value, lambda c: (0, 0, 0, 1))

    def other_y(value):
        return moved(value, lambda c: (0, 0, 1, 0))

    def diagonal(value):
        return moved(value, lambda c: (0, 0, 1, 1))

    def peer(value):
        return moved(value, lambda c: (apart, 0, 0, 0))

    def along_first(value, by):
        return moved(value, lambda c: (0, by, 0, 0) if c else (by, 0, 0, 0))

    def along_second(value, by):
        return moved(value, lambda c: (by, 0, 0, 0) if c else (0, by, 0, 0))

    def in_order(index, mine, theirs, axis):
        return jnp.where(
            index == 0, jnp.stack([mine, theirs], axis=axis), jnp.stack([theirs, mine], axis=axis)
        )

    both = jnp.concatenate([queries, grad_out], axis=1).reshape(PEERS, part, 2 * width)
    half = lax.div(z, apart)
    pieces = [jnp.where(half == 0, both[0], both[1]), peer(jnp.where(half == 0, both[1], both[0]))]

    docs = jnp.broadcast_to(low(block_docs)[:, None], (DOC_ROWS, HEAD))
    k_rows, v_rows = jnp.concatenate([keys, docs]), jnp.concatenate([values, docs])
    kept = jnp.where(core == 0, k_rows, v_rows)
    given = jnp.where(core == 0, v_rows, k_rows)
    near = in_order(core, kept, other_core(given), 0)
    far = in_order(core, other_y(kept), diagonal(given), 0)
    unit = in_order(y, near, far, 1)
    unit = jnp.concatenate(
        [unit[:, :, :BLOCK].reshape(4 * BLOCK, HEAD), unit[:, :, BLOCK : BLOCK + 4].reshape(DOC_ROWS, HEAD)]
    )
    line = jnp.stack([unit] + [along_first(unit, by) for by in range(1, lines)])
    line, *pieces = lax.optimization_barrier((line, *pieces))
    q = jnp.stack([piece[:, :width] for piece in pieces])
    g = jnp.stack([piece[:, width:] for piece in pieces])
    mine = [line] + [along_second(line, by) for by in range(1, lines)]
    theirs = [other_core(piece) for piece in mine]

    place = jnp.stack([z, x, y, core]).astype(jnp.int32)
    dq, *sums = grads_call((nz, nx), place, q, g, mine, theirs)
    keep, send = sums[:lines], sums[lines:]

    totals = [None] * lines
    for by in [*range(1, lines), 0]:
        totals[by] = low(added([keep[by], other_core(send[by])]))
    arrived = [along_second(totals[by], by) for by in range(1, lines)]
    dq, totals[0] = lax.optimization_barrier((dq, totals[0]))
    returned = peer(dq[1])
    arrived, returned = lax.optimization_barrier((arrived, returned))
    total = low(added([totals[0]] + arrived))
    total = low(added([total[0]] + [along_first(total[by], by) for by in range(1, lines)]))
    total = total.reshape(2, 2, BLOCK, HEAD)

    def block_at(other_of_core, other_of_y):
        c = 1 - core if other_of_core else core
        row = 1 - y if other_of_y else y
        return lax.dynamic_slice(total, (c, row, 0, 0), (1, 1, BLOCK, HEAD))[0, 0]

    first = added([block_at(False, False), other_y(block_at(False, True))])
    second = added([other_core(block_at(True, False)), diagonal(block_at(True, True))])
    grad_keys = low(SCALE * jnp.where(core == 0, first, second))
    grad_values = low(jnp.where(core == 0, second, first))
    grad_queries = in_order(half, dq[0], returned, 0).reshape(rows, width)
    return grad_queries, grad_keys, grad_values


def solution(mesh):
    wide = P(CONTEXT, "head")
    return jax.shard_map(
        per_device,
        mesh=mesh,
        in_specs=(wide, wide, wide, wide, P(CONTEXT)),
        out_specs=(wide, wide, wide),
        check_vma=False,
    )
```

```python
import math

import jax
import jax.numpy as jnp
from jax import lax
from jax.experimental import pallas as pl
from jax.experimental.pallas import tpu as pltpu
from jax.sharding import PartitionSpec as P

NEG = -1e30
HEAD = 128
BLOCK = 128
DOC_ROWS = 16
CHUNK_BLOCKS = 5
CHUNK = CHUNK_BLOCKS * BLOCK
LONGEST = 20
TILES = 4
PEERS = 2
SCALE = float(HEAD) ** (-0.5)
TO_EXP2 = SCALE * math.log2(math.e)
CONTEXT = ("inner", "outer")


def dot(lhs, rhs, over):
    return lax.dot_general(lhs, rhs, ((over[:1], over[1:]), ((), ())), preferred_element_type=jnp.float32)


class Setting:
    def __init__(self, sizes, refs, kv_all, docs_all, tile_docs, cols, rows=None):
        self.nz, self.nx = nz, nx = sizes
        lines = nz
        place_ref, doc_ref, own_ref, peer_ref, far_ref = refs[:5]
        pieces = (refs[5 : 5 + lines], refs[5 + lines : 5 + 2 * lines])
        self.z, self.x, self.y, self.core = (place_ref[i] for i in range(4))
        self.part = own_ref.shape[0]
        self.width = own_ref.shape[1] // 2
        self.heads = self.width // HEAD
        self.rows = self.heads * self.part
        self.kv_all, self.docs_all, self.tile_docs = kv_all, docs_all, tile_docs
        self.blocks = kv_all.shape[1]
        self.steps = steps = range(lines)
        z_at = [lax.rem(self.z + by, nz) * (2 * nx) for by in steps]
        x_at = [lax.rem(self.x + by, nx) for by in steps]

        def places(which):
            return [
                [
                    jnp.where(which == 0, x_at[i], z_at[i]) + jnp.where(which == 0, z_at[j], x_at[j])
                    for j in steps
                ]
                for i in steps
            ]

        self.spots = (places(self.core), places(1 - self.core))
        for which, arrived, spot in ((self.core, pieces[0], self.spots[0]), (1 - self.core, pieces[1], self.spots[1])):
            for i in steps:
                for j in steps:
                    for c in range(2):
                        kv_all[which, spot[-i][-j] + nx * c] = arrived[i][j, c * BLOCK : (c + 1) * BLOCK]
        for i in steps:
            for j in steps:
                docs_all[i * lines + j] = pieces[0][i][j, 2 * BLOCK :].astype(jnp.float32)
        part, width = self.part, self.width
        tile_docs[0] = doc_ref[...].astype(jnp.float32)
        tile_docs[1] = peer_ref[part:, :HEAD].astype(jnp.float32)
        tile_docs[2] = far_ref[2 * part :, :HEAD].astype(jnp.float32)
        tile_docs[3] = far_ref[2 * part :, width : width + HEAD].astype(jnp.float32)
        sources = ((own_ref, 0), (peer_ref, 0), (far_ref, 0), (far_ref, part))
        for t, (source, begin) in enumerate(sources):
            for side in range(2):
                whole = jnp.concatenate(
                    [
                        source[begin : begin + part, side * width + h * HEAD : side * width + (h + 1) * HEAD]
                        for h in range(self.heads)
                    ]
                )
                if rows is not None:
                    rows[side, t] = whole
                cols[side, t] = whole.T
        apart = nz // PEERS
        self.apart = apart
        self.row_token = lax.div(self.z, apart) * part + lax.rem(
            lax.broadcasted_iota(jnp.int32, (CHUNK, self.rows), 1), part
        )
        key_row = lax.broadcasted_iota(jnp.int32, (CHUNK, self.rows), 0)
        self.key_row = key_row
        self.key_token = key_row + lax.div(key_row, BLOCK) * BLOCK

    def tile(self, t):
        dz = lax.rem(t, 2) * self.apart
        row = jnp.where(t < 2, self.y, 1 - self.y)
        block = (lax.rem(self.z + self.nz - dz, self.nz) * 2 + self.core) * (2 * self.nx) + self.x * 2 + row
        doc = self.tile_docs[t, :1, :]
        before = jnp.sum(jnp.where(self.docs_all[...] < doc, 0.125, 0.0), axis=(0, 1))
        first = jnp.max(before).astype(jnp.int32)
        held = lax.div(block - self.y + 2, 2) - first
        chunks = lax.div(held + CHUNK_BLOCKS - 1, CHUNK_BLOCKS)
        last = jnp.maximum(chunks - 1, 0)

        def keys_at(n):
            return jnp.minimum(first + n * CHUNK_BLOCKS, self.blocks - CHUNK_BLOCKS)

        begin = keys_at(last)
        skipped = (first + last * CHUNK_BLOCKS - begin) * BLOCK
        reach = (block - 2 * begin - self.y) * BLOCK
        mask = (self.key_token <= self.row_token + reach) & (self.key_row >= skipped)
        return chunks, last, keys_at, mask

    def key_rows(self, which, at):
        return self.kv_all[which, pl.ds(at, CHUNK_BLOCKS)].reshape(CHUNK, HEAD)


def statistics(sizes, *refs):
    count = 5 + 2 * sizes[0]
    stats_ref = refs[count]
    kv_all, docs_all, tile_docs, cols, scores = refs[count + 1 :]
    s = Setting(sizes, refs, kv_all, docs_all, tile_docs, cols)
    rows = s.rows

    def fold(value, combine):
        return combine(value.reshape(CHUNK // 8, 8, rows), axis=0)

    def slot(n):
        return pl.ds(pl.multiple_of(n * CHUNK, CHUNK), CHUNK)

    def tile(t, carry):
        chunks, last, keys_at, mask = s.tile(t)

        def score(n, top, masked):
            value = dot(s.key_rows(0, keys_at(n)), cols[0, t], (1, 0))
            if masked:
                value = jnp.where(mask, value, NEG)
            scores[slot(n), :] = value
            return jnp.maximum(top, fold(value, jnp.max))

        top = jnp.full((8, rows), NEG, jnp.float32)
        top = lax.fori_loop(0, last, lambda n, top: score(n, top, False), top)
        top = lax.fori_loop(last, chunks, lambda n, top: score(n, top, True), top)
        top = jnp.max(top, axis=0, keepdims=True) * TO_EXP2

        def sums(n, state):
            norm, weighted = state
            e = jnp.exp2(scores[slot(n), :] * TO_EXP2 - top)
            dp = dot(s.key_rows(1, keys_at(n)), cols[1, t], (1, 0))
            return norm + fold(e, jnp.sum), weighted + fold(e * dp, jnp.sum)

        zeros = jnp.zeros((8, rows), jnp.float32)
        norm, weighted = lax.fori_loop(0, chunks, sums, (zeros, zeros))
        stats_ref[t, 0:1, :] = top
        stats_ref[t, 1:2, :] = jnp.sum(norm, axis=0, keepdims=True)
        stats_ref[t, 2:3, :] = jnp.sum(weighted, axis=0, keepdims=True)
        return carry

    stats_ref[...] = jnp.zeros_like(stats_ref)
    lax.fori_loop(0, TILES, tile, 0)


def gradients(sizes, *refs):
    lines = sizes[0]
    count = 5 + 2 * lines
    here_ref, there_ref, dq_ref = refs[count : count + 3]
    outs = refs[count + 3 : count + 3 + 2 * lines]
    kv_all, docs_all, tile_docs, cols, tile_rows, totals = refs[count + 3 + 2 * lines :]
    totals[...] = jnp.zeros_like(totals)
    s = Setting(sizes, refs, kv_all, docs_all, tile_docs, cols, tile_rows)
    part, rows = s.part, s.rows

    def tile(t, carry):
        chunks, last, keys_at, mask = s.tile(t)
        other = lax.rem(t + 2, TILES)
        top_here, top_there = here_ref[t, 0:1, :], there_ref[other, 0:1, :]
        top = jnp.maximum(top_here, top_there)
        weight_here, weight_there = jnp.exp2(top_here - top), jnp.exp2(top_there - top)
        norm = here_ref[t, 1:2, :] * weight_here + there_ref[other, 1:2, :] * weight_there
        weighted = here_ref[t, 2:3, :] * weight_here + there_ref[other, 2:3, :] * weight_there
        inverse = 1.0 / norm
        delta = weighted * inverse

        def work(n, dq, masked):
            at = keys_at(n)
            keys = pl.ds(pl.multiple_of(at * BLOCK, BLOCK), CHUNK)
            value = dot(s.key_rows(0, at), cols[0, t], (1, 0))
            if masked:
                value = jnp.where(mask, value, NEG)
            p = jnp.exp2(value * TO_EXP2 - top) * inverse
            ds = p * (dot(s.key_rows(1, at), cols[1, t], (1, 0)) - delta)
            p_low = p.astype(jnp.bfloat16)
            ds_low = ds.astype(jnp.bfloat16)
            totals[0, keys, :] += dot(ds_low, tile_rows[0, t], (1, 0))
            totals[1, keys, :] += dot(p_low, tile_rows[1, t], (1, 0))
            return dq + dot(s.key_rows(0, at), ds_low, (0, 0))

        dq = jnp.zeros((HEAD, rows), jnp.float32)
        dq = lax.fori_loop(0, last, lambda n, dq: work(n, dq, False), dq)
        dq = lax.fori_loop(last, chunks, lambda n, dq: work(n, dq, True), dq)
        dq = (dq * SCALE).T
        for h in range(s.heads):
            dq_ref[t, :, h * HEAD : (h + 1) * HEAD] = dq[h * part : (h + 1) * part, :]
        return carry

    lax.fori_loop(0, TILES, tile, 0)
    keep, send = outs[:lines], outs[lines:]
    for which, out, spot in ((s.core, keep, s.spots[0]), (1 - s.core, send, s.spots[1])):
        for i in s.steps:
            for j in s.steps:
                for c in range(2):
                    begin = pl.multiple_of((spot[i][j] + s.nx * c) * BLOCK, BLOCK)
                    out[i][j, c] = totals[which, pl.ds(begin, BLOCK), :].astype(jnp.bfloat16)


def kernel_call(kernel, sizes, operands, outs, extra, pairs):
    nz, nx = sizes
    part, width = operands[2].shape
    rows = part * width // (2 * HEAD)
    blocks = 2 * nz * nx
    whole = pl.BlockSpec(memory_space=pltpu.VMEM)
    return pl.pallas_call(
        lambda *refs: kernel(sizes, *refs),
        name=kernel.__name__,
        out_shape=outs,
        in_specs=[pl.BlockSpec(memory_space=pltpu.SMEM)] + [whole] * (len(operands) - 1),
        out_specs=(whole,) * len(outs),
        scratch_shapes=[
            pltpu.VMEM((2, blocks, BLOCK, HEAD), jnp.bfloat16),
            pltpu.VMEM((nz * nx, DOC_ROWS, HEAD), jnp.float32),
            pltpu.VMEM((TILES, DOC_ROWS, HEAD), jnp.float32),
            pltpu.VMEM((2, TILES, HEAD, rows), jnp.bfloat16),
        ]
        + extra(rows, blocks),
        compiler_params=pltpu.CompilerParams(vmem_limit_bytes=36 * 1024 * 1024),
        cost_estimate=pl.CostEstimate(
            flops=pairs * 2 * 24 * 1024 * 128 * 128, bytes_accessed=8 * 1024 * 1024, transcendentals=0
        ),
    )(*operands)


def statistics_call(sizes, *operands):
    rows = operands[2].shape[0] * operands[2].shape[1] // (2 * HEAD)
    slots = -(-LONGEST // CHUNK_BLOCKS) * CHUNK
    outs = (jax.ShapeDtypeStruct((TILES, 8, rows), jnp.float32),)
    return kernel_call(
        statistics, sizes, operands, outs, lambda rows, blocks: [pltpu.VMEM((slots, rows), jnp.float32)], 2
    )[0]


def gradients_call(sizes, *operands):
    nz, nx = sizes
    part, width = operands[2].shape
    outs = (jax.ShapeDtypeStruct((TILES, part, width // 2), jnp.float32),)
    outs += (jax.ShapeDtypeStruct((nx, 2, BLOCK, HEAD), jnp.bfloat16),) * (2 * nz)
    return kernel_call(
        gradients,
        sizes,
        operands,
        outs,
        lambda rows, blocks: [
            pltpu.VMEM((2, TILES, rows, HEAD), jnp.bfloat16),
            pltpu.VMEM((2, blocks * BLOCK, HEAD), jnp.float32),
        ],
        5,
    )


def low(value):
    return value.astype(jnp.bfloat16)


def added(terms):
    total = terms[0].astype(jnp.float32)
    for term in terms[1:]:
        total = total + term.astype(jnp.float32)
    return total


def per_device(queries, keys, values, grad_out, block_docs):
    rows, width = queries.shape
    inner_size, outer_size = lax.axis_size("inner"), lax.axis_size("outer")
    nz, nx = inner_size // 2, outer_size // 2
    inner, outer = lax.axis_index("inner"), lax.axis_index("outer")
    z, core = lax.div(inner, 2), lax.rem(inner, 2)
    x, y = lax.div(outer, 2), lax.rem(outer, 2)
    part = rows // PEERS
    apart = nz // PEERS
    lines = nz

    def moved(value, step):
        hops = []
        for source in range(inner_size * outer_size):
            i, o = divmod(source, outer_size)
            dz, dx, dy, dc = step(i % 2)
            to_inner = (i // 2 + dz) % nz * 2 + (i % 2 + dc) % 2
            to_outer = (o // 2 + dx) % nx * 2 + (o % 2 + dy) % 2
            hops.append((source, to_inner * outer_size + to_outer))
        return lax.ppermute(value, CONTEXT, hops)

    def other_core(value):
        return moved(value, lambda c: (0, 0, 0, 1))

    def other_y(value):
        return moved(value, lambda c: (0, 0, 1, 0))

    def peer(value):
        return moved(value, lambda c: (apart, 0, 0, 0))

    def along_first(value, by):
        return moved(value, lambda c: (0, by, 0, 0) if c else (by, 0, 0, 0))

    def along_second(value, by):
        return moved(value, lambda c: (by, 0, 0, 0) if c else (0, by, 0, 0))

    def in_order(index, mine, theirs, axis):
        return jnp.where(
            index == 0, jnp.stack([mine, theirs], axis=axis), jnp.stack([theirs, mine], axis=axis)
        )

    doc = jnp.broadcast_to(low(block_docs)[:, None], (DOC_ROWS, HEAD))
    both = jnp.concatenate([queries, grad_out], axis=1).reshape(PEERS, part, 2 * width)
    half = lax.div(z, apart)
    own = jnp.where(half == 0, both[0], both[1])
    lent = jnp.where(half == 0, both[1], both[0])
    wide_doc = jnp.broadcast_to(low(block_docs)[:, None], (DOC_ROWS, 2 * width))
    borrowed = peer(jnp.concatenate([lent, wide_doc]))
    docs_of_both = jnp.concatenate([wide_doc[:, :width], borrowed[part:, width:]], axis=1)
    far = other_y(jnp.concatenate([own, borrowed[:part], docs_of_both]))

    given = other_core(jnp.where(core == 0, values, keys))
    kept = jnp.where(core == 0, keys, values)
    unit_docs = other_core(doc)
    rows_in_order = in_order(core, kept, given, 0).reshape(2 * BLOCK, HEAD)
    docs_in_order = in_order(core, doc[:8], unit_docs[:8], 0).reshape(DOC_ROWS, HEAD)
    unit = jnp.concatenate([rows_in_order, docs_in_order])
    line = jnp.stack([unit] + [along_first(unit, by) for by in range(1, lines)])
    mine = [line] + [along_second(line, by) for by in range(1, lines)]
    theirs = [other_core(piece) for piece in mine]

    place = jnp.stack([z, x, y, core]).astype(jnp.int32)
    sizes = (nz, nx)
    operands = (place, doc, own, borrowed, far, *mine, *theirs)
    here = statistics_call(sizes, *operands)
    dq, *sums = gradients_call(sizes, *operands, here, other_y(here))
    keep, send = sums[:lines], sums[lines:]

    totals = [None] * lines
    for by in [*range(1, lines), 0]:
        totals[by] = low(added([keep[by], other_core(send[by])]))
    arrived = [along_second(totals[by], by) for by in range(1, lines)]
    dq, totals[0] = lax.optimization_barrier((dq, totals[0]))
    rest = other_y(low(dq[2:]))
    arrived, rest = lax.optimization_barrier((arrived, rest))
    dq = low(dq[:2] + rest.astype(jnp.float32))
    returned = peer(dq[1])
    total = low(added([totals[0]] + arrived))
    total = added([total[0]] + [along_first(total[by], by) for by in range(1, lines)])
    total = low(jnp.where(core == 0, SCALE * total, total))
    ours = jnp.where(core == 0, total[0], total[1])
    theirs = other_core(jnp.where(core == 0, total[1], total[0]))
    grad_keys = jnp.where(core == 0, ours, theirs)
    grad_values = jnp.where(core == 0, theirs, ours)
    grad_queries = in_order(half, dq[0], returned, 0).reshape(rows, width)
    return grad_queries, grad_keys, grad_values


def solution(mesh):
    wide = P(CONTEXT, "head")
    return jax.shard_map(
        per_device,
        mesh=mesh,
        in_specs=(wide, wide, wide, wide, P(CONTEXT)),
        out_specs=(wide, wide, wide),
        check_vma=False,
    )
```

```python
import math

import jax
import jax.numpy as jnp
from jax import lax
from jax.experimental import pallas as pl
from jax.experimental.pallas import tpu as pltpu
from jax.sharding import PartitionSpec as P

NEG = -1e30
HEAD = 128
BLOCK = 128
DOC_ROWS = 16
CHUNK_BLOCKS = 5
CHUNK = CHUNK_BLOCKS * BLOCK
TILES = 4
VMEM_MIB = 36
PEERS = 2
SCALE = float(HEAD) ** (-0.5)
TO_EXP2 = SCALE * math.log2(math.e)
CONTEXT = ("inner", "outer")


def dot(lhs, rhs, over):
    return lax.dot_general(lhs, rhs, ((over[:1], over[1:]), ((), ())), preferred_element_type=jnp.float32)


class Setting:
    def __init__(self, sizes, place_ref, kv_all, docs_all, tile_docs, rows, part):
        self.nz, self.nx = nz, nx = sizes
        lines = nz
        self.z, self.x, self.y, self.core = (place_ref[i] for i in range(4))
        self.part, self.rows = part, rows
        self.heads = rows // part
        self.kv_all, self.docs_all, self.tile_docs = kv_all, docs_all, tile_docs
        self.blocks = kv_all.shape[1]
        self.steps = steps = range(lines)
        z_at = [lax.rem(self.z + by, nz) * (2 * nx) for by in steps]
        x_at = [lax.rem(self.x + by, nx) for by in steps]

        def places(which):
            return [
                [
                    jnp.where(which == 0, x_at[i], z_at[i]) + jnp.where(which == 0, z_at[j], x_at[j])
                    for j in steps
                ]
                for i in steps
            ]

        self.spots = (places(self.core), places(1 - self.core))
        apart = nz // PEERS
        self.apart = apart
        self.row_token = lax.div(self.z, apart) * part + lax.rem(
            lax.broadcasted_iota(jnp.int32, (CHUNK, self.rows), 1), part
        )
        key_row = lax.broadcasted_iota(jnp.int32, (CHUNK, self.rows), 0)
        self.key_row = key_row
        self.key_token = key_row + lax.div(key_row, BLOCK) * BLOCK

    def tile(self, t):
        dz = lax.rem(t, 2) * self.apart
        row = jnp.where(t < 2, self.y, 1 - self.y)
        block = (lax.rem(self.z + self.nz - dz, self.nz) * 2 + self.core) * (2 * self.nx) + self.x * 2 + row
        doc = self.tile_docs[t, :1, :]
        before = jnp.sum(jnp.where(self.docs_all[...] < doc, 0.125, 0.0), axis=(0, 1))
        first = jnp.max(before).astype(jnp.int32)
        held = lax.div(block - self.y + 2, 2) - first
        chunks = lax.div(held + CHUNK_BLOCKS - 1, CHUNK_BLOCKS)
        last = jnp.maximum(chunks - 1, 0)

        def keys_at(n):
            return jnp.minimum(first + n * CHUNK_BLOCKS, self.blocks - CHUNK_BLOCKS)

        begin = keys_at(last)
        skipped = (first + last * CHUNK_BLOCKS - begin) * BLOCK
        reach = (block - 2 * begin - self.y) * BLOCK
        mask = (self.key_token <= self.row_token + reach) & (self.key_row >= skipped)
        return chunks, last, keys_at, mask

    def key_rows(self, which, at):
        return self.kv_all[which, pl.ds(at, CHUNK_BLOCKS)].reshape(CHUNK, HEAD)


def place_all(s, refs, pieces, kv_all, docs_all, tile_docs, cols, rows):
    doc_ref, own_ref, peer_ref, far_ref = refs
    lines, nx, steps = s.nz, s.nx, s.steps
    for which, arrived, spot in ((s.core, pieces[0], s.spots[0]), (1 - s.core, pieces[1], s.spots[1])):
        for i in steps:
            for j in steps:
                for c in range(2):
                    kv_all[which, spot[-i][-j] + nx * c] = arrived[i][j, c * BLOCK : (c + 1) * BLOCK]
    for i in steps:
        for j in steps:
            docs_all[i * lines + j] = pieces[0][i][j, 2 * BLOCK :].astype(jnp.float32)
    part, width = s.part, s.heads * HEAD
    tile_docs[0] = doc_ref[...].astype(jnp.float32)
    tile_docs[1] = peer_ref[part:, :HEAD].astype(jnp.float32)
    tile_docs[2] = far_ref[2 * part :, :HEAD].astype(jnp.float32)
    tile_docs[3] = far_ref[2 * part :, width : width + HEAD].astype(jnp.float32)
    sources = ((own_ref, 0), (peer_ref, 0), (far_ref, 0), (far_ref, part))
    for t, (source, begin) in enumerate(sources):
        for side in range(2):
            whole = jnp.concatenate(
                [
                    source[begin : begin + part, side * width + h * HEAD : side * width + (h + 1) * HEAD]
                    for h in range(s.heads)
                ]
            )
            rows[side, t] = whole
            cols[side, t] = whole.T


def statistics(sizes, *refs):
    lines = sizes[0]
    count = 5 + 2 * lines
    stats_ref, kv_all, docs_all, tile_docs, cols, tile_rows = refs[count : count + 6]
    part = refs[2].shape[0]
    s = Setting(sizes, refs[0], kv_all, docs_all, tile_docs, cols.shape[-1], part)
    pieces = (refs[5 : 5 + lines], refs[5 + lines : count])
    place_all(s, refs[1:5], pieces, kv_all, docs_all, tile_docs, cols, tile_rows)
    rows = s.rows

    def fold(value, combine):
        return combine(value.reshape(CHUNK // 8, 8, rows), axis=0)

    def tile(t, carry):
        chunks, last, keys_at, mask = s.tile(t)

        def step(n, state, masked):
            top, norm, weighted = state
            at = keys_at(n)
            value = dot(s.key_rows(0, at), cols[0, t], (1, 0))
            if masked:
                value = jnp.where(mask, value, NEG)
            dp = dot(s.key_rows(1, at), cols[1, t], (1, 0))
            raised = jnp.maximum(top, jnp.max(fold(value, jnp.max), axis=0, keepdims=True) * TO_EXP2)
            e = jnp.exp2(value * TO_EXP2 - raised)
            factor = jnp.exp2(top - raised)
            return raised, norm * factor + fold(e, jnp.sum), weighted * factor + fold(e * dp, jnp.sum)

        zeros = jnp.zeros((8, rows), jnp.float32)
        state = (jnp.full((1, rows), NEG, jnp.float32), zeros, zeros)
        state = lax.fori_loop(0, last, lambda n, state: step(n, state, False), state)
        top, norm, weighted = lax.fori_loop(last, chunks, lambda n, state: step(n, state, True), state)
        stats_ref[t, 0:1, :] = top
        stats_ref[t, 1:2, :] = jnp.sum(norm, axis=0, keepdims=True)
        stats_ref[t, 2:3, :] = jnp.sum(weighted, axis=0, keepdims=True)
        return carry

    stats_ref[...] = jnp.zeros_like(stats_ref)
    lax.fori_loop(0, TILES, tile, 0)


def gradients(sizes, *refs):
    lines = sizes[0]
    place_ref, here_ref, there_ref, kv_all, docs_all, tile_docs, cols, tile_rows, dq_ref = refs[:9]
    outs = refs[9 : 9 + 2 * lines]
    totals = refs[9 + 2 * lines]
    totals[...] = jnp.zeros_like(totals)
    s = Setting(sizes, place_ref, kv_all, docs_all, tile_docs, cols.shape[-1], dq_ref.shape[1])
    part, rows = s.part, s.rows

    def tile(t, carry):
        chunks, last, keys_at, mask = s.tile(t)
        other = lax.rem(t + 2, TILES)
        top_here, top_there = here_ref[t, 0:1, :], there_ref[other, 0:1, :]
        top = jnp.maximum(top_here, top_there)
        weight_here, weight_there = jnp.exp2(top_here - top), jnp.exp2(top_there - top)
        norm = here_ref[t, 1:2, :] * weight_here + there_ref[other, 1:2, :] * weight_there
        weighted = here_ref[t, 2:3, :] * weight_here + there_ref[other, 2:3, :] * weight_there
        delta = weighted / norm
        top = top + jnp.log2(norm)

        def work(n, dq, masked):
            at = keys_at(n)
            keys = pl.ds(pl.multiple_of(at * BLOCK, BLOCK), CHUNK)
            value = dot(s.key_rows(0, at), cols[0, t], (1, 0))
            if masked:
                value = jnp.where(mask, value, NEG)
            p = jnp.exp2(value * TO_EXP2 - top)
            ds = p * (dot(s.key_rows(1, at), cols[1, t], (1, 0)) - delta)
            p_low = p.astype(jnp.bfloat16)
            ds_low = ds.astype(jnp.bfloat16)
            totals[0, keys, :] += dot(ds_low, tile_rows[0, t], (1, 0))
            totals[1, keys, :] += dot(p_low, tile_rows[1, t], (1, 0))
            return dq + dot(s.key_rows(0, at), ds_low, (0, 0))

        dq = jnp.zeros((HEAD, rows), jnp.float32)
        dq = lax.fori_loop(0, last, lambda n, dq: work(n, dq, False), dq)
        dq = lax.fori_loop(last, chunks, lambda n, dq: work(n, dq, True), dq)
        dq = (dq * SCALE).T
        for h in range(s.heads):
            dq_ref[t, :, h * HEAD : (h + 1) * HEAD] = dq[h * part : (h + 1) * part, :]
        return carry

    lax.fori_loop(0, TILES, tile, 0)
    keep, send = outs[:lines], outs[lines:]
    for which, out, spot in ((s.core, keep, s.spots[0]), (1 - s.core, send, s.spots[1])):
        for i in s.steps:
            for j in s.steps:
                for c in range(2):
                    begin = pl.multiple_of((spot[i][j] + s.nx * c) * BLOCK, BLOCK)
                    out[i][j, c] = totals[which, pl.ds(begin, BLOCK), :].astype(jnp.bfloat16)


def kernel_call(kernel, sizes, operands, outs, scratch, products):
    whole = pl.BlockSpec(memory_space=pltpu.VMEM)
    return pl.pallas_call(
        lambda *refs: kernel(sizes, *refs),
        name=kernel.__name__,
        out_shape=outs,
        in_specs=[pl.BlockSpec(memory_space=pltpu.SMEM)] + [whole] * (len(operands) - 1),
        out_specs=(whole,) * len(outs),
        scratch_shapes=scratch,
        compiler_params=pltpu.CompilerParams(vmem_limit_bytes=VMEM_MIB * 1024 * 1024),
        cost_estimate=pl.CostEstimate(
            flops=products * 2 * 24 * 1024 * 128 * 128, bytes_accessed=8 * 1024 * 1024, transcendentals=0
        ),
    )(*operands)


def statistics_call(sizes, *operands):
    nz, nx = sizes
    part, width = operands[2].shape
    rows = part * width // (2 * HEAD)
    outs = (
        jax.ShapeDtypeStruct((TILES, 8, rows), jnp.float32),
        jax.ShapeDtypeStruct((2, 2 * nz * nx, BLOCK, HEAD), jnp.bfloat16),
        jax.ShapeDtypeStruct((nz * nx, DOC_ROWS, HEAD), jnp.float32),
        jax.ShapeDtypeStruct((TILES, DOC_ROWS, HEAD), jnp.float32),
        jax.ShapeDtypeStruct((2, TILES, HEAD, rows), jnp.bfloat16),
        jax.ShapeDtypeStruct((2, TILES, rows, HEAD), jnp.bfloat16),
    )
    return kernel_call(statistics, sizes, operands, outs, [], 2)


def gradients_call(sizes, part, place, here, there, kv, docs, tile_docs, cols, rows):
    nz, nx = sizes
    width = rows.shape[2] * HEAD // part
    outs = (jax.ShapeDtypeStruct((TILES, part, width), jnp.float32),)
    outs += (jax.ShapeDtypeStruct((nx, 2, BLOCK, HEAD), jnp.bfloat16),) * (2 * nz)
    scratch = [pltpu.VMEM((2, kv.shape[1] * BLOCK, HEAD), jnp.float32)]
    operands = (place, here, there, kv, docs, tile_docs, cols, rows)
    return kernel_call(gradients, sizes, operands, outs, scratch, 5)


def low(value):
    return value.astype(jnp.bfloat16)


def added(terms):
    total = terms[0].astype(jnp.float32)
    for term in terms[1:]:
        total = total + term.astype(jnp.float32)
    return total


def per_device(queries, keys, values, grad_out, block_docs):
    rows, width = queries.shape
    inner_size, outer_size = lax.axis_size("inner"), lax.axis_size("outer")
    nz, nx = inner_size // 2, outer_size // 2
    inner, outer = lax.axis_index("inner"), lax.axis_index("outer")
    z, core = lax.div(inner, 2), lax.rem(inner, 2)
    x, y = lax.div(outer, 2), lax.rem(outer, 2)
    part = rows // PEERS
    apart = nz // PEERS
    lines = nz

    def moved(value, step):
        hops = []
        for source in range(inner_size * outer_size):
            i, o = divmod(source, outer_size)
            dz, dx, dy, dc = step(i % 2)
            to_inner = (i // 2 + dz) % nz * 2 + (i % 2 + dc) % 2
            to_outer = (o // 2 + dx) % nx * 2 + (o % 2 + dy) % 2
            hops.append((source, to_inner * outer_size + to_outer))
        return lax.ppermute(value, CONTEXT, hops)

    def other_core(value):
        return moved(value, lambda c: (0, 0, 0, 1))

    def other_y(value):
        return moved(value, lambda c: (0, 0, 1, 0))

    def peer(value):
        return moved(value, lambda c: (apart, 0, 0, 0))

    def along_first(value, by):
        return moved(value, lambda c: (0, by, 0, 0) if c else (by, 0, 0, 0))

    def along_second(value, by):
        return moved(value, lambda c: (by, 0, 0, 0) if c else (0, by, 0, 0))

    def in_order(index, mine, theirs, axis):
        return jnp.where(
            index == 0, jnp.stack([mine, theirs], axis=axis), jnp.stack([theirs, mine], axis=axis)
        )

    doc = jnp.broadcast_to(low(block_docs)[:, None], (DOC_ROWS, HEAD))
    both = jnp.concatenate([queries, grad_out], axis=1).reshape(PEERS, part, 2 * width)
    half = lax.div(z, apart)
    own = jnp.where(half == 0, both[0], both[1])
    lent = jnp.where(half == 0, both[1], both[0])
    wide_doc = jnp.broadcast_to(low(block_docs)[:, None], (DOC_ROWS, 2 * width))
    borrowed = peer(jnp.concatenate([lent, wide_doc]))
    docs_of_both = jnp.concatenate([wide_doc[:, :width], borrowed[part:, width:]], axis=1)
    far = other_y(jnp.concatenate([own, borrowed[:part], docs_of_both]))

    given = other_core(jnp.where(core == 0, values, keys))
    kept = jnp.where(core == 0, keys, values)
    unit_docs = other_core(doc)
    rows_in_order = in_order(core, kept, given, 0).reshape(2 * BLOCK, HEAD)
    docs_in_order = in_order(core, doc[:8], unit_docs[:8], 0).reshape(DOC_ROWS, HEAD)
    unit = jnp.concatenate([rows_in_order, docs_in_order])
    line = jnp.stack([unit] + [along_first(unit, by) for by in range(1, lines)])
    mine = [line] + [along_second(line, by) for by in range(1, lines)]
    theirs = [other_core(piece) for piece in mine]

    place = jnp.stack([z, x, y, core]).astype(jnp.int32)
    sizes = (nz, nx)
    operands = (place, doc, own, borrowed, far, *mine, *theirs)
    here, *placed = statistics_call(sizes, *operands)
    dq, *sums = gradients_call(sizes, part, place, here, other_y(here), *placed)
    keep, send = sums[:lines], sums[lines:]

    totals = [None] * lines
    for by in [*range(1, lines), 0]:
        totals[by] = low(added([keep[by], other_core(send[by])]))
    arrived = [along_second(totals[by], by) for by in range(1, lines)]
    dq, totals[0] = lax.optimization_barrier((dq, totals[0]))
    rest = other_y(low(dq[2:]))
    arrived, rest = lax.optimization_barrier((arrived, rest))
    dq = low(dq[:2] + rest.astype(jnp.float32))
    returned = peer(dq[1])
    total = low(added([totals[0]] + arrived))
    short = [along_first(total[by], by) for by in range(1, lines)]
    short, returned = lax.optimization_barrier((short, returned))
    total = added([total[0]] + short)
    total = low(jnp.where(core == 0, SCALE * total, total))
    ours = jnp.where(core == 0, total[0], total[1])
    theirs = other_core(jnp.where(core == 0, total[1], total[0]))
    grad_keys = jnp.where(core == 0, ours, theirs)
    grad_values = jnp.where(core == 0, theirs, ours)
    grad_queries = in_order(half, dq[0], returned, 0).reshape(rows, width)
    return grad_queries, grad_keys, grad_values


def solution(mesh):
    wide = P(CONTEXT, "head")
    return jax.shard_map(
        per_device,
        mesh=mesh,
        in_specs=(wide, wide, wide, wide, P(CONTEXT)),
        out_specs=(wide, wide, wide),
        check_vma=False,
    )
```

```python
import math

import jax
import jax.numpy as jnp
from jax import lax
from jax.experimental import pallas as pl
from jax.experimental.pallas import tpu as pltpu
from jax.sharding import PartitionSpec as P

NEG = -1e30
HEAD = 128
BLOCK = 128
DOC_ROWS = 16
CHUNK_BLOCKS = 5
CHUNK = CHUNK_BLOCKS * BLOCK
TILES = 2
VMEM_MIB = 36
PEERS = 2
SCALE = float(HEAD) ** (-0.5)
TO_EXP2 = SCALE * math.log2(math.e)
CONTEXT = ("inner", "outer")


def dot(lhs, rhs, over):
    return lax.dot_general(lhs, rhs, ((over[:1], over[1:]), ((), ())), preferred_element_type=jnp.float32)


class Setting:
    def __init__(self, sizes, place_ref, kv_all, docs_all, tile_docs, rows, part, far):
        self.nz, self.nx = nz, nx = sizes
        lines = nz
        self.z, self.x, self.y, self.core = (place_ref[i] for i in range(4))
        self.part, self.rows = part, rows
        self.heads = rows // part
        self.row = 1 - self.y if far else self.y
        self.kv_all, self.docs_all, self.tile_docs = kv_all, docs_all, tile_docs
        self.blocks = kv_all.shape[1]
        self.steps = steps = range(lines)
        z_at = [lax.rem(self.z + by, nz) * (2 * nx) for by in steps]
        x_at = [lax.rem(self.x + by, nx) for by in steps]

        def places(which):
            return [
                [
                    jnp.where(which == 0, x_at[i], z_at[i]) + jnp.where(which == 0, z_at[j], x_at[j])
                    for j in steps
                ]
                for i in steps
            ]

        self.spots = (places(self.core), places(1 - self.core))
        apart = nz // PEERS
        self.apart = apart
        self.row_token = lax.div(self.z, apart) * part + lax.rem(
            lax.broadcasted_iota(jnp.int32, (CHUNK, self.rows), 1), part
        )
        key_row = lax.broadcasted_iota(jnp.int32, (CHUNK, self.rows), 0)
        self.key_row = key_row
        self.key_token = key_row + lax.div(key_row, BLOCK) * BLOCK

    def tile(self, t):
        dz = t * self.apart
        block = (lax.rem(self.z + self.nz - dz, self.nz) * 2 + self.core) * (2 * self.nx) + self.x * 2 + self.row
        doc = self.tile_docs[t, :1, :]
        before = jnp.sum(jnp.where(self.docs_all[...] < doc, 0.125, 0.0), axis=(0, 1))
        first = jnp.max(before).astype(jnp.int32)
        held = lax.div(block - self.y + 2, 2) - first
        chunks = lax.div(held + CHUNK_BLOCKS - 1, CHUNK_BLOCKS)
        last = jnp.maximum(chunks - 1, 0)

        def keys_at(n):
            return jnp.minimum(first + n * CHUNK_BLOCKS, self.blocks - CHUNK_BLOCKS)

        begin = keys_at(last)
        skipped = (first + last * CHUNK_BLOCKS - begin) * BLOCK
        reach = (block - 2 * begin - self.y) * BLOCK
        mask = (self.key_token <= self.row_token + reach) & (self.key_row >= skipped)
        return chunks, last, keys_at, mask

    def key_rows(self, which, at):
        return self.kv_all[which, pl.ds(at, CHUNK_BLOCKS)].reshape(CHUNK, HEAD)


def place_keys(s, pieces, kv_all, docs_all):
    for which, arrived, spot in ((s.core, pieces[0], s.spots[0]), (1 - s.core, pieces[1], s.spots[1])):
        for i in s.steps:
            for j in s.steps:
                for c in range(2):
                    kv_all[which, spot[-i][-j] + s.nx * c] = arrived[i][j, c * BLOCK : (c + 1) * BLOCK]
    for i in s.steps:
        for j in s.steps:
            docs_all[i * s.nz + j] = pieces[0][i][j, 2 * BLOCK :].astype(jnp.float32)


def place_rows(s, sources, tile_docs, cols, rows):
    part, width = s.part, s.heads * HEAD
    for t, (source, begin) in enumerate(sources):
        tile_docs[t] = source[begin : begin + DOC_ROWS, 2 * width :].astype(jnp.float32)
        for side in range(2):
            whole = jnp.concatenate(
                [
                    source[begin : begin + part, side * width + h * HEAD : side * width + (h + 1) * HEAD]
                    for h in range(s.heads)
                ]
            )
            rows[side, t] = whole
            cols[side, t] = whole.T


def near_statistics(sizes, *refs):
    lines = sizes[0]
    count = 3 + 2 * lines
    place_ref, own_ref, peer_ref = refs[:3]
    stats_ref, tile_docs, cols, tile_rows, kv_all, docs_all = refs[count:]
    s = Setting(sizes, place_ref, kv_all, docs_all, tile_docs, cols.shape[-1], own_ref.shape[0], False)
    place_keys(s, (refs[3 : 3 + lines], refs[3 + lines : count]), kv_all, docs_all)
    place_rows(s, ((own_ref, 0), (peer_ref, 0)), tile_docs, cols, tile_rows)
    statistics(s, stats_ref, cols)


def far_statistics(sizes, *refs):
    place_ref, far_ref, kv_all, docs_all, stats_ref, tile_docs, cols, tile_rows = refs
    part = far_ref.shape[0] // TILES
    s = Setting(sizes, place_ref, kv_all, docs_all, tile_docs, cols.shape[-1], part, True)
    place_rows(s, ((far_ref, 0), (far_ref, part)), tile_docs, cols, tile_rows)
    statistics(s, stats_ref, cols)


def statistics(s, stats_ref, cols):
    rows = s.rows

    def fold(value, combine):
        return combine(value.reshape(CHUNK // 8, 8, rows), axis=0)

    def tile(t, carry):
        chunks, last, keys_at, mask = s.tile(t)

        def step(n, state, masked):
            top, norm, weighted = state
            at = keys_at(n)
            value = dot(s.key_rows(0, at), cols[0, t], (1, 0))
            if masked:
                value = jnp.where(mask, value, NEG)
            dp = dot(s.key_rows(1, at), cols[1, t], (1, 0))
            raised = jnp.maximum(top, jnp.max(fold(value, jnp.max), axis=0, keepdims=True) * TO_EXP2)
            e = jnp.exp2(value * TO_EXP2 - raised)
            factor = jnp.exp2(top - raised)
            return raised, norm * factor + fold(e, jnp.sum), weighted * factor + fold(e * dp, jnp.sum)

        zeros = jnp.zeros((8, rows), jnp.float32)
        state = (jnp.full((1, rows), NEG, jnp.float32), zeros, zeros)
        state = lax.fori_loop(0, last, lambda n, state: step(n, state, False), state)
        top, norm, weighted = lax.fori_loop(last, chunks, lambda n, state: step(n, state, True), state)
        stats_ref[t, 0:1, :] = top
        stats_ref[t, 1:2, :] = jnp.sum(norm, axis=0, keepdims=True)
        stats_ref[t, 2:3, :] = jnp.sum(weighted, axis=0, keepdims=True)
        return carry

    stats_ref[...] = jnp.zeros_like(stats_ref)
    lax.fori_loop(0, TILES, tile, 0)


def far_gradients(sizes, *refs):
    place_ref, here_ref, there_ref, tile_docs, cols, tile_rows, kv_all, docs_all, dq_ref, totals = refs
    s = Setting(sizes, place_ref, kv_all, docs_all, tile_docs, cols.shape[-1], dq_ref.shape[1], True)
    totals[...] = jnp.zeros_like(totals)
    gradients(s, here_ref, there_ref, cols, tile_rows, dq_ref, totals)


def near_gradients(sizes, *refs):
    lines = sizes[0]
    place_ref, here_ref, there_ref, tile_docs, cols, tile_rows, kv_all, docs_all, so_far, dq_ref = refs[:10]
    keep, send = refs[10 : 10 + lines], refs[10 + lines : 10 + 2 * lines]
    totals = refs[10 + 2 * lines]
    s = Setting(sizes, place_ref, kv_all, docs_all, tile_docs, cols.shape[-1], dq_ref.shape[1], False)
    totals[...] = so_far[...]
    gradients(s, here_ref, there_ref, cols, tile_rows, dq_ref, totals)
    for which, out, spot in ((s.core, keep, s.spots[0]), (1 - s.core, send, s.spots[1])):
        for i in s.steps:
            for j in s.steps:
                for c in range(2):
                    begin = pl.multiple_of((spot[i][j] + s.nx * c) * BLOCK, BLOCK)
                    out[i][j, c] = totals[which, pl.ds(begin, BLOCK), :].astype(jnp.bfloat16)


def gradients(s, here_ref, there_ref, cols, tile_rows, dq_ref, totals):
    part, rows = s.part, s.rows

    def tile(t, carry):
        chunks, last, keys_at, mask = s.tile(t)
        top_here, top_there = here_ref[t, 0:1, :], there_ref[t, 0:1, :]
        top = jnp.maximum(top_here, top_there)
        weight_here, weight_there = jnp.exp2(top_here - top), jnp.exp2(top_there - top)
        norm = here_ref[t, 1:2, :] * weight_here + there_ref[t, 1:2, :] * weight_there
        weighted = here_ref[t, 2:3, :] * weight_here + there_ref[t, 2:3, :] * weight_there
        delta = weighted / norm
        top = top + jnp.log2(norm)

        def work(n, dq, masked):
            at = keys_at(n)
            keys = pl.ds(pl.multiple_of(at * BLOCK, BLOCK), CHUNK)
            value = dot(s.key_rows(0, at), cols[0, t], (1, 0))
            if masked:
                value = jnp.where(mask, value, NEG)
            p = jnp.exp2(value * TO_EXP2 - top)
            ds = p * (dot(s.key_rows(1, at), cols[1, t], (1, 0)) - delta)
            p_low = p.astype(jnp.bfloat16)
            ds_low = ds.astype(jnp.bfloat16)
            totals[0, keys, :] += dot(ds_low, tile_rows[0, t], (1, 0))
            totals[1, keys, :] += dot(p_low, tile_rows[1, t], (1, 0))
            return dq + dot(s.key_rows(0, at), ds_low, (0, 0))

        dq = jnp.zeros((HEAD, rows), jnp.float32)
        dq = lax.fori_loop(0, last, lambda n, dq: work(n, dq, False), dq)
        dq = lax.fori_loop(last, chunks, lambda n, dq: work(n, dq, True), dq)
        dq = (dq * SCALE).T
        for h in range(s.heads):
            dq_ref[t, :, h * HEAD : (h + 1) * HEAD] = dq[h * part : (h + 1) * part, :].astype(dq_ref.dtype)
        return carry

    lax.fori_loop(0, TILES, tile, 0)

def kernel_call(kernel, sizes, operands, outs, scratch, products):
    whole = pl.BlockSpec(memory_space=pltpu.VMEM)
    return pl.pallas_call(
        lambda *refs: kernel(sizes, *refs),
        name=kernel.__name__,
        out_shape=outs,
        in_specs=[pl.BlockSpec(memory_space=pltpu.SMEM)] + [whole] * (len(operands) - 1),
        out_specs=(whole,) * len(outs),
        scratch_shapes=scratch,
        compiler_params=pltpu.CompilerParams(vmem_limit_bytes=VMEM_MIB * 1024 * 1024),
        cost_estimate=pl.CostEstimate(
            flops=products * 2 * 12 * 1024 * 128 * 128, bytes_accessed=8 * 1024 * 1024, transcendentals=0
        ),
    )(*operands)


def tile_outs(rows):
    return (
        jax.ShapeDtypeStruct((TILES, 8, rows), jnp.float32),
        jax.ShapeDtypeStruct((TILES, DOC_ROWS, HEAD), jnp.float32),
        jax.ShapeDtypeStruct((2, TILES, HEAD, rows), jnp.bfloat16),
        jax.ShapeDtypeStruct((2, TILES, rows, HEAD), jnp.bfloat16),
    )


def near_statistics_call(sizes, rows, *operands):
    nz, nx = sizes
    outs = tile_outs(rows) + (
        jax.ShapeDtypeStruct((2, 2 * nz * nx, BLOCK, HEAD), jnp.bfloat16),
        jax.ShapeDtypeStruct((nz * nx, DOC_ROWS, HEAD), jnp.float32),
    )
    outs = kernel_call(near_statistics, sizes, operands, outs, [], 2)
    return outs[0], outs[1:4], outs[4:]


def far_statistics_call(sizes, rows, *operands):
    outs = kernel_call(far_statistics, sizes, operands, tile_outs(rows), [], 2)
    return outs[0], outs[1:]


def far_gradients_call(sizes, dq_shape, *operands):
    nz, nx = sizes
    totals = jax.ShapeDtypeStruct((2, 2 * nz * nx * BLOCK, HEAD), jnp.float32)
    outs = (jax.ShapeDtypeStruct(dq_shape, jnp.bfloat16), totals)
    return kernel_call(far_gradients, sizes, operands, outs, [], 5)


def near_gradients_call(sizes, dq_shape, *operands):
    nz, nx = sizes
    outs = (jax.ShapeDtypeStruct(dq_shape, jnp.float32),)
    outs += (jax.ShapeDtypeStruct((nx, 2, BLOCK, HEAD), jnp.bfloat16),) * (2 * nz)
    scratch = [pltpu.VMEM((2, 2 * nz * nx * BLOCK, HEAD), jnp.float32)]
    return kernel_call(near_gradients, sizes, operands, outs, scratch, 5)


def low(value):
    return value.astype(jnp.bfloat16)


def added(terms):
    total = terms[0].astype(jnp.float32)
    for term in terms[1:]:
        total = total + term.astype(jnp.float32)
    return total


def per_device(queries, keys, values, grad_out, block_docs):
    rows, width = queries.shape
    inner_size, outer_size = lax.axis_size("inner"), lax.axis_size("outer")
    nz, nx = inner_size // 2, outer_size // 2
    inner, outer = lax.axis_index("inner"), lax.axis_index("outer")
    z, core = lax.div(inner, 2), lax.rem(inner, 2)
    x, y = lax.div(outer, 2), lax.rem(outer, 2)
    part = rows // PEERS
    apart = nz // PEERS
    lines = nz

    def moved(value, step):
        hops = []
        for source in range(inner_size * outer_size):
            i, o = divmod(source, outer_size)
            dz, dx, dy, dc = step(i % 2)
            to_inner = (i // 2 + dz) % nz * 2 + (i % 2 + dc) % 2
            to_outer = (o // 2 + dx) % nx * 2 + (o % 2 + dy) % 2
            hops.append((source, to_inner * outer_size + to_outer))
        return lax.ppermute(value, CONTEXT, hops)

    def other_core(value):
        return moved(value, lambda c: (0, 0, 0, 1))

    def other_y(value):
        return moved(value, lambda c: (0, 0, 1, 0))

    def peer(value):
        return moved(value, lambda c: (apart, 0, 0, 0))

    def along_first(value, by):
        return moved(value, lambda c: (0, by, 0, 0) if c else (by, 0, 0, 0))

    def along_second(value, by):
        return moved(value, lambda c: (by, 0, 0, 0) if c else (0, by, 0, 0))

    def in_order(index, mine, theirs, axis):
        return jnp.where(
            index == 0, jnp.stack([mine, theirs], axis=axis), jnp.stack([theirs, mine], axis=axis)
        )

    doc = jnp.broadcast_to(low(block_docs)[:, None], (DOC_ROWS, HEAD))
    half = lax.div(z, apart)

    def rows_of(which):
        cut = [lax.dynamic_slice_in_dim(whole, which * part, part, 0) for whole in (queries, grad_out)]
        return jnp.concatenate(cut + [jnp.broadcast_to(low(block_docs)[:, None], (part, HEAD))], axis=1)

    own = rows_of(half)
    borrowed = peer(rows_of(1 - half))
    shared = jnp.concatenate([own, borrowed])

    given = other_core(jnp.where(core == 0, values, keys))
    kept = jnp.where(core == 0, keys, values)
    unit_docs = other_core(doc)
    rows_in_order = in_order(core, kept, given, 0).reshape(2 * BLOCK, HEAD)
    docs_in_order = in_order(core, doc[:8], unit_docs[:8], 0).reshape(DOC_ROWS, HEAD)
    unit = jnp.concatenate([rows_in_order, docs_in_order])
    line = jnp.stack([unit] + [along_first(unit, by) for by in range(1, lines)])
    line, shared = lax.optimization_barrier((line, shared))
    far = other_y(shared)
    mine = [line] + [along_second(line, by) for by in range(1, lines)]
    theirs = [other_core(piece) for piece in mine]

    place = jnp.stack([z, x, y, core]).astype(jnp.int32)
    sizes = (nz, nx)
    tile_rows = part * width // HEAD
    near_here, near_tiles, keys_all = near_statistics_call(sizes, tile_rows, place, own, borrowed, *mine, *theirs)
    far_there = other_y(near_here)
    far_here, far_tiles = far_statistics_call(sizes, tile_rows, place, far, *keys_all)
    near_there = other_y(far_here)
    dq_shape = (TILES, part, width)
    far_dq, so_far = far_gradients_call(sizes, dq_shape, place, far_here, far_there, *far_tiles, *keys_all)
    rest = other_y(far_dq)
    dq, *sums = near_gradients_call(
        sizes, dq_shape, place, near_here, near_there, *near_tiles, *keys_all, so_far
    )
    rest, *sums = lax.optimization_barrier((rest, *sums))
    keep, send = sums[:lines], sums[lines:]

    totals = [None] * lines
    for by in [*range(1, lines), 0]:
        totals[by] = low(added([keep[by], other_core(send[by])]))
    arrived = [along_second(totals[by], by) for by in range(1, lines)]
    dq, totals[0] = lax.optimization_barrier((dq, totals[0]))
    dq = low(dq + rest.astype(jnp.float32))
    returned = peer(dq[1])
    arrived, returned = lax.optimization_barrier((arrived, returned))
    total = low(added([totals[0]] + arrived))
    short = [along_first(total[by], by) for by in range(1, lines)]
    total = added([total[0]] + short)
    total = low(jnp.where(core == 0, SCALE * total, total))
    ours = jnp.where(core == 0, total[0], total[1])
    theirs = other_core(jnp.where(core == 0, total[1], total[0]))
    grad_keys = jnp.where(core == 0, ours, theirs)
    grad_values = jnp.where(core == 0, theirs, ours)
    grad_queries = in_order(half, dq[0], returned, 0).reshape(rows, width)
    return grad_queries, grad_keys, grad_values


def solution(mesh):
    wide = P(CONTEXT, "head")
    return jax.shard_map(
        per_device,
        mesh=mesh,
        in_specs=(wide, wide, wide, wide, P(CONTEXT)),
        out_specs=(wide, wide, wide),
        check_vma=False,
    )
```

```python
import math

import jax
import jax.numpy as jnp
from jax import lax
from jax.experimental import pallas as pl
from jax.experimental.pallas import tpu as pltpu
from jax.sharding import PartitionSpec as P

NEG = -1e30
HEAD = 128
BLOCK = 128
DOC_ROWS = 16
CHUNK_BLOCKS = 5
CHUNK = CHUNK_BLOCKS * BLOCK
TILES = 2
VMEM_MIB = 36
PEERS = 2
SCALE = float(HEAD) ** (-0.5)
TO_EXP2 = SCALE * math.log2(math.e)
CONTEXT = ("inner", "outer")


def dot(lhs, rhs, over):
    return lax.dot_general(lhs, rhs, ((over[:1], over[1:]), ((), ())), preferred_element_type=jnp.float32)


class Setting:
    def __init__(self, sizes, place_ref, kv_all, docs_all, tile_docs, rows, part, far):
        self.nz, self.nx = nz, nx = sizes
        lines = nz
        self.z, self.x, self.y, self.core = (place_ref[i] for i in range(4))
        self.part, self.rows = part, rows
        self.heads = rows // part
        self.row = 1 - self.y if far else self.y
        self.kv_all, self.docs_all, self.tile_docs = kv_all, docs_all, tile_docs
        self.blocks = kv_all.shape[1]
        self.steps = steps = range(lines)
        z_at = [lax.rem(self.z + by, nz) * (2 * nx) for by in steps]
        x_at = [lax.rem(self.x + by, nx) for by in steps]

        def places(which):
            return [
                [
                    jnp.where(which == 0, x_at[i], z_at[i]) + jnp.where(which == 0, z_at[j], x_at[j])
                    for j in steps
                ]
                for i in steps
            ]

        self.spots = (places(self.core), places(1 - self.core))
        apart = nz // PEERS
        self.apart = apart
        self.row_token = lax.div(self.z, apart) * part + lax.rem(
            lax.broadcasted_iota(jnp.int32, (CHUNK, self.rows), 1), part
        )
        key_row = lax.broadcasted_iota(jnp.int32, (CHUNK, self.rows), 0)
        self.key_row = key_row
        self.key_token = key_row + lax.div(key_row, BLOCK) * BLOCK

    def tile(self, t):
        dz = t * self.apart
        block = (lax.rem(self.z + self.nz - dz, self.nz) * 2 + self.core) * (2 * self.nx) + self.x * 2 + self.row
        doc = self.tile_docs[t, :1, :]
        before = jnp.sum(jnp.where(self.docs_all[...] < doc, 0.125, 0.0), axis=(0, 1))
        first = jnp.max(before).astype(jnp.int32)
        held = lax.div(block - self.y + 2, 2) - first
        chunks = lax.div(held + CHUNK_BLOCKS - 1, CHUNK_BLOCKS)
        last = jnp.maximum(chunks - 1, 0)

        def keys_at(n):
            return jnp.minimum(first + n * CHUNK_BLOCKS, self.blocks - CHUNK_BLOCKS)

        begin = keys_at(last)
        skipped = (first + last * CHUNK_BLOCKS - begin) * BLOCK
        reach = (block - 2 * begin - self.y) * BLOCK
        mask = (self.key_token <= self.row_token + reach) & (self.key_row >= skipped)
        return chunks, last, keys_at, mask

    def key_rows(self, which, at):
        return self.kv_all[which, pl.ds(at, CHUNK_BLOCKS)].reshape(CHUNK, HEAD)


def place_keys(s, pieces, kv_all, docs_all):
    for which, arrived, spot in ((s.core, pieces[0], s.spots[0]), (1 - s.core, pieces[1], s.spots[1])):
        for i in s.steps:
            for j in s.steps:
                for c in range(2):
                    kv_all[which, spot[-i][-j] + s.nx * c] = arrived[i][j, c * BLOCK : (c + 1) * BLOCK]
    for i in s.steps:
        for j in s.steps:
            docs_all[i * s.nz + j] = pieces[0][i][j, 2 * BLOCK :].astype(jnp.float32)


def place_rows(s, sources, tile_docs, cols, rows):
    part, width = s.part, s.heads * HEAD
    for t, (source, begin) in enumerate(sources):
        tile_docs[t] = source[begin : begin + DOC_ROWS, 2 * width :].astype(jnp.float32)
        for side in range(2):
            whole = jnp.concatenate(
                [
                    source[begin : begin + part, side * width + h * HEAD : side * width + (h + 1) * HEAD]
                    for h in range(s.heads)
                ]
            )
            rows[side, t] = whole
            cols[side, t] = whole.T


def near_statistics(sizes, *refs):
    lines = sizes[0]
    count = 3 + 2 * lines
    place_ref, own_ref, peer_ref = refs[:3]
    stats_ref, tile_docs, cols, tile_rows, kv_all, docs_all = refs[count:]
    s = Setting(sizes, place_ref, kv_all, docs_all, tile_docs, cols.shape[-1], own_ref.shape[0], False)
    place_keys(s, (refs[3 : 3 + lines], refs[3 + lines : count]), kv_all, docs_all)
    place_rows(s, ((own_ref, 0), (peer_ref, 0)), tile_docs, cols, tile_rows)
    statistics(s, stats_ref, cols)


def far_statistics(sizes, *refs):
    place_ref, far_ref, kv_all, docs_all, stats_ref, tile_docs, cols, tile_rows = refs
    part = far_ref.shape[0] // TILES
    s = Setting(sizes, place_ref, kv_all, docs_all, tile_docs, cols.shape[-1], part, True)
    place_rows(s, ((far_ref, 0), (far_ref, part)), tile_docs, cols, tile_rows)
    statistics(s, stats_ref, cols)


def statistics(s, stats_ref, cols):
    rows = s.rows

    def fold(value, combine):
        return combine(value.reshape(CHUNK // 8, 8, rows), axis=0)

    def tile(t, carry):
        chunks, last, keys_at, mask = s.tile(t)

        def step(n, state, masked):
            top, norm, weighted = state
            at = keys_at(n)
            value = dot(s.key_rows(0, at), cols[0, t], (1, 0))
            if masked:
                value = jnp.where(mask, value, NEG)
            dp = dot(s.key_rows(1, at), cols[1, t], (1, 0))
            raised = jnp.maximum(top, jnp.max(fold(value, jnp.max), axis=0, keepdims=True) * TO_EXP2)
            e = jnp.exp2(value * TO_EXP2 - raised)
            factor = jnp.exp2(top - raised)
            return raised, norm * factor + fold(e, jnp.sum), weighted * factor + fold(e * dp, jnp.sum)

        zeros = jnp.zeros((8, rows), jnp.float32)
        state = (jnp.full((1, rows), NEG, jnp.float32), zeros, zeros)
        state = lax.fori_loop(0, last, lambda n, state: step(n, state, False), state)
        top, norm, weighted = lax.fori_loop(last, chunks, lambda n, state: step(n, state, True), state)
        stats_ref[t, 0:1, :] = top
        stats_ref[t, 1:2, :] = jnp.sum(norm, axis=0, keepdims=True)
        stats_ref[t, 2:3, :] = jnp.sum(weighted, axis=0, keepdims=True)
        return carry

    stats_ref[...] = jnp.zeros_like(stats_ref)
    lax.fori_loop(0, TILES, tile, 0)


def far_gradients(sizes, *refs):
    place_ref, here_ref, there_ref, tile_docs, cols, tile_rows, kv_all, docs_all, dq_ref, totals = refs
    s = Setting(sizes, place_ref, kv_all, docs_all, tile_docs, cols.shape[-1], dq_ref.shape[1], True)
    totals[...] = jnp.zeros_like(totals)
    gradients(s, here_ref, there_ref, cols, tile_rows, dq_ref, totals)


def near_gradients(sizes, *refs):
    lines = sizes[0]
    place_ref, here_ref, there_ref, tile_docs, cols, tile_rows, kv_all, docs_all, so_far, dq_ref = refs[:10]
    keep, send = refs[10 : 10 + lines], refs[10 + lines : 10 + 2 * lines]
    totals = refs[10 + 2 * lines]
    s = Setting(sizes, place_ref, kv_all, docs_all, tile_docs, cols.shape[-1], dq_ref.shape[1], False)
    totals[...] = so_far[...]
    gradients(s, here_ref, there_ref, cols, tile_rows, dq_ref, totals)
    for which, out, spot in ((s.core, keep, s.spots[0]), (1 - s.core, send, s.spots[1])):
        for i in s.steps:
            for j in s.steps:
                for c in range(2):
                    begin = pl.multiple_of((spot[i][j] + s.nx * c) * BLOCK, BLOCK)
                    out[i][j, c] = totals[which, pl.ds(begin, BLOCK), :].astype(jnp.bfloat16)


def gradients(s, here_ref, there_ref, cols, tile_rows, dq_ref, totals):
    part, rows = s.part, s.rows

    def tile(t, carry):
        chunks, last, keys_at, mask = s.tile(t)
        top_here, top_there = here_ref[t, 0:1, :], there_ref[t, 0:1, :]
        top = jnp.maximum(top_here, top_there)
        weight_here, weight_there = jnp.exp2(top_here - top), jnp.exp2(top_there - top)
        norm = here_ref[t, 1:2, :] * weight_here + there_ref[t, 1:2, :] * weight_there
        weighted = here_ref[t, 2:3, :] * weight_here + there_ref[t, 2:3, :] * weight_there
        delta = weighted / norm
        top = top + jnp.log2(norm)

        def work(n, dq, masked):
            at = keys_at(n)
            keys = pl.ds(pl.multiple_of(at * BLOCK, BLOCK), CHUNK)
            value = dot(s.key_rows(0, at), cols[0, t], (1, 0))
            if masked:
                value = jnp.where(mask, value, NEG)
            p = jnp.exp2(value * TO_EXP2 - top)
            ds = p * (dot(s.key_rows(1, at), cols[1, t], (1, 0)) - delta)
            p_low = p.astype(jnp.bfloat16)
            ds_low = ds.astype(jnp.bfloat16)
            totals[0, keys, :] += dot(ds_low, tile_rows[0, t], (1, 0))
            totals[1, keys, :] += dot(p_low, tile_rows[1, t], (1, 0))
            return dq + dot(s.key_rows(0, at), ds_low, (0, 0))

        dq = jnp.zeros((HEAD, rows), jnp.float32)
        dq = lax.fori_loop(0, last, lambda n, dq: work(n, dq, False), dq)
        dq = lax.fori_loop(last, chunks, lambda n, dq: work(n, dq, True), dq)
        dq = (dq * SCALE).T
        for h in range(s.heads):
            dq_ref[t, :, h * HEAD : (h + 1) * HEAD] = dq[h * part : (h + 1) * part, :].astype(dq_ref.dtype)
        return carry

    lax.fori_loop(0, TILES, tile, 0)

def kernel_call(kernel, sizes, operands, outs, scratch, products):
    whole = pl.BlockSpec(memory_space=pltpu.VMEM)
    return pl.pallas_call(
        lambda *refs: kernel(sizes, *refs),
        name=kernel.__name__,
        out_shape=outs,
        in_specs=[pl.BlockSpec(memory_space=pltpu.SMEM)] + [whole] * (len(operands) - 1),
        out_specs=(whole,) * len(outs),
        scratch_shapes=scratch,
        compiler_params=pltpu.CompilerParams(vmem_limit_bytes=VMEM_MIB * 1024 * 1024),
        cost_estimate=pl.CostEstimate(
            flops=products * 2 * 12 * 1024 * 128 * 128, bytes_accessed=8 * 1024 * 1024, transcendentals=0
        ),
    )(*operands)


def tile_outs(rows):
    return (
        jax.ShapeDtypeStruct((TILES, 8, rows), jnp.float32),
        jax.ShapeDtypeStruct((TILES, DOC_ROWS, HEAD), jnp.float32),
        jax.ShapeDtypeStruct((2, TILES, HEAD, rows), jnp.bfloat16),
        jax.ShapeDtypeStruct((2, TILES, rows, HEAD), jnp.bfloat16),
    )


def near_statistics_call(sizes, rows, *operands):
    nz, nx = sizes
    outs = tile_outs(rows) + (
        jax.ShapeDtypeStruct((2, 2 * nz * nx, BLOCK, HEAD), jnp.bfloat16),
        jax.ShapeDtypeStruct((nz * nx, DOC_ROWS, HEAD), jnp.float32),
    )
    outs = kernel_call(near_statistics, sizes, operands, outs, [], 2)
    return outs[0], outs[1:4], outs[4:]


def far_statistics_call(sizes, rows, *operands):
    outs = kernel_call(far_statistics, sizes, operands, tile_outs(rows), [], 2)
    return outs[0], outs[1:]


def far_gradients_call(sizes, dq_shape, *operands):
    nz, nx = sizes
    totals = jax.ShapeDtypeStruct((2, 2 * nz * nx * BLOCK, HEAD), jnp.float32)
    outs = (jax.ShapeDtypeStruct(dq_shape, jnp.bfloat16), totals)
    return kernel_call(far_gradients, sizes, operands, outs, [], 5)


def near_gradients_call(sizes, dq_shape, *operands):
    nz, nx = sizes
    outs = (jax.ShapeDtypeStruct(dq_shape, jnp.float32),)
    outs += (jax.ShapeDtypeStruct((nx, 2, BLOCK, HEAD), jnp.bfloat16),) * (2 * nz)
    scratch = [pltpu.VMEM((2, 2 * nz * nx * BLOCK, HEAD), jnp.float32)]
    return kernel_call(near_gradients, sizes, operands, outs, scratch, 5)


def low(value):
    return value.astype(jnp.bfloat16)


def added(terms):
    total = terms[0].astype(jnp.float32)
    for term in terms[1:]:
        total = total + term.astype(jnp.float32)
    return total


def per_device(queries, keys, values, grad_out, block_docs):
    rows, width = queries.shape
    inner_size, outer_size = lax.axis_size("inner"), lax.axis_size("outer")
    nz, nx = inner_size // 2, outer_size // 2
    inner, outer = lax.axis_index("inner"), lax.axis_index("outer")
    z, core = lax.div(inner, 2), lax.rem(inner, 2)
    x, y = lax.div(outer, 2), lax.rem(outer, 2)
    part = rows // PEERS
    apart = nz // PEERS
    lines = nz

    def moved(value, step):
        hops = []
        for source in range(inner_size * outer_size):
            i, o = divmod(source, outer_size)
            dz, dx, dy, dc = step(i % 2)
            to_inner = (i // 2 + dz) % nz * 2 + (i % 2 + dc) % 2
            to_outer = (o // 2 + dx) % nx * 2 + (o % 2 + dy) % 2
            hops.append((source, to_inner * outer_size + to_outer))
        return lax.ppermute(value, CONTEXT, hops)

    def other_core(value):
        return moved(value, lambda c: (0, 0, 0, 1))

    def other_y(value):
        return moved(value, lambda c: (0, 0, 1, 0))

    def peer(value):
        return moved(value, lambda c: (apart, 0, 0, 0))

    def along_first(value, by):
        return moved(value, lambda c: (0, by, 0, 0) if c else (by, 0, 0, 0))

    def along_second(value, by):
        return moved(value, lambda c: (by, 0, 0, 0) if c else (0, by, 0, 0))

    def in_order(index, mine, theirs, axis):
        return jnp.where(
            index == 0, jnp.stack([mine, theirs], axis=axis), jnp.stack([theirs, mine], axis=axis)
        )

    doc = jnp.broadcast_to(low(block_docs)[:, None], (DOC_ROWS, HEAD))
    half = lax.div(z, apart)

    def rows_of(which):
        cut = [lax.dynamic_slice_in_dim(whole, which * part, part, 0) for whole in (queries, grad_out)]
        return jnp.concatenate(cut + [jnp.broadcast_to(low(block_docs)[:, None], (part, HEAD))], axis=1)

    own = rows_of(half)
    borrowed = peer(rows_of(1 - half))
    shared = jnp.concatenate([own, borrowed])

    given = other_core(jnp.where(core == 0, values, keys))
    kept = jnp.where(core == 0, keys, values)
    unit_docs = other_core(doc)
    rows_in_order = in_order(core, kept, given, 0).reshape(2 * BLOCK, HEAD)
    docs_in_order = in_order(core, doc[:8], unit_docs[:8], 0).reshape(DOC_ROWS, HEAD)
    unit = jnp.concatenate([rows_in_order, docs_in_order])
    line = jnp.stack([unit] + [along_first(unit, by) for by in range(1, lines)])
    line, shared = lax.optimization_barrier((line, shared))
    far = other_y(shared)
    mine = [line] + [along_second(line, by) for by in range(1, lines)]
    theirs = [other_core(piece) for piece in mine]

    place = jnp.stack([z, x, y, core]).astype(jnp.int32)
    sizes = (nz, nx)
    tile_rows = part * width // HEAD
    near_here, near_tiles, keys_all = near_statistics_call(sizes, tile_rows, place, own, borrowed, *mine, *theirs)
    far_there = other_y(near_here)
    far_here, far_tiles = far_statistics_call(sizes, tile_rows, place, far, *keys_all)
    near_there = other_y(far_here)
    dq_shape = (TILES, part, width)
    far_dq, so_far = far_gradients_call(sizes, dq_shape, place, far_here, far_there, *far_tiles, *keys_all)
    far_dq, near_there = lax.optimization_barrier((far_dq, near_there))
    rest = other_y(far_dq)
    dq, *sums = near_gradients_call(
        sizes, dq_shape, place, near_here, near_there, *near_tiles, *keys_all, so_far
    )
    rest, *sums = lax.optimization_barrier((rest, *sums))
    keep, send = sums[:lines], sums[lines:]

    totals = [None] * lines
    for by in [*range(1, lines), 0]:
        totals[by] = low(added([keep[by], other_core(send[by])]))
    arrived = [along_second(totals[by], by) for by in range(1, lines)]
    dq, totals[0] = lax.optimization_barrier((dq, totals[0]))
    dq = low(dq + rest.astype(jnp.float32))
    returned = peer(dq[1])
    total = low(added([totals[0]] + arrived))
    short = [along_first(total[by], by) for by in range(1, lines)]
    short, returned = lax.optimization_barrier((short, returned))
    total = added([total[0]] + short)
    total = low(jnp.where(core == 0, SCALE * total, total))
    ours = jnp.where(core == 0, total[0], total[1])
    theirs = other_core(jnp.where(core == 0, total[1], total[0]))
    grad_keys = jnp.where(core == 0, ours, theirs)
    grad_values = jnp.where(core == 0, theirs, ours)
    grad_queries = in_order(half, dq[0], returned, 0).reshape(rows, width)
    return grad_queries, grad_keys, grad_values


def solution(mesh):
    wide = P(CONTEXT, "head")
    return jax.shard_map(
        per_device,
        mesh=mesh,
        in_specs=(wide, wide, wide, wide, P(CONTEXT)),
        out_specs=(wide, wide, wide),
        check_vma=False,
    )
```

```python
import math

import jax
import jax.numpy as jnp
from jax import lax
from jax.experimental import pallas as pl
from jax.experimental.pallas import tpu as pltpu
from jax.sharding import PartitionSpec as P

NEG = -1e30
HEAD = 128
BLOCK = 128
DOC_ROWS = 16
CHUNK_BLOCKS = 5
CHUNK = CHUNK_BLOCKS * BLOCK
TILES = 2
VMEM_MIB = 36
PEERS = 2
SCALE = float(HEAD) ** (-0.5)
TO_EXP2 = SCALE * math.log2(math.e)
CONTEXT = ("inner", "outer")


def dot(lhs, rhs, over):
    return lax.dot_general(lhs, rhs, ((over[:1], over[1:]), ((), ())), preferred_element_type=jnp.float32)


class Setting:
    def __init__(self, sizes, place_ref, kv_all, docs_all, tile_docs, rows, part, far):
        self.nz, self.nx = nz, nx = sizes
        self.z, self.x, self.y, self.core = (place_ref[i] for i in range(4))
        self.part, self.rows = part, rows
        self.heads = rows // part
        self.row = 1 - self.y if far else self.y
        self.kv_all, self.docs_all, self.tile_docs = kv_all, docs_all, tile_docs
        self.blocks = kv_all.shape[1]
        apart = nz // PEERS
        self.apart = apart
        self.row_token = lax.div(self.z, apart) * part + lax.rem(
            lax.broadcasted_iota(jnp.int32, (CHUNK, self.rows), 1), part
        )
        key_row = lax.broadcasted_iota(jnp.int32, (CHUNK, self.rows), 0)
        self.key_row = key_row
        self.key_token = key_row + lax.div(key_row, BLOCK) * BLOCK

    def tile(self, t):
        dz = t * self.apart
        block = (lax.rem(self.z + self.nz - dz, self.nz) * 2 + self.core) * (2 * self.nx) + self.x * 2 + self.row
        doc = self.tile_docs[t, :1, :]
        before = jnp.sum(jnp.where(self.docs_all[...] < doc, 0.125, 0.0), axis=(0, 1))
        first = jnp.max(before).astype(jnp.int32)
        held = lax.div(block - self.y + 2, 2) - first
        chunks = lax.div(held + CHUNK_BLOCKS - 1, CHUNK_BLOCKS)
        last = jnp.maximum(chunks - 1, 0)

        def keys_at(n):
            return jnp.minimum(first + n * CHUNK_BLOCKS, self.blocks - CHUNK_BLOCKS)

        begin = keys_at(last)
        skipped = (first + last * CHUNK_BLOCKS - begin) * BLOCK
        reach = (block - 2 * begin - self.y) * BLOCK
        mask = (self.key_token <= self.row_token + reach) & (self.key_row >= skipped)
        return chunks, last, keys_at, mask

    def key_rows(self, which, at):
        return self.kv_all[which, pl.ds(at, CHUNK_BLOCKS)].reshape(CHUNK, HEAD)


def place_keys(s, pieces, kv_all, docs_all):
    for which, arrived in ((s.core, pieces[0]), (1 - s.core, pieces[1])):
        for chip in range(s.nz * s.nx):
            for c in range(2):
                at = chip // s.nx * 2 * s.nx + c * s.nx + chip % s.nx
                kv_all[which, at] = arrived[chip, c * BLOCK : (c + 1) * BLOCK]
    docs_all[...] = pieces[0][:, 2 * BLOCK :].astype(jnp.float32)


def place_rows(s, sources, tile_docs, cols, rows):
    part, width = s.part, s.heads * HEAD
    for t, source in enumerate(sources):
        tile_docs[t] = source[:DOC_ROWS, 2 * width :].astype(jnp.float32)
        for side in range(2):
            whole = jnp.concatenate(
                [
                    source[:, side * width + h * HEAD : side * width + (h + 1) * HEAD]
                    for h in range(s.heads)
                ]
            )
            rows[side, t] = whole
            cols[side, t] = whole.T


def near_statistics(sizes, *refs):
    place_ref, own_ref, peer_ref, mine, theirs, stats_ref, tile_docs, cols, tile_rows, kv_all, docs_all = refs
    s = Setting(sizes, place_ref, kv_all, docs_all, tile_docs, cols.shape[-1], own_ref.shape[0], False)
    place_keys(s, (mine, theirs), kv_all, docs_all)
    place_rows(s, (own_ref, peer_ref), tile_docs, cols, tile_rows)
    statistics(s, stats_ref, cols)


def far_statistics(sizes, *refs):
    place_ref, own_ref, peer_ref, kv_all, docs_all, stats_ref, tile_docs, cols, tile_rows = refs
    s = Setting(sizes, place_ref, kv_all, docs_all, tile_docs, cols.shape[-1], own_ref.shape[0], True)
    place_rows(s, (own_ref, peer_ref), tile_docs, cols, tile_rows)
    statistics(s, stats_ref, cols)


def statistics(s, stats_ref, cols):
    rows = s.rows

    def fold(value, combine):
        return combine(value.reshape(CHUNK // 8, 8, rows), axis=0)

    def tile(t, carry):
        chunks, last, keys_at, mask = s.tile(t)

        def step(n, state, masked):
            top, norm, weighted = state
            at = keys_at(n)
            value = dot(s.key_rows(0, at), cols[0, t], (1, 0))
            if masked:
                value = jnp.where(mask, value, NEG)
            dp = dot(s.key_rows(1, at), cols[1, t], (1, 0))
            raised = jnp.maximum(top, jnp.max(fold(value, jnp.max), axis=0, keepdims=True) * TO_EXP2)
            e = jnp.exp2(value * TO_EXP2 - raised)
            factor = jnp.exp2(top - raised)
            return raised, norm * factor + fold(e, jnp.sum), weighted * factor + fold(e * dp, jnp.sum)

        zeros = jnp.zeros((8, rows), jnp.float32)
        state = (jnp.full((1, rows), NEG, jnp.float32), zeros, zeros)
        state = lax.fori_loop(0, last, lambda n, state: step(n, state, False), state)
        top, norm, weighted = lax.fori_loop(last, chunks, lambda n, state: step(n, state, True), state)
        stats_ref[t, 0:1, :] = top
        stats_ref[t, 1:2, :] = jnp.sum(norm, axis=0, keepdims=True)
        stats_ref[t, 2:3, :] = jnp.sum(weighted, axis=0, keepdims=True)
        return carry

    stats_ref[...] = jnp.zeros_like(stats_ref)
    lax.fori_loop(0, TILES, tile, 0)


def far_gradients(sizes, *refs):
    place_ref, here_ref, there_ref, tile_docs, cols, tile_rows, kv_all, docs_all, dq_ref, totals = refs
    s = Setting(sizes, place_ref, kv_all, docs_all, tile_docs, cols.shape[-1], dq_ref.shape[1], True)
    totals[...] = jnp.zeros_like(totals)
    gradients(s, here_ref, there_ref, cols, tile_rows, dq_ref, totals)


def near_gradients(sizes, *refs):
    place_ref, here_ref, there_ref, tile_docs, cols, tile_rows, kv_all, docs_all, so_far = refs[:9]
    dq_ref, keep, send, totals = refs[9:]
    s = Setting(sizes, place_ref, kv_all, docs_all, tile_docs, cols.shape[-1], dq_ref.shape[1], False)
    totals[...] = so_far[...]
    gradients(s, here_ref, there_ref, cols, tile_rows, dq_ref, totals)
    for which, out in ((s.core, keep), (1 - s.core, send)):
        for chip in range(s.nz * s.nx):
            for c in range(2):
                begin = (chip // s.nx * 2 * s.nx + c * s.nx + chip % s.nx) * BLOCK
                out[chip, c] = totals[which, begin : begin + BLOCK, :].astype(jnp.bfloat16)


def gradients(s, here_ref, there_ref, cols, tile_rows, dq_ref, totals):
    part, rows = s.part, s.rows

    def tile(t, carry):
        chunks, last, keys_at, mask = s.tile(t)
        top_here, top_there = here_ref[t, 0:1, :], there_ref[t, 0:1, :]
        top = jnp.maximum(top_here, top_there)
        weight_here, weight_there = jnp.exp2(top_here - top), jnp.exp2(top_there - top)
        norm = here_ref[t, 1:2, :] * weight_here + there_ref[t, 1:2, :] * weight_there
        weighted = here_ref[t, 2:3, :] * weight_here + there_ref[t, 2:3, :] * weight_there
        delta = weighted / norm
        top = top + jnp.log2(norm)

        def work(n, dq, masked):
            at = keys_at(n)
            keys = pl.ds(pl.multiple_of(at * BLOCK, BLOCK), CHUNK)
            value = dot(s.key_rows(0, at), cols[0, t], (1, 0))
            if masked:
                value = jnp.where(mask, value, NEG)
            p = jnp.exp2(value * TO_EXP2 - top)
            ds = p * (dot(s.key_rows(1, at), cols[1, t], (1, 0)) - delta)
            p_low = p.astype(jnp.bfloat16)
            ds_low = ds.astype(jnp.bfloat16)
            totals[0, keys, :] += dot(ds_low, tile_rows[0, t], (1, 0))
            totals[1, keys, :] += dot(p_low, tile_rows[1, t], (1, 0))
            return dq + dot(s.key_rows(0, at), ds_low, (0, 0))

        dq = jnp.zeros((HEAD, rows), jnp.float32)
        dq = lax.fori_loop(0, last, lambda n, dq: work(n, dq, False), dq)
        dq = lax.fori_loop(last, chunks, lambda n, dq: work(n, dq, True), dq)
        dq = (dq * SCALE).T
        for h in range(s.heads):
            dq_ref[t, :, h * HEAD : (h + 1) * HEAD] = dq[h * part : (h + 1) * part, :].astype(dq_ref.dtype)
        return carry

    lax.fori_loop(0, TILES, tile, 0)

def kernel_call(kernel, sizes, operands, outs, scratch, products):
    whole = pl.BlockSpec(memory_space=pltpu.VMEM)
    return pl.pallas_call(
        lambda *refs: kernel(sizes, *refs),
        name=kernel.__name__,
        out_shape=outs,
        in_specs=[pl.BlockSpec(memory_space=pltpu.SMEM)] + [whole] * (len(operands) - 1),
        out_specs=(whole,) * len(outs),
        scratch_shapes=scratch,
        compiler_params=pltpu.CompilerParams(vmem_limit_bytes=VMEM_MIB * 1024 * 1024),
        cost_estimate=pl.CostEstimate(
            flops=products * 2 * 12 * 1024 * 128 * 128, bytes_accessed=8 * 1024 * 1024, transcendentals=0
        ),
    )(*operands)


def tile_outs(rows):
    return (
        jax.ShapeDtypeStruct((TILES, 8, rows), jnp.float32),
        jax.ShapeDtypeStruct((TILES, DOC_ROWS, HEAD), jnp.float32),
        jax.ShapeDtypeStruct((2, TILES, HEAD, rows), jnp.bfloat16),
        jax.ShapeDtypeStruct((2, TILES, rows, HEAD), jnp.bfloat16),
    )


def near_statistics_call(sizes, rows, *operands):
    nz, nx = sizes
    outs = tile_outs(rows) + (
        jax.ShapeDtypeStruct((2, 2 * nz * nx, BLOCK, HEAD), jnp.bfloat16),
        jax.ShapeDtypeStruct((nz * nx, DOC_ROWS, HEAD), jnp.float32),
    )
    outs = kernel_call(near_statistics, sizes, operands, outs, [], 2)
    return outs[0], outs[1:4], outs[4:]


def far_statistics_call(sizes, rows, *operands):
    outs = kernel_call(far_statistics, sizes, operands, tile_outs(rows), [], 2)
    return outs[0], outs[1:]


def far_gradients_call(sizes, dq_shape, *operands):
    nz, nx = sizes
    totals = jax.ShapeDtypeStruct((2, 2 * nz * nx * BLOCK, HEAD), jnp.float32)
    outs = (jax.ShapeDtypeStruct(dq_shape, jnp.bfloat16), totals)
    return kernel_call(far_gradients, sizes, operands, outs, [], 5)


def near_gradients_call(sizes, dq_shape, *operands):
    nz, nx = sizes
    outs = (jax.ShapeDtypeStruct(dq_shape, jnp.float32),)
    outs += (jax.ShapeDtypeStruct((nz * nx, 2, BLOCK, HEAD), jnp.bfloat16),) * 2
    scratch = [pltpu.VMEM((2, 2 * nz * nx * BLOCK, HEAD), jnp.float32)]
    return kernel_call(near_gradients, sizes, operands, outs, scratch, 5)


def low(value):
    return value.astype(jnp.bfloat16)


def added(terms):
    total = terms[0].astype(jnp.float32)
    for term in terms[1:]:
        total = total + term.astype(jnp.float32)
    return total


def per_device(queries, keys, values, grad_out, block_docs):
    rows, width = queries.shape
    inner_size, outer_size = lax.axis_size("inner"), lax.axis_size("outer")
    nz, nx = inner_size // 2, outer_size // 2
    inner, outer = lax.axis_index("inner"), lax.axis_index("outer")
    z, core = lax.div(inner, 2), lax.rem(inner, 2)
    x, y = lax.div(outer, 2), lax.rem(outer, 2)
    part = rows // PEERS
    apart = nz // PEERS

    def moved(value, step):
        hops = []
        for source in range(inner_size * outer_size):
            i, o = divmod(source, outer_size)
            dz, dx, dy, dc = step(i % 2)
            to_inner = (i // 2 + dz) % nz * 2 + (i % 2 + dc) % 2
            to_outer = (o // 2 + dx) % nx * 2 + (o % 2 + dy) % 2
            hops.append((source, to_inner * outer_size + to_outer))
        return lax.ppermute(value, CONTEXT, hops)

    def other_core(value):
        return moved(value, lambda c: (0, 0, 0, 1))

    def other_y(value):
        return moved(value, lambda c: (0, 0, 1, 0))

    def peer(value):
        return moved(value, lambda c: (apart, 0, 0, 0))

    members = [
        [(iz * 2 + c) * outer_size + ix * 2 + iy for iz in range(nz) for ix in range(nx)]
        for iy in range(2)
        for c in range(2)
    ]

    def exchanged(value):
        return lax.all_to_all(value, CONTEXT, 0, 0, tiled=True, axis_index_groups=members)

    def in_order(index, mine, theirs, axis):
        return jnp.where(
            index == 0, jnp.stack([mine, theirs], axis=axis), jnp.stack([theirs, mine], axis=axis)
        )

    doc = jnp.broadcast_to(low(block_docs)[:, None], (DOC_ROWS, HEAD))
    half = lax.div(z, apart)

    def rows_of(which):
        cut = [lax.dynamic_slice_in_dim(whole, which * part, part, 0) for whole in (queries, grad_out)]
        return jnp.concatenate(cut + [jnp.broadcast_to(low(block_docs)[:, None], (part, HEAD))], axis=1)

    own = rows_of(half)
    borrowed = peer(rows_of(1 - half))
    far_own = other_y(own)

    given = other_core(jnp.concatenate([jnp.where(core == 0, values, keys), doc]))
    kept = jnp.where(core == 0, keys, values)
    rows_in_order = in_order(core, kept, given[:BLOCK], 0).reshape(2 * BLOCK, HEAD)
    docs_in_order = in_order(core, doc[:8], given[BLOCK : BLOCK + 8], 0).reshape(DOC_ROWS, HEAD)
    unit = jnp.concatenate([rows_in_order, docs_in_order])
    mine = exchanged(jnp.broadcast_to(unit, (nz * nx, *unit.shape)))
    mine, borrowed, far_own = lax.optimization_barrier((mine, borrowed, far_own))
    far_borrowed = other_y(borrowed)
    theirs = other_core(mine)

    place = jnp.stack([z, x, y, core]).astype(jnp.int32)
    sizes = (nz, nx)
    tile_rows = part * width // HEAD
    near_here, near_tiles, keys_all = near_statistics_call(sizes, tile_rows, place, own, borrowed, mine, theirs)
    far_there = other_y(near_here)
    far_here, far_tiles = far_statistics_call(sizes, tile_rows, place, far_own, far_borrowed, *keys_all)
    near_there = other_y(far_here)
    dq_shape = (TILES, part, width)
    far_dq, so_far = far_gradients_call(sizes, dq_shape, place, far_here, far_there, *far_tiles, *keys_all)
    far_dq, near_there = lax.optimization_barrier((far_dq, near_there))
    rest = other_y(far_dq)
    dq, keep, send = near_gradients_call(
        sizes, dq_shape, place, near_here, near_there, *near_tiles, *keys_all, so_far
    )
    rest, dq, keep, send = lax.optimization_barrier((rest, dq, keep, send))
    dq = low(dq + rest.astype(jnp.float32))
    returned = peer(dq[1])

    total = exchanged(low(added([keep, other_core(send)])))
    total, returned = lax.optimization_barrier((total, returned))
    total = jnp.sum(total.astype(jnp.float32), axis=0)
    total = low(jnp.where(core == 0, SCALE * total, total))
    ours = jnp.where(core == 0, total[0], total[1])
    theirs = other_core(jnp.where(core == 0, total[1], total[0]))
    grad_keys = jnp.where(core == 0, ours, theirs)
    grad_values = jnp.where(core == 0, theirs, ours)
    grad_queries = in_order(half, dq[0], returned, 0).reshape(rows, width)
    return grad_queries, grad_keys, grad_values


def solution(mesh):
    wide = P(CONTEXT, "head")
    return jax.shard_map(
        per_device,
        mesh=mesh,
        in_specs=(wide, wide, wide, wide, P(CONTEXT)),
        out_specs=(wide, wide, wide),
        check_vma=False,
    )
```

```python
import math

import jax
import jax.numpy as jnp
from jax import lax
from jax.experimental import pallas as pl
from jax.experimental.pallas import tpu as pltpu
from jax.sharding import PartitionSpec as P

NEG = -1e30
HEAD = 128
BLOCK = 128
DOC_ROWS = 16
CHUNK_BLOCKS = 5
CHUNK = CHUNK_BLOCKS * BLOCK
TILES = 2
VMEM_MIB = 36
PEERS = 2
SCALE = float(HEAD) ** (-0.5)
TO_EXP2 = SCALE * math.log2(math.e)
CONTEXT = ("inner", "outer")


def dot(lhs, rhs, over):
    return lax.dot_general(lhs, rhs, ((over[:1], over[1:]), ((), ())), preferred_element_type=jnp.float32)


class Setting:
    def __init__(self, sizes, place_ref, kv_all, docs_all, tile_docs, rows, part, far):
        self.nz, self.nx = nz, nx = sizes
        lines = nz
        self.z, self.x, self.y, self.core = (place_ref[i] for i in range(4))
        self.part, self.rows = part, rows
        self.heads = rows // part
        self.row = 1 - self.y if far else self.y
        self.kv_all, self.docs_all, self.tile_docs = kv_all, docs_all, tile_docs
        self.blocks = kv_all.shape[1]
        self.steps = steps = range(lines)
        z_at = [lax.rem(self.z + by, nz) * (2 * nx) for by in steps]
        x_at = [lax.rem(self.x + by, nx) for by in steps]

        def places(which):
            return [
                [
                    jnp.where(which == 0, x_at[i], z_at[i]) + jnp.where(which == 0, z_at[j], x_at[j])
                    for j in steps
                ]
                for i in steps
            ]

        self.spots = (places(self.core), places(1 - self.core))
        apart = nz // PEERS
        self.apart = apart
        self.row_token = lax.div(self.z, apart) * part + lax.rem(
            lax.broadcasted_iota(jnp.int32, (CHUNK, self.rows), 1), part
        )
        key_row = lax.broadcasted_iota(jnp.int32, (CHUNK, self.rows), 0)
        self.key_row = key_row
        self.key_token = key_row + lax.div(key_row, BLOCK) * BLOCK

    def tile(self, t):
        dz = t * self.apart
        block = (lax.rem(self.z + self.nz - dz, self.nz) * 2 + self.core) * (2 * self.nx) + self.x * 2 + self.row
        doc = self.tile_docs[t, :1, :]
        before = jnp.sum(jnp.where(self.docs_all[...] < doc, 0.125, 0.0), axis=(0, 1))
        first = jnp.max(before).astype(jnp.int32)
        held = lax.div(block - self.y + 2, 2) - first
        chunks = lax.div(held + CHUNK_BLOCKS - 1, CHUNK_BLOCKS)
        last = jnp.maximum(chunks - 1, 0)

        def keys_at(n):
            return jnp.minimum(first + n * CHUNK_BLOCKS, self.blocks - CHUNK_BLOCKS)

        begin = keys_at(last)
        skipped = (first + last * CHUNK_BLOCKS - begin) * BLOCK
        reach = (block - 2 * begin - self.y) * BLOCK
        mask = (self.key_token <= self.row_token + reach) & (self.key_row >= skipped)
        return chunks, last, keys_at, mask

    def key_rows(self, which, at):
        return self.kv_all[which, pl.ds(at, CHUNK_BLOCKS)].reshape(CHUNK, HEAD)


def place_keys(s, pieces, kv_all, docs_all):
    for which, arrived, spot in ((s.core, pieces[0], s.spots[0]), (1 - s.core, pieces[1], s.spots[1])):
        for i in s.steps:
            for j in s.steps:
                for c in range(2):
                    kv_all[which, spot[-i][-j] + s.nx * c] = arrived[i][j, c * BLOCK : (c + 1) * BLOCK]
    for i in s.steps:
        for j in s.steps:
            docs_all[i * s.nz + j] = pieces[0][i][j, 2 * BLOCK :].astype(jnp.float32)


def place_rows(s, sources, tile_docs, cols, rows):
    part, width = s.part, s.heads * HEAD
    for t, (source, begin) in enumerate(sources):
        tile_docs[t] = source[begin : begin + DOC_ROWS, 2 * width :].astype(jnp.float32)
        for side in range(2):
            whole = jnp.concatenate(
                [
                    source[begin : begin + part, side * width + h * HEAD : side * width + (h + 1) * HEAD]
                    for h in range(s.heads)
                ]
            )
            rows[side, t] = whole
            cols[side, t] = whole.T


def near_statistics(sizes, *refs):
    lines = sizes[0]
    count = 3 + 2 * lines
    place_ref, own_ref, peer_ref = refs[:3]
    stats_ref, tile_docs, cols, tile_rows, kv_all, docs_all = refs[count:]
    s = Setting(sizes, place_ref, kv_all, docs_all, tile_docs, cols.shape[-1], own_ref.shape[0], False)
    place_keys(s, (refs[3 : 3 + lines], refs[3 + lines : count]), kv_all, docs_all)
    place_rows(s, ((own_ref, 0), (peer_ref, 0)), tile_docs, cols, tile_rows)
    statistics(s, stats_ref, cols)


def far_statistics(sizes, *refs):
    place_ref, far_ref, kv_all, docs_all, stats_ref, tile_docs, cols, tile_rows = refs
    part = far_ref.shape[0] // TILES
    s = Setting(sizes, place_ref, kv_all, docs_all, tile_docs, cols.shape[-1], part, True)
    place_rows(s, ((far_ref, 0), (far_ref, part)), tile_docs, cols, tile_rows)
    statistics(s, stats_ref, cols)


def statistics(s, stats_ref, cols):
    rows = s.rows

    def fold(value, combine):
        return combine(value.reshape(CHUNK // 8, 8, rows), axis=0)

    def tile(t, carry):
        chunks, last, keys_at, mask = s.tile(t)

        def step(n, state, masked):
            top, norm, weighted = state
            at = keys_at(n)
            value = dot(s.key_rows(0, at), cols[0, t], (1, 0))
            if masked:
                value = jnp.where(mask, value, NEG)
            dp = dot(s.key_rows(1, at), cols[1, t], (1, 0))
            raised = jnp.maximum(top, jnp.max(fold(value, jnp.max), axis=0, keepdims=True) * TO_EXP2)
            e = jnp.exp2(value * TO_EXP2 - raised)
            factor = jnp.exp2(top - raised)
            return raised, norm * factor + fold(e, jnp.sum), weighted * factor + fold(e * dp, jnp.sum)

        zeros = jnp.zeros((8, rows), jnp.float32)
        state = (jnp.full((1, rows), NEG, jnp.float32), zeros, zeros)
        state = lax.fori_loop(0, last, lambda n, state: step(n, state, False), state)
        top, norm, weighted = lax.fori_loop(last, chunks, lambda n, state: step(n, state, True), state)
        stats_ref[t, 0:1, :] = top
        stats_ref[t, 1:2, :] = jnp.sum(norm, axis=0, keepdims=True)
        stats_ref[t, 2:3, :] = jnp.sum(weighted, axis=0, keepdims=True)
        return carry

    stats_ref[...] = jnp.zeros_like(stats_ref)
    lax.fori_loop(0, TILES, tile, 0)


def far_gradients(sizes, *refs):
    place_ref, here_ref, there_ref, tile_docs, cols, tile_rows, kv_all, docs_all, dq_ref, totals = refs
    s = Setting(sizes, place_ref, kv_all, docs_all, tile_docs, cols.shape[-1], dq_ref.shape[1], True)
    totals[...] = jnp.zeros_like(totals)
    gradients(s, here_ref, there_ref, cols, tile_rows, dq_ref, totals)


def near_gradients(sizes, *refs):
    lines = sizes[0]
    place_ref, here_ref, there_ref, tile_docs, cols, tile_rows, kv_all, docs_all, so_far, dq_ref = refs[:10]
    keep, send = refs[10 : 10 + lines], refs[10 + lines : 10 + 2 * lines]
    totals = refs[10 + 2 * lines]
    s = Setting(sizes, place_ref, kv_all, docs_all, tile_docs, cols.shape[-1], dq_ref.shape[1], False)
    totals[...] = so_far[...]
    gradients(s, here_ref, there_ref, cols, tile_rows, dq_ref, totals)
    for which, out, spot in ((s.core, keep, s.spots[0]), (1 - s.core, send, s.spots[1])):
        for i in s.steps:
            for j in s.steps:
                for c in range(2):
                    begin = pl.multiple_of((spot[i][j] + s.nx * c) * BLOCK, BLOCK)
                    out[i][j, c] = totals[which, pl.ds(begin, BLOCK), :].astype(jnp.bfloat16)


def gradients(s, here_ref, there_ref, cols, tile_rows, dq_ref, totals):
    part, rows = s.part, s.rows

    def tile(t, carry):
        chunks, last, keys_at, mask = s.tile(t)
        top_here, top_there = here_ref[t, 0:1, :], there_ref[t, 0:1, :]
        top = jnp.maximum(top_here, top_there)
        weight_here, weight_there = jnp.exp2(top_here - top), jnp.exp2(top_there - top)
        norm = here_ref[t, 1:2, :] * weight_here + there_ref[t, 1:2, :] * weight_there
        weighted = here_ref[t, 2:3, :] * weight_here + there_ref[t, 2:3, :] * weight_there
        delta = weighted / norm
        top = top + jnp.log2(norm)

        def work(n, dq, masked):
            at = keys_at(n)
            keys = pl.ds(pl.multiple_of(at * BLOCK, BLOCK), CHUNK)
            value = dot(s.key_rows(0, at), cols[0, t], (1, 0))
            if masked:
                value = jnp.where(mask, value, NEG)
            p = jnp.exp2(value * TO_EXP2 - top)
            ds = p * (dot(s.key_rows(1, at), cols[1, t], (1, 0)) - delta)
            p_low = p.astype(jnp.bfloat16)
            ds_low = ds.astype(jnp.bfloat16)
            totals[0, keys, :] += dot(ds_low, tile_rows[0, t], (1, 0))
            totals[1, keys, :] += dot(p_low, tile_rows[1, t], (1, 0))
            return dq + dot(s.key_rows(0, at), ds_low, (0, 0))

        dq = jnp.zeros((HEAD, rows), jnp.float32)
        dq = lax.fori_loop(0, last, lambda n, dq: work(n, dq, False), dq)
        dq = lax.fori_loop(last, chunks, lambda n, dq: work(n, dq, True), dq)
        dq = (dq * SCALE).T
        for h in range(s.heads):
            dq_ref[t, :, h * HEAD : (h + 1) * HEAD] = dq[h * part : (h + 1) * part, :].astype(dq_ref.dtype)
        return carry

    lax.fori_loop(0, TILES, tile, 0)

def kernel_call(kernel, sizes, operands, outs, scratch, products):
    whole = pl.BlockSpec(memory_space=pltpu.VMEM)
    return pl.pallas_call(
        lambda *refs: kernel(sizes, *refs),
        name=kernel.__name__,
        out_shape=outs,
        in_specs=[pl.BlockSpec(memory_space=pltpu.SMEM)] + [whole] * (len(operands) - 1),
        out_specs=(whole,) * len(outs),
        scratch_shapes=scratch,
        compiler_params=pltpu.CompilerParams(vmem_limit_bytes=VMEM_MIB * 1024 * 1024),
        cost_estimate=pl.CostEstimate(
            flops=products * 2 * 12 * 1024 * 128 * 128, bytes_accessed=8 * 1024 * 1024, transcendentals=0
        ),
    )(*operands)


def tile_outs(rows):
    return (
        jax.ShapeDtypeStruct((TILES, 8, rows), jnp.float32),
        jax.ShapeDtypeStruct((TILES, DOC_ROWS, HEAD), jnp.float32),
        jax.ShapeDtypeStruct((2, TILES, HEAD, rows), jnp.bfloat16),
        jax.ShapeDtypeStruct((2, TILES, rows, HEAD), jnp.bfloat16),
    )


def near_statistics_call(sizes, rows, *operands):
    nz, nx = sizes
    outs = tile_outs(rows) + (
        jax.ShapeDtypeStruct((2, 2 * nz * nx, BLOCK, HEAD), jnp.bfloat16),
        jax.ShapeDtypeStruct((nz * nx, DOC_ROWS, HEAD), jnp.float32),
    )
    outs = kernel_call(near_statistics, sizes, operands, outs, [], 2)
    return outs[0], outs[1:4], outs[4:]


def far_statistics_call(sizes, rows, *operands):
    outs = kernel_call(far_statistics, sizes, operands, tile_outs(rows), [], 2)
    return outs[0], outs[1:]


def far_gradients_call(sizes, dq_shape, *operands):
    nz, nx = sizes
    totals = jax.ShapeDtypeStruct((2, 2 * nz * nx * BLOCK, HEAD), jnp.float32)
    outs = (jax.ShapeDtypeStruct(dq_shape, jnp.bfloat16), totals)
    return kernel_call(far_gradients, sizes, operands, outs, [], 5)


def near_gradients_call(sizes, dq_shape, *operands):
    nz, nx = sizes
    outs = (jax.ShapeDtypeStruct(dq_shape, jnp.float32),)
    outs += (jax.ShapeDtypeStruct((nx, 2, BLOCK, HEAD), jnp.bfloat16),) * (2 * nz)
    scratch = [pltpu.VMEM((2, 2 * nz * nx * BLOCK, HEAD), jnp.float32)]
    return kernel_call(near_gradients, sizes, operands, outs, scratch, 5)


def low(value):
    return value.astype(jnp.bfloat16)


def added(terms):
    total = terms[0].astype(jnp.float32)
    for term in terms[1:]:
        total = total + term.astype(jnp.float32)
    return total


def per_device(queries, keys, values, grad_out, block_docs):
    rows, width = queries.shape
    inner_size, outer_size = lax.axis_size("inner"), lax.axis_size("outer")
    nz, nx = inner_size // 2, outer_size // 2
    inner, outer = lax.axis_index("inner"), lax.axis_index("outer")
    z, core = lax.div(inner, 2), lax.rem(inner, 2)
    x, y = lax.div(outer, 2), lax.rem(outer, 2)
    part = rows // PEERS
    apart = nz // PEERS
    lines = nz

    def moved(value, step):
        hops = []
        for source in range(inner_size * outer_size):
            i, o = divmod(source, outer_size)
            dz, dx, dy, dc = step(i % 2)
            to_inner = (i // 2 + dz) % nz * 2 + (i % 2 + dc) % 2
            to_outer = (o // 2 + dx) % nx * 2 + (o % 2 + dy) % 2
            hops.append((source, to_inner * outer_size + to_outer))
        return lax.ppermute(value, CONTEXT, hops)

    def other_core(value):
        return moved(value, lambda c: (0, 0, 0, 1))

    def other_y(value):
        return moved(value, lambda c: (0, 0, 1, 0))

    def peer(value):
        return moved(value, lambda c: (apart, 0, 0, 0))

    def along_first(value, by):
        return moved(value, lambda c: (0, by, 0, 0) if c else (by, 0, 0, 0))

    def along_second(value, by):
        return moved(value, lambda c: (by, 0, 0, 0) if c else (0, by, 0, 0))

    def in_order(index, mine, theirs, axis):
        return jnp.where(
            index == 0, jnp.stack([mine, theirs], axis=axis), jnp.stack([theirs, mine], axis=axis)
        )

    doc = jnp.broadcast_to(low(block_docs)[:, None], (DOC_ROWS, HEAD))
    half = lax.div(z, apart)

    def rows_of(which):
        cut = [lax.dynamic_slice_in_dim(whole, which * part, part, 0) for whole in (queries, grad_out)]
        return jnp.concatenate(cut + [jnp.broadcast_to(low(block_docs)[:, None], (part, HEAD))], axis=1)

    own = rows_of(half)
    borrowed = peer(rows_of(1 - half))
    shared = jnp.concatenate([own, borrowed])

    given = other_core(jnp.concatenate([jnp.where(core == 0, values, keys), doc]))
    kept = jnp.where(core == 0, keys, values)
    rows_in_order = in_order(core, kept, given[:BLOCK], 0).reshape(2 * BLOCK, HEAD)
    docs_in_order = in_order(core, doc[:8], given[BLOCK : BLOCK + 8], 0).reshape(DOC_ROWS, HEAD)
    unit = jnp.concatenate([rows_in_order, docs_in_order])
    line = jnp.stack([unit] + [along_first(unit, by) for by in range(1, lines)])
    far = other_y(shared)
    mine = [line] + [along_second(line, by) for by in range(1, lines)]
    theirs = [other_core(piece) for piece in mine]

    place = jnp.stack([z, x, y, core]).astype(jnp.int32)
    sizes = (nz, nx)
    tile_rows = part * width // HEAD
    near_here, near_tiles, keys_all = near_statistics_call(sizes, tile_rows, place, own, borrowed, *mine, *theirs)
    far_there = other_y(near_here)
    far_here, far_tiles = far_statistics_call(sizes, tile_rows, place, far, *keys_all)
    near_there = other_y(far_here)
    dq_shape = (TILES, part, width)
    far_dq, so_far = far_gradients_call(sizes, dq_shape, place, far_here, far_there, *far_tiles, *keys_all)
    far_dq, near_there = lax.optimization_barrier((far_dq, near_there))
    rest = other_y(far_dq)
    dq, *sums = near_gradients_call(
        sizes, dq_shape, place, near_here, near_there, *near_tiles, *keys_all, so_far
    )
    rest, *sums = lax.optimization_barrier((rest, *sums))
    keep, send = sums[:lines], sums[lines:]

    totals = [None] * lines
    for by in (2, 1, 3, 0):
        totals[by] = low(added([keep[by], other_core(send[by])]))
    arrived = [along_second(totals[by], by) for by in (2, 1, 3)]
    dq, totals[0] = lax.optimization_barrier((dq, totals[0]))
    dq = low(dq + rest.astype(jnp.float32))
    returned = peer(dq[1])
    total = low(added([totals[0]] + arrived))
    short = [along_first(total[by], by) for by in range(1, lines)]
    short, returned = lax.optimization_barrier((short, returned))
    total = added([total[0]] + short)
    total = low(jnp.where(core == 0, SCALE * total, total))
    ours = jnp.where(core == 0, total[0], total[1])
    theirs = other_core(jnp.where(core == 0, total[1], total[0]))
    grad_keys = jnp.where(core == 0, ours, theirs)
    grad_values = jnp.where(core == 0, theirs, ours)
    grad_queries = in_order(half, dq[0], returned, 0).reshape(rows, width)
    return grad_queries, grad_keys, grad_values


def solution(mesh):
    wide = P(CONTEXT, "head")
    return jax.shard_map(
        per_device,
        mesh=mesh,
        in_specs=(wide, wide, wide, wide, P(CONTEXT)),
        out_specs=(wide, wide, wide),
        check_vma=False,
    )
```

```python
import math

import jax
import jax.numpy as jnp
from jax import lax
from jax.experimental import pallas as pl
from jax.experimental.pallas import tpu as pltpu
from jax.sharding import PartitionSpec as P

NEG = -1e30
HEAD = 128
BLOCK = 128
DOC_ROWS = 16
CHUNK_BLOCKS = 4
CHUNK = CHUNK_BLOCKS * BLOCK
TILES = 2
VMEM_MIB = 36
PEERS = 2
SCALE = float(HEAD) ** (-0.5)
TO_EXP2 = SCALE * math.log2(math.e)
CONTEXT = ("inner", "outer")


def dot(lhs, rhs, over):
    return lax.dot_general(lhs, rhs, ((over[:1], over[1:]), ((), ())), preferred_element_type=jnp.float32)


class Setting:
    def __init__(self, sizes, place_ref, kv_all, docs_all, tile_docs, rows, part, far):
        self.nz, self.nx = nz, nx = sizes
        lines = nz
        self.z, self.x, self.y, self.core = (place_ref[i] for i in range(4))
        self.part, self.rows = part, rows
        self.heads = rows // part
        self.row = 1 - self.y if far else self.y
        self.kv_all, self.docs_all, self.tile_docs = kv_all, docs_all, tile_docs
        self.blocks = kv_all.shape[1]
        self.steps = steps = range(lines)
        z_at = [lax.rem(self.z + by, nz) * (2 * nx) for by in steps]
        x_at = [lax.rem(self.x + by, nx) for by in steps]

        def places(which):
            return [
                [
                    jnp.where(which == 0, x_at[i], z_at[i]) + jnp.where(which == 0, z_at[j], x_at[j])
                    for j in steps
                ]
                for i in steps
            ]

        self.spots = (places(self.core), places(1 - self.core))
        apart = nz // PEERS
        self.apart = apart
        self.row_token = lax.div(self.z, apart) * part + lax.rem(
            lax.broadcasted_iota(jnp.int32, (CHUNK, self.rows), 1), part
        )
        key_row = lax.broadcasted_iota(jnp.int32, (CHUNK, self.rows), 0)
        self.key_row = key_row
        self.key_token = key_row + lax.div(key_row, BLOCK) * BLOCK

    def tile(self, t):
        dz = t * self.apart
        block = (lax.rem(self.z + self.nz - dz, self.nz) * 2 + self.core) * (2 * self.nx) + self.x * 2 + self.row
        doc = self.tile_docs[t, :1, :]
        before = jnp.sum(jnp.where(self.docs_all[...] < doc, 0.125, 0.0), axis=(0, 1))
        first = jnp.max(before).astype(jnp.int32)
        held = lax.div(block - self.y + 2, 2) - first
        chunks = lax.div(held + CHUNK_BLOCKS - 1, CHUNK_BLOCKS)
        last = jnp.maximum(chunks - 1, 0)

        def keys_at(n):
            return jnp.minimum(first + n * CHUNK_BLOCKS, self.blocks - CHUNK_BLOCKS)

        begin = keys_at(last)
        skipped = (first + last * CHUNK_BLOCKS - begin) * BLOCK
        reach = (block - 2 * begin - self.y) * BLOCK
        mask = (self.key_token <= self.row_token + reach) & (self.key_row >= skipped)
        return chunks, last, keys_at, mask

    def key_rows(self, which, at):
        return self.kv_all[which, pl.ds(at, CHUNK_BLOCKS)].reshape(CHUNK, HEAD)


def place_keys(s, pieces, kv_all, docs_all):
    for which, arrived, spot in ((s.core, pieces[0], s.spots[0]), (1 - s.core, pieces[1], s.spots[1])):
        for i in s.steps:
            for j in s.steps:
                for c in range(2):
                    kv_all[which, spot[-i][-j] + s.nx * c] = arrived[i][j, c * BLOCK : (c + 1) * BLOCK]
    for i in s.steps:
        for j in s.steps:
            docs_all[i * s.nz + j] = pieces[0][i][j, 2 * BLOCK :].astype(jnp.float32)


def place_rows(s, sources, tile_docs, cols, rows):
    part, width = s.part, s.heads * HEAD
    for t, (source, begin) in enumerate(sources):
        tile_docs[t] = source[begin : begin + DOC_ROWS, 2 * width :].astype(jnp.float32)
        for side in range(2):
            whole = jnp.concatenate(
                [
                    source[begin : begin + part, side * width + h * HEAD : side * width + (h + 1) * HEAD]
                    for h in range(s.heads)
                ]
            )
            rows[side, t] = whole
            cols[side, t] = whole.T


def near_statistics(sizes, *refs):
    lines = sizes[0]
    count = 3 + 2 * lines
    place_ref, own_ref, peer_ref = refs[:3]
    stats_ref, tile_docs, cols, tile_rows, kv_all, docs_all = refs[count:]
    s = Setting(sizes, place_ref, kv_all, docs_all, tile_docs, cols.shape[-1], own_ref.shape[0], False)
    place_keys(s, (refs[3 : 3 + lines], refs[3 + lines : count]), kv_all, docs_all)
    place_rows(s, ((own_ref, 0), (peer_ref, 0)), tile_docs, cols, tile_rows)
    statistics(s, stats_ref, cols)


def far_statistics(sizes, *refs):
    place_ref, far_ref, kv_all, docs_all, stats_ref, tile_docs, cols, tile_rows = refs
    part = far_ref.shape[0] // TILES
    s = Setting(sizes, place_ref, kv_all, docs_all, tile_docs, cols.shape[-1], part, True)
    place_rows(s, ((far_ref, 0), (far_ref, part)), tile_docs, cols, tile_rows)
    statistics(s, stats_ref, cols)


def statistics(s, stats_ref, cols):
    rows = s.rows

    def fold(value, combine):
        return combine(value.reshape(CHUNK // 8, 8, rows), axis=0)

    def tile(t, carry):
        chunks, last, keys_at, mask = s.tile(t)

        def step(n, state, masked):
            top, norm, weighted = state
            at = keys_at(n)
            value = dot(s.key_rows(0, at), cols[0, t], (1, 0))
            if masked:
                value = jnp.where(mask, value, NEG)
            dp = dot(s.key_rows(1, at), cols[1, t], (1, 0))
            raised = jnp.maximum(top, jnp.max(fold(value, jnp.max), axis=0, keepdims=True) * TO_EXP2)
            e = jnp.exp2(value * TO_EXP2 - raised)
            factor = jnp.exp2(top - raised)
            return raised, norm * factor + fold(e, jnp.sum), weighted * factor + fold(e * dp, jnp.sum)

        zeros = jnp.zeros((8, rows), jnp.float32)
        state = (jnp.full((1, rows), NEG, jnp.float32), zeros, zeros)
        state = lax.fori_loop(0, last, lambda n, state: step(n, state, False), state)
        top, norm, weighted = lax.fori_loop(last, chunks, lambda n, state: step(n, state, True), state)
        stats_ref[t, 0:1, :] = top
        stats_ref[t, 1:2, :] = jnp.sum(norm, axis=0, keepdims=True)
        stats_ref[t, 2:3, :] = jnp.sum(weighted, axis=0, keepdims=True)
        return carry

    stats_ref[...] = jnp.zeros_like(stats_ref)
    lax.fori_loop(0, TILES, tile, 0)


def far_gradients(sizes, *refs):
    place_ref, here_ref, there_ref, tile_docs, cols, tile_rows, kv_all, docs_all, dq_ref, totals = refs
    s = Setting(sizes, place_ref, kv_all, docs_all, tile_docs, cols.shape[-1], dq_ref.shape[1], True)
    totals[...] = jnp.zeros_like(totals)
    gradients(s, here_ref, there_ref, cols, tile_rows, dq_ref, totals)


def near_gradients(sizes, *refs):
    lines = sizes[0]
    place_ref, here_ref, there_ref, tile_docs, cols, tile_rows, kv_all, docs_all, so_far, dq_ref = refs[:10]
    keep, send = refs[10 : 10 + lines], refs[10 + lines : 10 + 2 * lines]
    totals = refs[10 + 2 * lines]
    s = Setting(sizes, place_ref, kv_all, docs_all, tile_docs, cols.shape[-1], dq_ref.shape[1], False)
    totals[...] = so_far[...]
    gradients(s, here_ref, there_ref, cols, tile_rows, dq_ref, totals)
    for which, out, spot in ((s.core, keep, s.spots[0]), (1 - s.core, send, s.spots[1])):
        for i in s.steps:
            for j in s.steps:
                for c in range(2):
                    begin = pl.multiple_of((spot[i][j] + s.nx * c) * BLOCK, BLOCK)
                    out[i][j, c] = totals[which, pl.ds(begin, BLOCK), :].astype(jnp.bfloat16)


def gradients(s, here_ref, there_ref, cols, tile_rows, dq_ref, totals):
    part, rows = s.part, s.rows

    def tile(t, carry):
        chunks, last, keys_at, mask = s.tile(t)
        top_here, top_there = here_ref[t, 0:1, :], there_ref[t, 0:1, :]
        top = jnp.maximum(top_here, top_there)
        weight_here, weight_there = jnp.exp2(top_here - top), jnp.exp2(top_there - top)
        norm = here_ref[t, 1:2, :] * weight_here + there_ref[t, 1:2, :] * weight_there
        weighted = here_ref[t, 2:3, :] * weight_here + there_ref[t, 2:3, :] * weight_there
        delta = weighted / norm
        top = top + jnp.log2(norm)

        def work(n, dq, masked):
            at = keys_at(n)
            keys = pl.ds(pl.multiple_of(at * BLOCK, BLOCK), CHUNK)
            value = dot(s.key_rows(0, at), cols[0, t], (1, 0))
            if masked:
                value = jnp.where(mask, value, NEG)
            p = jnp.exp2(value * TO_EXP2 - top)
            ds = p * (dot(s.key_rows(1, at), cols[1, t], (1, 0)) - delta)
            p_low = p.astype(jnp.bfloat16)
            ds_low = ds.astype(jnp.bfloat16)
            totals[0, keys, :] += dot(ds_low, tile_rows[0, t], (1, 0))
            totals[1, keys, :] += dot(p_low, tile_rows[1, t], (1, 0))
            return dq + dot(s.key_rows(0, at), ds_low, (0, 0))

        dq = jnp.zeros((HEAD, rows), jnp.float32)
        dq = lax.fori_loop(0, last, lambda n, dq: work(n, dq, False), dq)
        dq = lax.fori_loop(last, chunks, lambda n, dq: work(n, dq, True), dq)
        dq = (dq * SCALE).T
        for h in range(s.heads):
            dq_ref[t, :, h * HEAD : (h + 1) * HEAD] = dq[h * part : (h + 1) * part, :].astype(dq_ref.dtype)
        return carry

    lax.fori_loop(0, TILES, tile, 0)

def kernel_call(kernel, sizes, operands, outs, scratch, products):
    whole = pl.BlockSpec(memory_space=pltpu.VMEM)
    return pl.pallas_call(
        lambda *refs: kernel(sizes, *refs),
        name=kernel.__name__,
        out_shape=outs,
        in_specs=[pl.BlockSpec(memory_space=pltpu.SMEM)] + [whole] * (len(operands) - 1),
        out_specs=(whole,) * len(outs),
        scratch_shapes=scratch,
        compiler_params=pltpu.CompilerParams(vmem_limit_bytes=VMEM_MIB * 1024 * 1024),
        cost_estimate=pl.CostEstimate(
            flops=products * 2 * 12 * 1024 * 128 * 128, bytes_accessed=8 * 1024 * 1024, transcendentals=0
        ),
    )(*operands)


def tile_outs(rows):
    return (
        jax.ShapeDtypeStruct((TILES, 8, rows), jnp.float32),
        jax.ShapeDtypeStruct((TILES, DOC_ROWS, HEAD), jnp.float32),
        jax.ShapeDtypeStruct((2, TILES, HEAD, rows), jnp.bfloat16),
        jax.ShapeDtypeStruct((2, TILES, rows, HEAD), jnp.bfloat16),
    )


def near_statistics_call(sizes, rows, *operands):
    nz, nx = sizes
    outs = tile_outs(rows) + (
        jax.ShapeDtypeStruct((2, 2 * nz * nx, BLOCK, HEAD), jnp.bfloat16),
        jax.ShapeDtypeStruct((nz * nx, DOC_ROWS, HEAD), jnp.float32),
    )
    outs = kernel_call(near_statistics, sizes, operands, outs, [], 2)
    return outs[0], outs[1:4], outs[4:]


def far_statistics_call(sizes, rows, *operands):
    outs = kernel_call(far_statistics, sizes, operands, tile_outs(rows), [], 2)
    return outs[0], outs[1:]


def far_gradients_call(sizes, dq_shape, *operands):
    nz, nx = sizes
    totals = jax.ShapeDtypeStruct((2, 2 * nz * nx * BLOCK, HEAD), jnp.float32)
    outs = (jax.ShapeDtypeStruct(dq_shape, jnp.bfloat16), totals)
    return kernel_call(far_gradients, sizes, operands, outs, [], 5)


def near_gradients_call(sizes, dq_shape, *operands):
    nz, nx = sizes
    outs = (jax.ShapeDtypeStruct(dq_shape, jnp.float32),)
    outs += (jax.ShapeDtypeStruct((nx, 2, BLOCK, HEAD), jnp.bfloat16),) * (2 * nz)
    scratch = [pltpu.VMEM((2, 2 * nz * nx * BLOCK, HEAD), jnp.float32)]
    return kernel_call(near_gradients, sizes, operands, outs, scratch, 5)


def low(value):
    return value.astype(jnp.bfloat16)


def added(terms):
    total = terms[0].astype(jnp.float32)
    for term in terms[1:]:
        total = total + term.astype(jnp.float32)
    return total


def per_device(queries, keys, values, grad_out, block_docs):
    rows, width = queries.shape
    inner_size, outer_size = lax.axis_size("inner"), lax.axis_size("outer")
    nz, nx = inner_size // 2, outer_size // 2
    inner, outer = lax.axis_index("inner"), lax.axis_index("outer")
    z, core = lax.div(inner, 2), lax.rem(inner, 2)
    x, y = lax.div(outer, 2), lax.rem(outer, 2)
    part = rows // PEERS
    apart = nz // PEERS
    lines = nz

    def moved(value, step):
        hops = []
        for source in range(inner_size * outer_size):
            i, o = divmod(source, outer_size)
            dz, dx, dy, dc = step(i % 2)
            to_inner = (i // 2 + dz) % nz * 2 + (i % 2 + dc) % 2
            to_outer = (o // 2 + dx) % nx * 2 + (o % 2 + dy) % 2
            hops.append((source, to_inner * outer_size + to_outer))
        return lax.ppermute(value, CONTEXT, hops)

    def other_core(value):
        return moved(value, lambda c: (0, 0, 0, 1))

    def other_y(value):
        return moved(value, lambda c: (0, 0, 1, 0))

    def peer(value):
        return moved(value, lambda c: (apart, 0, 0, 0))

    def along_first(value, by):
        return moved(value, lambda c: (0, by, 0, 0) if c else (by, 0, 0, 0))

    def along_second(value, by):
        return moved(value, lambda c: (by, 0, 0, 0) if c else (0, by, 0, 0))

    def in_order(index, mine, theirs, axis):
        return jnp.where(
            index == 0, jnp.stack([mine, theirs], axis=axis), jnp.stack([theirs, mine], axis=axis)
        )

    doc = jnp.broadcast_to(low(block_docs)[:, None], (DOC_ROWS, HEAD))
    half = lax.div(z, apart)

    def rows_of(which):
        cut = [lax.dynamic_slice_in_dim(whole, which * part, part, 0) for whole in (queries, grad_out)]
        return jnp.concatenate(cut + [jnp.broadcast_to(low(block_docs)[:, None], (part, HEAD))], axis=1)

    own = rows_of(half)
    borrowed = peer(rows_of(1 - half))
    shared = jnp.concatenate([own, borrowed])

    given = other_core(jnp.concatenate([jnp.where(core == 0, values, keys), doc]))
    kept = jnp.where(core == 0, keys, values)
    rows_in_order = in_order(core, kept, given[:BLOCK], 0).reshape(2 * BLOCK, HEAD)
    docs_in_order = in_order(core, doc[:8], given[BLOCK : BLOCK + 8], 0).reshape(DOC_ROWS, HEAD)
    unit = jnp.concatenate([rows_in_order, docs_in_order])
    line = jnp.stack([unit] + [along_first(unit, by) for by in range(1, lines)])
    far = other_y(shared)
    mine, theirs = [line] + [None] * (lines - 1), [None] * lines
    for by in (2, 1, 3):
        mine[by] = along_second(line, by)
    for by in (0, 1, 3, 2):
        theirs[by] = other_core(mine[by])

    place = jnp.stack([z, x, y, core]).astype(jnp.int32)
    sizes = (nz, nx)
    tile_rows = part * width // HEAD
    near_here, near_tiles, keys_all = near_statistics_call(sizes, tile_rows, place, own, borrowed, *mine, *theirs)
    far_there = other_y(near_here)
    far_here, far_tiles = far_statistics_call(sizes, tile_rows, place, far, *keys_all)
    near_there = other_y(far_here)
    dq_shape = (TILES, part, width)
    far_dq, so_far = far_gradients_call(sizes, dq_shape, place, far_here, far_there, *far_tiles, *keys_all)
    far_dq, near_there = lax.optimization_barrier((far_dq, near_there))
    rest = other_y(far_dq)
    dq, *sums = near_gradients_call(
        sizes, dq_shape, place, near_here, near_there, *near_tiles, *keys_all, so_far
    )
    rest, *sums = lax.optimization_barrier((rest, *sums))
    keep, send = sums[:lines], sums[lines:]

    totals = [None] * lines
    for by in (2, 1, 3, 0):
        totals[by] = low(added([keep[by], other_core(send[by])]))
    arrived = [along_second(totals[by], by) for by in (2, 1, 3)]
    dq, totals[0] = lax.optimization_barrier((dq, totals[0]))
    dq = low(dq + rest.astype(jnp.float32))
    returned = peer(dq[1])
    total = low(added([totals[0]] + arrived))
    short = [along_first(total[by], by) for by in (2, 1, 3)]
    short, returned = lax.optimization_barrier((short, returned))
    total = added([total[0]] + short)
    total = low(jnp.where(core == 0, SCALE * total, total))
    ours = jnp.where(core == 0, total[0], total[1])
    theirs = other_core(jnp.where(core == 0, total[1], total[0]))
    grad_keys = jnp.where(core == 0, ours, theirs)
    grad_values = jnp.where(core == 0, theirs, ours)
    grad_queries = in_order(half, dq[0], returned, 0).reshape(rows, width)
    return grad_queries, grad_keys, grad_values


def solution(mesh):
    wide = P(CONTEXT, "head")
    return jax.shard_map(
        per_device,
        mesh=mesh,
        in_specs=(wide, wide, wide, wide, P(CONTEXT)),
        out_specs=(wide, wide, wide),
        check_vma=False,
    )
```

```python
import math

import jax
import jax.numpy as jnp
from jax import lax
from jax.experimental import pallas as pl
from jax.experimental.pallas import tpu as pltpu
from jax.sharding import PartitionSpec as P

NEG = -1e30
HEAD = 128
BLOCK = 128
DOC_ROWS = 16
CHUNK_BLOCKS = 5
CHUNK = CHUNK_BLOCKS * BLOCK
TILES = 2
VMEM_MIB = 36
PEERS = 2
SCALE = float(HEAD) ** (-0.5)
TO_EXP2 = SCALE * math.log2(math.e)
CONTEXT = ("inner", "outer")


def dot(lhs, rhs, over):
    return lax.dot_general(lhs, rhs, ((over[:1], over[1:]), ((), ())), preferred_element_type=jnp.float32)


class Setting:
    def __init__(self, sizes, place_ref, kv_all, docs_all, tile_docs, rows, part, far):
        self.nz, self.nx = nz, nx = sizes
        lines = nz
        self.z, self.x, self.y, self.core = (place_ref[i] for i in range(4))
        self.part, self.rows = part, rows
        self.heads = rows // part
        self.row = 1 - self.y if far else self.y
        self.kv_all, self.docs_all, self.tile_docs = kv_all, docs_all, tile_docs
        self.blocks = kv_all.shape[1]
        self.steps = steps = range(lines)
        z_at = [lax.rem(self.z + by, nz) * (2 * nx) for by in steps]
        x_at = [lax.rem(self.x + by, nx) for by in steps]

        def places(which):
            return [
                [
                    jnp.where(which == 0, x_at[i], z_at[i]) + jnp.where(which == 0, z_at[j], x_at[j])
                    for j in steps
                ]
                for i in steps
            ]

        self.spots = (places(self.core), places(1 - self.core))
        apart = nz // PEERS
        self.apart = apart
        self.row_token = lax.div(self.z, apart) * part + lax.rem(
            lax.broadcasted_iota(jnp.int32, (CHUNK, self.rows), 1), part
        )
        key_row = lax.broadcasted_iota(jnp.int32, (CHUNK, self.rows), 0)
        self.key_row = key_row
        self.key_token = key_row + lax.div(key_row, BLOCK) * BLOCK

    def tile(self, t):
        dz = t * self.apart
        block = (lax.rem(self.z + self.nz - dz, self.nz) * 2 + self.core) * (2 * self.nx) + self.x * 2 + self.row
        doc = self.tile_docs[t, :1, :]
        before = jnp.sum(jnp.where(self.docs_all[...] < doc, 0.125, 0.0), axis=(0, 1))
        first = jnp.max(before).astype(jnp.int32)
        held = lax.div(block - self.y + 2, 2) - first
        chunks = lax.div(held + CHUNK_BLOCKS - 1, CHUNK_BLOCKS)
        last = jnp.maximum(chunks - 1, 0)

        def keys_at(n):
            return jnp.minimum(first + n * CHUNK_BLOCKS, self.blocks - CHUNK_BLOCKS)

        begin = keys_at(last)
        skipped = (first + last * CHUNK_BLOCKS - begin) * BLOCK
        reach = (block - 2 * begin - self.y) * BLOCK
        mask = (self.key_token <= self.row_token + reach) & (self.key_row >= skipped)
        return chunks, last, keys_at, mask

    def key_rows(self, which, at):
        return self.kv_all[which, pl.ds(at, CHUNK_BLOCKS)].reshape(CHUNK, HEAD)


def place_keys(s, pieces, kv_all, docs_all):
    for which, arrived, spot in ((s.core, pieces[0], s.spots[0]), (1 - s.core, pieces[1], s.spots[1])):
        for i in s.steps:
            for j in s.steps:
                for c in range(2):
                    kv_all[which, spot[-i][-j] + s.nx * c] = arrived[i][j, c * BLOCK : (c + 1) * BLOCK]
    for i in s.steps:
        for j in s.steps:
            docs_all[i * s.nz + j] = pieces[0][i][j, 2 * BLOCK :].astype(jnp.float32)


def place_rows(s, sources, tile_docs, cols, rows):
    part, width = s.part, s.heads * HEAD
    for t, (source, begin) in enumerate(sources):
        tile_docs[t] = source[begin : begin + DOC_ROWS, 2 * width :].astype(jnp.float32)
        for side in range(2):
            whole = jnp.concatenate(
                [
                    source[begin : begin + part, side * width + h * HEAD : side * width + (h + 1) * HEAD]
                    for h in range(s.heads)
                ]
            )
            rows[side, t] = whole
            cols[side, t] = whole.T


def near_statistics(sizes, *refs):
    lines = sizes[0]
    count = 3 + 2 * lines
    place_ref, own_ref, peer_ref = refs[:3]
    stats_ref, tile_docs, cols, tile_rows, kv_all, docs_all = refs[count:]
    s = Setting(sizes, place_ref, kv_all, docs_all, tile_docs, cols.shape[-1], own_ref.shape[0], False)
    place_keys(s, (refs[3 : 3 + lines], refs[3 + lines : count]), kv_all, docs_all)
    place_rows(s, ((own_ref, 0), (peer_ref, 0)), tile_docs, cols, tile_rows)
    statistics(s, stats_ref, cols)


def far_statistics(sizes, *refs):
    place_ref, far_ref, kv_all, docs_all, stats_ref, tile_docs, cols, tile_rows = refs
    part = far_ref.shape[0] // TILES
    s = Setting(sizes, place_ref, kv_all, docs_all, tile_docs, cols.shape[-1], part, True)
    place_rows(s, ((far_ref, 0), (far_ref, part)), tile_docs, cols, tile_rows)
    statistics(s, stats_ref, cols)


def statistics(s, stats_ref, cols):
    rows = s.rows

    def fold(value, combine):
        return combine(value.reshape(CHUNK // 8, 8, rows), axis=0)

    def tile(t, carry):
        chunks, last, keys_at, mask = s.tile(t)

        def step(n, state, masked):
            top, norm, weighted = state
            at = keys_at(n)
            value = dot(s.key_rows(0, at), cols[0, t], (1, 0))
            if masked:
                value = jnp.where(mask, value, NEG)
            dp = dot(s.key_rows(1, at), cols[1, t], (1, 0))
            raised = jnp.maximum(top, jnp.max(fold(value, jnp.max), axis=0, keepdims=True) * TO_EXP2)
            e = jnp.exp2(value * TO_EXP2 - raised)
            factor = jnp.exp2(top - raised)
            return raised, norm * factor + fold(e, jnp.sum), weighted * factor + fold(e * dp, jnp.sum)

        zeros = jnp.zeros((8, rows), jnp.float32)
        state = (jnp.full((1, rows), NEG, jnp.float32), zeros, zeros)
        state = lax.fori_loop(0, last, lambda n, state: step(n, state, False), state)
        top, norm, weighted = lax.fori_loop(last, chunks, lambda n, state: step(n, state, True), state)
        stats_ref[t, 0:1, :] = top
        stats_ref[t, 1:2, :] = jnp.sum(norm, axis=0, keepdims=True)
        stats_ref[t, 2:3, :] = jnp.sum(weighted, axis=0, keepdims=True)
        return carry

    stats_ref[...] = jnp.zeros_like(stats_ref)
    lax.fori_loop(0, TILES, tile, 0)


def far_gradients(sizes, *refs):
    place_ref, here_ref, there_ref, tile_docs, cols, tile_rows, kv_all, docs_all, dq_ref, totals = refs
    s = Setting(sizes, place_ref, kv_all, docs_all, tile_docs, cols.shape[-1], dq_ref.shape[1], True)
    totals[...] = jnp.zeros_like(totals)
    gradients(s, here_ref, there_ref, cols, tile_rows, dq_ref, totals)


def near_gradients(sizes, *refs):
    lines = sizes[0]
    place_ref, here_ref, there_ref, tile_docs, cols, tile_rows, kv_all, docs_all, so_far, dq_ref = refs[:10]
    keep, send = refs[10 : 10 + lines], refs[10 + lines : 10 + 2 * lines]
    totals = refs[10 + 2 * lines]
    s = Setting(sizes, place_ref, kv_all, docs_all, tile_docs, cols.shape[-1], dq_ref.shape[1], False)
    totals[...] = so_far[...]
    gradients(s, here_ref, there_ref, cols, tile_rows, dq_ref, totals)
    for which, out, spot in ((s.core, keep, s.spots[0]), (1 - s.core, send, s.spots[1])):
        for i in s.steps:
            for j in s.steps:
                for c in range(2):
                    begin = pl.multiple_of((spot[i][j] + s.nx * c) * BLOCK, BLOCK)
                    out[i][j, c] = totals[which, pl.ds(begin, BLOCK), :].astype(jnp.bfloat16)


def gradients(s, here_ref, there_ref, cols, tile_rows, dq_ref, totals):
    part, rows = s.part, s.rows

    def tile(t, carry):
        chunks, last, keys_at, mask = s.tile(t)
        top_here, top_there = here_ref[t, 0:1, :], there_ref[t, 0:1, :]
        top = jnp.maximum(top_here, top_there)
        weight_here, weight_there = jnp.exp2(top_here - top), jnp.exp2(top_there - top)
        norm = here_ref[t, 1:2, :] * weight_here + there_ref[t, 1:2, :] * weight_there
        weighted = here_ref[t, 2:3, :] * weight_here + there_ref[t, 2:3, :] * weight_there
        delta = weighted / norm
        top = top + jnp.log2(norm)

        def work(n, dq, masked):
            at = keys_at(n)
            keys = pl.ds(pl.multiple_of(at * BLOCK, BLOCK), CHUNK)
            value = dot(s.key_rows(0, at), cols[0, t], (1, 0))
            if masked:
                value = jnp.where(mask, value, NEG)
            p = jnp.exp2(value * TO_EXP2 - top)
            ds = p * (dot(s.key_rows(1, at), cols[1, t], (1, 0)) - delta)
            p_low = p.astype(jnp.bfloat16)
            ds_low = ds.astype(jnp.bfloat16)
            totals[0, keys, :] += dot(ds_low, tile_rows[0, t], (1, 0))
            totals[1, keys, :] += dot(p_low, tile_rows[1, t], (1, 0))
            return dq + dot(s.key_rows(0, at), ds_low, (0, 0))

        dq = jnp.zeros((HEAD, rows), jnp.float32)
        dq = lax.fori_loop(0, last, lambda n, dq: work(n, dq, False), dq)
        dq = lax.fori_loop(last, chunks, lambda n, dq: work(n, dq, True), dq)
        dq = (dq * SCALE).T
        for h in range(s.heads):
            dq_ref[t, :, h * HEAD : (h + 1) * HEAD] = dq[h * part : (h + 1) * part, :].astype(dq_ref.dtype)
        return carry

    lax.fori_loop(0, TILES, tile, 0)

def kernel_call(kernel, sizes, operands, outs, scratch, products):
    whole = pl.BlockSpec(memory_space=pltpu.VMEM)
    return pl.pallas_call(
        lambda *refs: kernel(sizes, *refs),
        name=kernel.__name__,
        out_shape=outs,
        in_specs=[pl.BlockSpec(memory_space=pltpu.SMEM)] + [whole] * (len(operands) - 1),
        out_specs=(whole,) * len(outs),
        scratch_shapes=scratch,
        compiler_params=pltpu.CompilerParams(vmem_limit_bytes=VMEM_MIB * 1024 * 1024),
        cost_estimate=pl.CostEstimate(
            flops=products * 2 * 12 * 1024 * 128 * 128, bytes_accessed=8 * 1024 * 1024, transcendentals=0
        ),
    )(*operands)


def tile_outs(rows):
    return (
        jax.ShapeDtypeStruct((TILES, 8, rows), jnp.float32),
        jax.ShapeDtypeStruct((TILES, DOC_ROWS, HEAD), jnp.float32),
        jax.ShapeDtypeStruct((2, TILES, HEAD, rows), jnp.bfloat16),
        jax.ShapeDtypeStruct((2, TILES, rows, HEAD), jnp.bfloat16),
    )


def near_statistics_call(sizes, rows, *operands):
    nz, nx = sizes
    outs = tile_outs(rows) + (
        jax.ShapeDtypeStruct((2, 2 * nz * nx, BLOCK, HEAD), jnp.bfloat16),
        jax.ShapeDtypeStruct((nz * nx, DOC_ROWS, HEAD), jnp.float32),
    )
    outs = kernel_call(near_statistics, sizes, operands, outs, [], 2)
    return outs[0], outs[1:4], outs[4:]


def far_statistics_call(sizes, rows, *operands):
    outs = kernel_call(far_statistics, sizes, operands, tile_outs(rows), [], 2)
    return outs[0], outs[1:]


def far_gradients_call(sizes, dq_shape, *operands):
    nz, nx = sizes
    totals = jax.ShapeDtypeStruct((2, 2 * nz * nx * BLOCK, HEAD), jnp.float32)
    outs = (jax.ShapeDtypeStruct(dq_shape, jnp.bfloat16), totals)
    return kernel_call(far_gradients, sizes, operands, outs, [], 5)


def near_gradients_call(sizes, dq_shape, *operands):
    nz, nx = sizes
    outs = (jax.ShapeDtypeStruct(dq_shape, jnp.float32),)
    outs += (jax.ShapeDtypeStruct((nx, 2, BLOCK, HEAD), jnp.bfloat16),) * (2 * nz)
    scratch = [pltpu.VMEM((2, 2 * nz * nx * BLOCK, HEAD), jnp.float32)]
    return kernel_call(near_gradients, sizes, operands, outs, scratch, 5)


def low(value):
    return value.astype(jnp.bfloat16)


def added(terms):
    total = terms[0].astype(jnp.float32)
    for term in terms[1:]:
        total = total + term.astype(jnp.float32)
    return total


def per_device(queries, keys, values, grad_out, block_docs):
    rows, width = queries.shape
    inner_size, outer_size = lax.axis_size("inner"), lax.axis_size("outer")
    nz, nx = inner_size // 2, outer_size // 2
    inner, outer = lax.axis_index("inner"), lax.axis_index("outer")
    z, core = lax.div(inner, 2), lax.rem(inner, 2)
    x, y = lax.div(outer, 2), lax.rem(outer, 2)
    part = rows // PEERS
    apart = nz // PEERS
    lines = nz

    def moved(value, step):
        hops = []
        for source in range(inner_size * outer_size):
            i, o = divmod(source, outer_size)
            dz, dx, dy, dc = step(i % 2)
            to_inner = (i // 2 + dz) % nz * 2 + (i % 2 + dc) % 2
            to_outer = (o // 2 + dx) % nx * 2 + (o % 2 + dy) % 2
            hops.append((source, to_inner * outer_size + to_outer))
        return lax.ppermute(value, CONTEXT, hops)

    def other_core(value):
        return moved(value, lambda c: (0, 0, 0, 1))

    def other_y(value):
        return moved(value, lambda c: (0, 0, 1, 0))

    def peer(value):
        return moved(value, lambda c: (apart, 0, 0, 0))

    def along_first(value, by):
        return moved(value, lambda c: (0, by, 0, 0) if c else (by, 0, 0, 0))

    def along_second(value, by):
        return moved(value, lambda c: (by, 0, 0, 0) if c else (0, by, 0, 0))

    def in_order(index, mine, theirs, axis):
        return jnp.where(
            index == 0, jnp.stack([mine, theirs], axis=axis), jnp.stack([theirs, mine], axis=axis)
        )

    doc = jnp.broadcast_to(low(block_docs)[:, None], (DOC_ROWS, HEAD))
    half = lax.div(z, apart)

    def rows_of(which):
        cut = [lax.dynamic_slice_in_dim(whole, which * part, part, 0) for whole in (queries, grad_out)]
        return jnp.concatenate(cut + [jnp.broadcast_to(low(block_docs)[:, None], (part, HEAD))], axis=1)

    own = rows_of(half)
    borrowed = peer(rows_of(1 - half))
    shared = jnp.concatenate([own, borrowed])

    given = other_core(jnp.concatenate([jnp.where(core == 0, values, keys), doc]))
    kept = jnp.where(core == 0, keys, values)
    rows_in_order = in_order(core, kept, given[:BLOCK], 0).reshape(2 * BLOCK, HEAD)
    docs_in_order = in_order(core, doc[:8], given[BLOCK : BLOCK + 8], 0).reshape(DOC_ROWS, HEAD)
    unit = jnp.concatenate([rows_in_order, docs_in_order])
    line = jnp.stack([unit] + [along_first(unit, by) for by in range(1, lines)])
    far = other_y(shared)
    mine, theirs = [line] + [None] * (lines - 1), [None] * lines
    for by in (2, 1, 3):
        mine[by] = along_second(line, by)
    for by in (0, 1, 3, 2):
        theirs[by] = other_core(mine[by])

    place = jnp.stack([z, x, y, core]).astype(jnp.int32)
    sizes = (nz, nx)
    tile_rows = part * width // HEAD
    near_here, near_tiles, keys_all = near_statistics_call(sizes, tile_rows, place, own, borrowed, *mine, *theirs)
    far_there = other_y(near_here)
    far_here, far_tiles = far_statistics_call(sizes, tile_rows, place, far, *keys_all)
    near_there = other_y(far_here)
    dq_shape = (TILES, part, width)
    far_dq, so_far = far_gradients_call(sizes, dq_shape, place, far_here, far_there, *far_tiles, *keys_all)
    far_dq, near_there = lax.optimization_barrier((far_dq, near_there))
    rest = other_y(far_dq)
    dq, *sums = near_gradients_call(
        sizes, dq_shape, place, near_here, near_there, *near_tiles, *keys_all, so_far
    )
    rest, *sums = lax.optimization_barrier((rest, *sums))
    keep, send = sums[:lines], sums[lines:]

    totals = [None] * lines
    for by in (2, 1, 3, 0):
        totals[by] = low(added([keep[by], other_core(send[by])]))
    arrived = [along_second(totals[by], by) for by in (2, 1, 3)]
    dq, totals[0] = lax.optimization_barrier((dq, totals[0]))
    dq = low(dq + rest.astype(jnp.float32))
    returned = peer(dq[1])
    total = low(added([totals[0]] + arrived))
    short = [along_first(total[by], by) for by in (2, 1, 3)]
    short, returned = lax.optimization_barrier((short, returned))
    total = added([total[0]] + short)
    total = low(jnp.where(core == 0, SCALE * total, total))
    ours = jnp.where(core == 0, total[0], total[1])
    theirs = other_core(jnp.where(core == 0, total[1], total[0]))
    grad_keys = jnp.where(core == 0, ours, theirs)
    grad_values = jnp.where(core == 0, theirs, ours)
    grad_queries = in_order(half, dq[0], returned, 0).reshape(rows, width)
    return grad_queries, grad_keys, grad_values


def solution(mesh):
    wide = P(CONTEXT, "head")
    return jax.shard_map(
        per_device,
        mesh=mesh,
        in_specs=(wide, wide, wide, wide, P(CONTEXT)),
        out_specs=(wide, wide, wide),
        check_vma=False,
    )
```
